32 devices in a mesh: seg: 8 (over y, x, core), tok: 4 (over z).
Axes of the slice: x: 2, y: 2, z: 4, core: 2. Of those that a mesh axis runs over, the one named last changes fastest.
Arguments:
- incoming_items: bfloat16 [8, 1280, 1024], P('seg', 'tok'), may hold values from -6 to 6
- upstream_slope: bfloat16 [8, 1280, 1024], P('seg', 'tok'), may hold values from -6 to 6
- timemix_prior_entry: bfloat16 [8, 1024], P('seg'), may hold values from -6 to 6
- featmix_prior_entry: bfloat16 [8, 1024], P('seg'), may hold values from -6 to 6
- opening_dividend: float32 [8, 1024], P('seg', 'tok'), may hold values from -6 to 6
- opening_divisor: float32 [8, 1024], P('seg', 'tok'), may hold values from 0.5 to 4
- opening_power: float32 [8, 1024], P('seg', 'tok'), may hold values from -4 to 4
- normalize_scales: float32 [2, 1024], replicated, may hold values from 0.5 to 1.5
- normalize_shifts: float32 [2, 1024], replicated, may hold values from -1 to 1
- shift_blends: float32 [5, 1024], replicated, may hold values from 0.05 to 0.95
- logarithmic_fading_speed: float32 [1024], replicated, may hold values from -11.5 to -3
- present_reward: float32 [1024], replicated, may hold values from -1 to 1
- timemix_lookup_coeffs: bfloat16 [1024, 1024], replicated, may hold values from -0.1875 to 0.1875
- timemix_payload_coeffs: bfloat16 [1024, 1024], replicated, may hold values from -0.1875 to 0.1875
- timemix_accept_coeffs: bfloat16 [1024, 1024], replicated, may hold values from -0.1875 to 0.1875
- timemix_emit_coeffs: bfloat16 [1024, 1024], replicated, may hold values from -0.75 to 0.75
- featmix_lookup_coeffs: bfloat16 [1024, 4096], replicated, may hold values from -0.1875 to 0.1875
- featmix_payload_coeffs: bfloat16 [4096, 1024], replicated, may hold values from -0.09375 to 0.09375
- featmix_accept_coeffs: bfloat16 [1024, 1024], replicated, may hold values from -0.1875 to 0.1875
Outputs:
- layer_out: bfloat16 [8, 1280, 1024], P('seg', 'tok')
- token_grad: bfloat16 [8, 1280, 1024], P('seg', 'tok')
- final_num: float32 [8, 1024], P('seg', 'tok')
- final_den: float32 [8, 1024], P('seg', 'tok')
- final_top: float32 [8, 1024], P('seg', 'tok')
- gains_grad: float32 [2, 1024], P(None, ('seg', 'tok'))
- biases_grad: float32 [2, 1024], P(None, ('seg', 'tok'))
- mixes_grad: float32 [5, 1024], P(None, ('seg', 'tok'))
- decay_grad: float32 [1024], P(('seg', 'tok'))
- bonus_grad: float32 [1024], P(('seg', 'tok'))
- att_key_grad: float32 [1024, 1024], P(('seg', 'tok'))
- att_value_grad: float32 [1024, 1024], P(('seg', 'tok'))
- att_recept_grad: float32 [1024, 1024], P(('seg', 'tok'))
- att_out_grad: float32 [1024, 1024], P(('seg', 'tok'))
- ffn_key_grad: float32 [1024, 4096], P(('seg', 'tok'))
- ffn_value_grad: float32 [4096, 1024], P(('seg', 'tok'))
- ffn_recept_grad: float32 [1024, 1024], P(('seg', 'tok'))
The draws below stay inside these ranges and needn't reach their ends.
All inputs are finite; a program needn't handle non-finite values.
Results may differ from the reference program's by a relative error of at most 0.024.
Values may be sent and summed in bfloat16 or wider, within the bound.
A program may use at most 192 MiB of HBM per device.

```python
import math
from functools import partial
import jax
import jax.numpy as jnp
from jax import lax

EMBED_SIZE = 1024
FF = 4096
SPAN = 128
SEQ_LEN = 1280
SEQS_ALL = 8


def level_of(own_key, extent, split, least, top_value):
    level = 1.0
    for dim, parts in split:
        draws = jax.random.uniform(jax.random.fold_in(jax.random.fold_in(own_key, 6), dim), (parts,), jnp.float32, least / len(split), top_value / len(split))
        level = level * jnp.repeat(jnp.exp(draws), extent[dim] // parts).reshape((-1,) + (1,) * (len(extent) - 1 - dim))
    return level


def gaussian(rng, dims, width, most, pieces=(), kind=jnp.bfloat16):
    array = width * jax.random.normal(rng, dims, jnp.float32)
    if pieces:
        array = array * level_of(rng, dims, pieces, -0.22, 0.18)
    return jnp.clip(array, -most, most).astype(kind)


def setup_inputs(seed: int = 0) -> dict:
    splits = jax.random.split(jax.random.key(seed), 20)
    return {
        "incoming_items": gaussian(splits[0], (SEQS_ALL, SEQ_LEN, EMBED_SIZE), 1.0, 6.0, ((0, 8), (1, 4))),
        "upstream_slope": gaussian(splits[1], (SEQS_ALL, SEQ_LEN, EMBED_SIZE), 1.0, 6.0, ((0, 8), (1, 4))),
        "timemix_prior_entry": gaussian(splits[2], (SEQS_ALL, EMBED_SIZE), 1.0, 6.0, ((0, 8),)),
        "featmix_prior_entry": gaussian(splits[3], (SEQS_ALL, EMBED_SIZE), 1.0, 6.0, ((0, 8),)),
        "opening_dividend": gaussian(splits[4], (SEQS_ALL, EMBED_SIZE), 1.0, 6.0, ((0, 8), (1, 4)), jnp.float32),
        "opening_divisor": jnp.clip(jnp.exp(math.log(4.0) - 2.0794415 * jax.random.uniform(splits[5], (SEQS_ALL, EMBED_SIZE), jnp.float32) ** level_of(splits[5], (SEQS_ALL, EMBED_SIZE), ((0, 8), (1, 4)), -0.2, 0.2)), 0.5, 4.0),
        "opening_power": gaussian(splits[6], (SEQS_ALL, EMBED_SIZE), 1.0, 4.0, ((0, 8), (1, 4)), jnp.float32),
        "normalize_scales": jnp.clip(1.0 + 0.1 * jax.random.normal(splits[7], (2, EMBED_SIZE), jnp.float32), 0.5, 1.5),
        "normalize_shifts": gaussian(splits[8], (2, EMBED_SIZE), 0.2, 1.0, (), jnp.float32),
        "shift_blends": jnp.clip(jax.random.uniform(splits[9], (5, EMBED_SIZE), jnp.float32, 0.05, 0.95), 0.05, 0.95),
        "logarithmic_fading_speed": jnp.clip(jax.random.uniform(splits[10], (EMBED_SIZE,), jnp.float32, -11.5, -3.0), -11.5, -3.0),
        "present_reward": jnp.clip(jax.random.uniform(splits[11], (EMBED_SIZE,), jnp.float32, -1.0, 1.0), -1.0, 1.0),
        "timemix_lookup_coeffs": gaussian(splits[12], (EMBED_SIZE, EMBED_SIZE), EMBED_SIZE ** -0.5, 0.1875),
        "timemix_payload_coeffs": gaussian(splits[13], (EMBED_SIZE, EMBED_SIZE), EMBED_SIZE ** -0.5, 0.1875),
        "timemix_accept_coeffs": gaussian(splits[14], (EMBED_SIZE, EMBED_SIZE), EMBED_SIZE ** -0.5, 0.1875),
        "timemix_emit_coeffs": gaussian(splits[15], (EMBED_SIZE, EMBED_SIZE), (EMBED_SIZE // 16) ** -0.5, 0.75),
        "featmix_lookup_coeffs": gaussian(splits[16], (EMBED_SIZE, FF), EMBED_SIZE ** -0.5, 0.1875),
        "featmix_payload_coeffs": gaussian(splits[17], (FF, EMBED_SIZE), FF ** -0.5, 0.09375),
        "featmix_accept_coeffs": gaussian(splits[18], (EMBED_SIZE, EMBED_SIZE), EMBED_SIZE ** -0.5, 0.1875),
    }


@jax.custom_vjp
def low(v):
    return lax.optimization_barrier(v.astype(jnp.bfloat16)).astype(jnp.float32)

@jax.custom_vjp
def low_back(v):
    return v

def low_keep(v):
    return (low(v), None)

def low_pass(kept, grad):
    return (grad,)

def back_keep(v):
    return (v, None)

def back_low(kept, grad):
    return (low(grad),)
low.defvjp(low_keep, low_pass)
low_back.defvjp(back_keep, back_low)

def matmul(left, right):
    return jnp.dot(left, right, precision=lax.Precision.HIGHEST, preferred_element_type=jnp.float32)

def layer_norm(values, gain_row, bias_row):
    centre = values - lax.optimization_barrier(jnp.mean(values, axis=-1, keepdims=True))
    spread = lax.optimization_barrier(jnp.mean(centre * centre, axis=-1, keepdims=True))
    return centre * lax.rsqrt(spread + 1e-05) * gain_row + bias_row

def iterative_item(handed_memory, stratum_arguments, fading_multiplier, present_reward):
    numer, denom, stable = handed_memory
    lookup_item_entry, value_row = stratum_arguments
    present_memory = present_reward + lookup_item_entry
    peak_now = jnp.maximum(stable, present_memory)
    old_part = jnp.exp(stable - peak_now)
    new_part = jnp.exp(present_memory - peak_now)
    result = (old_part * numer + new_part * value_row) / (old_part * denom + new_part)
    faded = stable - fading_multiplier
    peak_next = jnp.maximum(faded, lookup_item_entry)
    old_keep = jnp.exp(faded - peak_next)
    new_keep = jnp.exp(lookup_item_entry - peak_next)
    return ((old_keep * numer + new_keep * value_row, old_keep * denom + new_keep, peak_next), result)

def iterative_series(lookup_series, payload_series, fading_multiplier, present_reward, first_feature):
    length, portion_breadth = lookup_series.shape
    blocks = length // SPAN

    def block_step(handed_memory, stratum_arguments):
        return lax.scan(partial(iterative_item, fading_multiplier=fading_multiplier, present_reward=present_reward), handed_memory, stratum_arguments)
    closing_memories, outputs = lax.scan(jax.checkpoint(block_step), first_feature, (lookup_series.reshape(blocks, SPAN, portion_breadth), payload_series.reshape(blocks, SPAN, portion_breadth)))
    return (outputs.reshape(length, portion_breadth), closing_memories)

def forward(stratum_settings, sequence, prev_att, prev_ffn, first_feature):
    normalize_scales, normalize_shifts, shift_blends, logarithmic_fading_speed, present_reward, timemix_lookup_coeffs, timemix_payload_coeffs, timemix_accept_coeffs, timemix_emit_coeffs, featmix_lookup_coeffs, featmix_payload_coeffs, featmix_accept_coeffs = stratum_settings
    normed = low(layer_norm(sequence, normalize_scales[0], normalize_shifts[0]))
    before = low_back(jnp.concatenate([prev_att[None, :], normed[:-1]], axis=0))
    key_mix = low(normed * shift_blends[0] + before * (1.0 - shift_blends[0]))
    value_mix = low(normed * shift_blends[1] + before * (1.0 - shift_blends[1]))
    recept_mix = low(normed * shift_blends[2] + before * (1.0 - shift_blends[2]))
    lookup_mapped = low(low_back(matmul(key_mix, timemix_lookup_coeffs)))
    payload_mapped = low(low_back(matmul(value_mix, timemix_payload_coeffs)))
    recept = jax.nn.sigmoid(low_back(matmul(recept_mix, timemix_accept_coeffs)))
    blended_entries, closing_memories = iterative_series(lookup_mapped, payload_mapped, jnp.exp(logarithmic_fading_speed), present_reward, first_feature)
    blended_entries = low(low_back(blended_entries))
    middle = sequence + low_back(matmul(low(recept * blended_entries), timemix_emit_coeffs))
    normed_two = low(layer_norm(middle, normalize_scales[1], normalize_shifts[1]))
    before_two = low_back(jnp.concatenate([prev_ffn[None, :], normed_two[:-1]], axis=0))
    key_two = low(normed_two * shift_blends[3] + before_two * (1.0 - shift_blends[3]))
    recept_two = low(normed_two * shift_blends[4] + before_two * (1.0 - shift_blends[4]))
    hidden = low_back(matmul(key_two, featmix_lookup_coeffs))
    squared = low(jnp.square(jax.nn.relu(hidden)))
    handed_memory = low_back(matmul(squared, featmix_payload_coeffs))
    gate_two = jax.nn.sigmoid(low_back(matmul(recept_two, featmix_accept_coeffs)))
    return (middle + gate_two * handed_memory, closing_memories)

def reference(incoming_items, upstream_slope, timemix_prior_entry, featmix_prior_entry, opening_dividend, opening_divisor, opening_power, normalize_scales, normalize_shifts, shift_blends, logarithmic_fading_speed, present_reward, timemix_lookup_coeffs, timemix_payload_coeffs, timemix_accept_coeffs, timemix_emit_coeffs, featmix_lookup_coeffs, featmix_payload_coeffs, featmix_accept_coeffs):
    stratum_settings = tuple((coefficient_table.astype(jnp.float32) for coefficient_table in (normalize_scales, normalize_shifts, shift_blends, logarithmic_fading_speed, present_reward, timemix_lookup_coeffs, timemix_payload_coeffs, timemix_accept_coeffs, timemix_emit_coeffs, featmix_lookup_coeffs, featmix_payload_coeffs, featmix_accept_coeffs)))

    def per_sequence(totals, stratum_arguments):
        sequence, upstream, prev_att, prev_ffn, num_in, den_in, top_in = stratum_arguments
        prev_att = prev_att.astype(jnp.float32)
        prev_ffn = prev_ffn.astype(jnp.float32)

        def layer(weights, seq_in):
            return forward(weights, seq_in, prev_att, prev_ffn, (num_in, den_in, top_in))
        result, pull, closing_memories = jax.vjp(layer, stratum_settings, sequence.astype(jnp.float32), has_aux=True)
        grad_params, grad_seq = pull(upstream.astype(jnp.float32))
        totals = jax.tree.map(jnp.add, totals, grad_params)
        return (totals, (result.astype(jnp.bfloat16), grad_seq.astype(jnp.bfloat16), closing_memories[0], closing_memories[1], closing_memories[2]))
    zero_state = jax.tree.map(jnp.zeros_like, stratum_settings)
    totals, outs = lax.scan(per_sequence, zero_state, (incoming_items, upstream_slope, timemix_prior_entry, featmix_prior_entry, opening_dividend, opening_divisor, opening_power))
    layer_out, token_grad, final_num, final_den, final_top = outs
    return (layer_out, token_grad, final_num, final_den, final_top, totals[0], totals[1], totals[2], totals[3], totals[4], totals[5], totals[6], totals[7], totals[8], totals[9], totals[10], totals[11])
```

```python
from functools import partial

import jax
import jax.numpy as jnp
from jax import lax
from jax.experimental import pallas as pl
from jax.experimental.pallas import tpu as pltpu
from jax.sharding import PartitionSpec as P

EMBED_SIZE = 1024
FF = 4096
SPAN = 128
VMEM_BYTES = 62 << 20
MESH = pl.DeviceIdType.MESH


def passed_along(value, axis, steps):
    count = lax.axis_size(axis)
    first, last = (max(0, -steps), min(count, count - steps))
    return lax.ppermute(value, axis, [(source, source + steps) for source in range(first, last)])


def layer_norm(values, gain_row, bias_row):
    centre = values - jnp.mean(values, axis=-1, keepdims=True)
    spread = jnp.mean(centre * centre, axis=-1, keepdims=True)
    return centre * lax.rsqrt(spread + 1e-05) * gain_row + bias_row


def dense(left, right):
    return jnp.dot(left, right, preferred_element_type=jnp.float32)


def dense_back(left, right):
    return lax.dot_general(
        left, right, (((2,), (1,)), ((), ())), preferred_element_type=jnp.float32
    )


def blend(normed_low, before_low, weight_row):
    return normed_low * weight_row + before_low * (1.0 - weight_row)


def unmix(grads, weight_rows, normed_low, before_low):
    direct = grads[0] * weight_rows[0]
    across = grads[0] * (1.0 - weight_rows[0])
    for grad_item, weight_row in zip(grads[1:], weight_rows[1:]):
        direct = direct + grad_item * weight_row
        across = across + grad_item * (1.0 - weight_row)
    difference = normed_low - before_low
    totals = [jnp.sum(grad_item * difference, axis=(0, 1)) for grad_item in grads]
    return (direct, across.astype(jnp.bfloat16), totals)


def portion_iteration(lookup_series, payload_series, fading_portion, reward_portion, first_feature):
    seqs_here, length, portion_breadth = lookup_series.shape
    blocks = length // SPAN
    fading_multiplier = jnp.exp(fading_portion)
    steps = jnp.arange(SPAN, dtype=jnp.float32)
    lower = (steps[:, None] > steps[None, :]).astype(jnp.float32)
    place = steps[None, :, None]

    def block_step(handed_memory, stratum_arguments):
        numer, denom, stable = handed_memory
        lookup_tile_entries, value_blk = stratum_arguments
        lifted = lookup_tile_entries + place * fading_multiplier
        top = jnp.max(lifted, axis=1)
        scaled = jnp.exp(lifted - top[:, None, :])
        scaled_value = scaled * value_blk
        past_num = jnp.einsum("ts,nsc->ntc", lower, scaled_value, precision=lax.Precision.HIGHEST)
        past_den = jnp.einsum("ts,nsc->ntc", lower, scaled, precision=lax.Precision.HIGHEST)
        past_expo = top[:, None, :] - (place - 1.0) * fading_multiplier
        state_expo = stable[:, None, :] - place * fading_multiplier
        present_power = reward_portion + lookup_tile_entries
        peak = jnp.maximum(jnp.maximum(state_expo, present_power), past_expo)
        past_scale = jnp.exp(past_expo - peak)
        state_scale = jnp.exp(state_expo - peak)
        now_scale = jnp.exp(present_power - peak)
        numer_out = state_scale * numer[:, None, :] + past_scale * past_num + now_scale * value_blk
        denom_out = state_scale * denom[:, None, :] + past_scale * past_den + now_scale
        end_top = top - (SPAN - 1.0) * fading_multiplier
        faded = stable - SPAN * fading_multiplier
        peak_end = jnp.maximum(faded, end_top)
        keep_old = jnp.exp(faded - peak_end)
        keep_new = jnp.exp(end_top - peak_end)
        new_state = (
            keep_old * numer + keep_new * jnp.sum(scaled_value, axis=1),
            keep_old * denom + keep_new * jnp.sum(scaled, axis=1),
            peak_end,
        )
        return (new_state, numer_out / denom_out)

    key_blocks = lookup_series.reshape(seqs_here, blocks, SPAN, portion_breadth).transpose(
        1, 0, 2, 3
    )
    value_blocks = payload_series.reshape(seqs_here, blocks, SPAN, portion_breadth).transpose(
        1, 0, 2, 3
    )
    closing_memories, outputs = lax.scan(
        jax.checkpoint(block_step), first_feature, (key_blocks, value_blocks)
    )
    return (
        outputs.transpose(1, 0, 2, 3).reshape(seqs_here, length, portion_breadth),
        closing_memories,
    )


class Plan:
    def __init__(self, count_seg, count_tok):
        self.count_seg, self.count_tok = count_seg, count_tok
        self.bits = count_seg.bit_length() - 1
        self.seg_rows = EMBED_SIZE // count_seg
        self.seg_rows_ff = FF // count_seg
        self.low_bits = max(0, (128 // self.seg_rows).bit_length() - 1)
        self.pair = self.low_bits
        self.rest = [b for b in range(self.bits) if b != self.pair]
        self.orders = (self.rest, self.rest[::-1])
        self.stages = len(self.rest)
        self.slots = 1 << self.stages
        self.rows = self.seg_rows // count_tok
        self.rows_ff = self.seg_rows_ff // count_tok
        self.tok_here = self.rows % 16 == 0

    def recv_offset(self, stage):
        return self.slots - (self.slots >> stage)

    def slot(self, order, relative):
        total = 0
        for place, bit in enumerate(order):
            total = total + relative[bit] * (1 << (self.stages - 1 - place))
        return total


def bit_of(value, bit):
    return lax.rem(lax.div(value, 1 << bit), 2)


def flip(value, bit):
    return value + (1 - 2 * bit_of(value, bit)) * (1 << bit)


def seg_block(plan, seg, relative):
    total = bit_of(seg, plan.pair) * (1 << plan.pair)
    for bit, rel in relative.items():
        own = bit_of(seg, bit)
        total = total + (own + rel - 2 * own * rel) * (1 << bit)
    return total


def combos(bits):
    for index in range(1 << len(bits)):
        yield {bit: (index >> place) & 1 for place, bit in enumerate(bits)}


class Wire:
    def __init__(self, plan, seg, tok, own, recv, last, send_sem, recv_sem, far_send, far_recv):
        self.plan, self.seg, self.tok = plan, seg, tok
        self.own, self.recv, self.last = own, recv, last
        self.send_sem, self.recv_sem = send_sem, recv_sem
        self.far_send, self.far_recv = far_send, far_recv

    def views(self, chunk, half):
        kind, place = chunk[0], chunk[1]
        pick = 0 if kind == "S" else 1
        return (
            self.own[pick].at[place, half],
            self.recv[pick].at[place, half],
            self.last[pick].at[place, half],
        )

    def copy(self, chunk, half, stage):
        plan = self.plan
        own, recv, _ = self.views(chunk, half)
        size = plan.slots >> (stage + 1)
        return pltpu.make_async_remote_copy(
            src_ref=own.at[pl.ds(size, size)],
            dst_ref=recv.at[pl.ds(plan.recv_offset(stage), size)],
            send_sem=self.send_sem.at[chunk[2], half, stage],
            recv_sem=self.recv_sem.at[chunk[2], half, stage],
            device_id={"seg": flip(self.seg, plan.orders[half][stage])},
            device_id_type=MESH,
        )

    def far_copy(self, chunk, half, step):
        plan = self.plan
        own, _, last = self.views(chunk, half)
        rows = plan.rows if chunk[0] == "S" else plan.rows_ff
        target = lax.rem(self.tok + step, plan.count_tok)
        return pltpu.make_async_remote_copy(
            src_ref=own.at[0, pl.ds(pl.multiple_of(target * rows, rows), rows)],
            dst_ref=last.at[step - 1],
            send_sem=self.far_send.at[chunk[2], half, step - 1],
            recv_sem=self.far_recv.at[chunk[2], half, step - 1],
            device_id={"tok": target},
            device_id_type=MESH,
        )

    def start(self, chunk, stage):
        plan = self.plan
        for half in range(2):
            if stage < plan.stages:
                self.copy(chunk, half, stage).start()
            elif plan.tok_here:
                for step in range(1, plan.count_tok):
                    self.far_copy(chunk, half, step).start()

    def arrive(self, chunk, stage):
        plan = self.plan
        size = plan.slots >> (stage + 1)
        for half in range(2):
            self.copy(chunk, half, stage).wait()
            own, recv, _ = self.views(chunk, half)
            base = plan.recv_offset(stage)

            @pl.loop(0, size)
            def _(slot):
                total = own[slot].astype(jnp.float32) + recv[base + slot].astype(jnp.float32)
                own[slot] = total.astype(jnp.bfloat16)

        self.start(chunk, stage + 1)

    def finish(self, chunk, out_ref, column):
        plan = self.plan
        rows = plan.rows if chunk[0] == "S" else plan.rows_ff
        for half in range(2):
            own, _, last = self.views(chunk, half)
            wide = own.shape[-1]
            place = pl.ds(column + half * wide, wide)
            if not plan.tok_here:
                out_ref[:, place] = own[0].astype(jnp.float32)
                continue
            mine = pl.multiple_of(self.tok * rows, rows)
            total = own[0, pl.ds(mine, rows)].astype(jnp.float32)
            for step in range(1, plan.count_tok):
                self.far_copy(chunk, half, step).wait()
                total = total + last[step - 1].astype(jnp.float32)
            out_ref[:, place] = total


def greet(plan, seg, tok):
    barrier = pltpu.get_barrier_semaphore()
    for bit in range(plan.bits):
        pl.semaphore_signal(
            barrier, inc=1, device_id={"seg": flip(seg, bit)}, device_id_type=MESH
        )
    for step in range(1, plan.count_tok):
        pl.semaphore_signal(
            barrier,
            inc=1,
            device_id={"tok": lax.rem(tok + step, plan.count_tok)},
            device_id_type=MESH,
        )
    pl.semaphore_wait(barrier, plan.bits + plan.count_tok - 1)


def outer_chunk(plan, seg, chunk, wire, left, right, column):
    low = range(plan.low_bits)
    nsub = 1 << plan.low_bits
    high = [b for b in plan.rest if b >= plan.low_bits]
    wide = 512 if chunk[0] == "S" else 128
    rows = plan.seg_rows if chunk[0] == "S" else plan.seg_rows_ff
    for relative in combos(high):
        block = seg_block(plan, seg, relative)
        if chunk[0] == "S":
            block = lax.div(block, nsub)
            parts = [(rows * nsub, block, None)]
        else:
            parts = [(rows, block + sub, sub) for sub in range(nsub)]
        for span, index, sub in parts:
            start = pl.multiple_of(index * span, span)
            taken = left[:, pl.ds(start, span)]
            for half in range(2):
                result = lax.dot_general(
                    taken,
                    right[:, pl.ds(column + half * wide, wide)],
                    (((0,), (0,)), ((), ())),
                    preferred_element_type=jnp.float32,
                ).astype(jnp.bfloat16)
                own, _, _ = wire.views(chunk, half)
                for part in range(nsub) if sub is None else (sub,):
                    full = dict(relative)
                    for bit in low:
                        mine = bit_of(seg, bit)
                        want = (part >> bit) & 1
                        full[bit] = mine + want - 2 * mine * want
                    piece = result[part * rows : (part + 1) * rows] if sub is None else result
                    own[plan.slot(plan.orders[half], full)] = piece


CHUNKS = []
for _j in range(4):
    CHUNKS.append((("F", _j, len(CHUNKS)), 0, 256 * _j, "value", 256 * _j))
CHUNKS.append((("S", 0, len(CHUNKS)), 1, 0, "frecept", 0))
for _j in range(4):
    CHUNKS.append((("S", 1 + _j, len(CHUNKS)), 2, 1024 * _j, "fkey", 1024 * _j))
for _j, _name in enumerate(("out", "recept", "avalue", "akey")):
    CHUNKS.append((("S", 5 + _j, len(CHUNKS)), 3 + _j, 0, _name, 0))
NAMES = ("value", "frecept", "fkey", "out", "recept", "avalue", "akey")


def gradient_kernel(plan, *refs):
    lefts, refs = refs[:7], refs[7:]
    rights, refs = refs[:7], refs[7:]
    small_in, refs = refs[0], refs[1:]
    outs, refs = dict(zip(NAMES, refs[:7])), refs[7:]
    small_out, refs = refs[0], refs[1:]
    left_cat, refs = refs[:7], refs[7:]
    right_cat, refs = refs[:7], refs[7:]
    own, recv, last, refs = refs[:2], refs[2:4], refs[4:6], refs[6:]
    (small_recv, sems, far_sems, pair_sems, local_sems, small_sems) = refs
    seg, tok = lax.axis_index("seg"), lax.axis_index("tok")
    greet(plan, seg, tok)
    wire = Wire(
        plan, seg, tok, own, recv, last, sems.at[0], sems.at[1], far_sems.at[0], far_sems.at[1]
    )
    tokens = lefts[0].shape[0]
    partner = flip(seg, plan.pair)
    width = max(128, plan.seg_rows)
    blocks = EMBED_SIZE // width
    theirs = 1 - bit_of(seg, plan.pair)

    def pair_copies(index):
        wide = width * (lefts[index].shape[1] // EMBED_SIZE)
        for pick in range(blocks // 2):
            place = pl.ds(pl.multiple_of((2 * pick + theirs) * wide, wide), wide)
            yield (
                lefts[index].at[:, place],
                left_cat[index].at[pl.ds(tokens, tokens), place],
                pick,
            )
        yield (rights[index], right_cat[index].at[pl.ds(tokens, tokens)], blocks // 2)

    def pair_copy(index, item):
        source, target, number = item
        return pltpu.make_async_remote_copy(
            src_ref=source,
            dst_ref=target,
            send_sem=pair_sems.at[0, index, number],
            recv_sem=pair_sems.at[1, index, number],
            device_id={"seg": partner},
            device_id_type=MESH,
        )

    def local_copies(index):
        return (
            pltpu.make_async_copy(
                lefts[index], left_cat[index].at[pl.ds(0, tokens)], local_sems.at[0, index]
            ),
            pltpu.make_async_copy(
                rights[index], right_cat[index].at[pl.ds(0, tokens)], local_sems.at[1, index]
            ),
        )

    for index in range(7):
        for item in pair_copies(index):
            pair_copy(index, item).start()
        for copy in local_copies(index):
            copy.start()

    ready = set()
    for chunk, index, column, _, _ in CHUNKS:
        if index not in ready:
            ready.add(index)
            for item in pair_copies(index):
                pair_copy(index, item).wait()
            for copy in local_copies(index):
                copy.wait()
        outer_chunk(plan, seg, chunk, wire, left_cat[index], right_cat[index], column)
        wire.start(chunk, 0)

    small_out[...] = small_in[...]
    for bit in range(plan.bits):
        copy = pltpu.make_async_remote_copy(
            src_ref=small_out,
            dst_ref=small_recv.at[bit],
            send_sem=small_sems.at[0, bit],
            recv_sem=small_sems.at[1, bit],
            device_id={"seg": flip(seg, bit)},
            device_id_type=MESH,
        )
        copy.start()
        copy.wait()
        small_out[...] += small_recv[bit]
    copies = []
    for step in range(1, plan.count_tok):
        place = plan.bits + step - 1
        copies.append(
            pltpu.make_async_remote_copy(
                src_ref=small_out,
                dst_ref=small_recv.at[place],
                send_sem=small_sems.at[0, place],
                recv_sem=small_sems.at[1, place],
                device_id={"tok": lax.rem(tok + step, plan.count_tok)},
                device_id_type=MESH,
            )
        )
        copies[-1].start()
    for copy in copies:
        copy.wait()
    total = small_out[...]
    for step in range(1, plan.count_tok):
        total = total + small_recv[plan.bits + step - 1]
    small_out[...] = total

    count = len(CHUNKS)
    for turn in range(count + plan.stages):
        for stage in range(plan.stages):
            if 0 <= turn - stage < count:
                wire.arrive(CHUNKS[turn - stage][0], stage)
        if turn >= plan.stages:
            chunk, _, _, name, column = CHUNKS[turn - plan.stages]
            wire.finish(chunk, outs[name], column)


def gradient_sums(plan, lefts, rights, small):
    tokens = lefts[0].shape[0]
    rows = plan.rows if plan.tok_here else plan.seg_rows
    rows_ff = plan.rows_ff if plan.tok_here else plan.seg_rows_ff
    shapes = {name: (rows, EMBED_SIZE) for name in NAMES}
    shapes["fkey"] = (rows, FF)
    shapes["value"] = (rows_ff, EMBED_SIZE)
    out_shape = [jax.ShapeDtypeStruct(shapes[name], jnp.float32) for name in NAMES]
    out_shape.append(jax.ShapeDtypeStruct(small.shape, jnp.float32))
    far = max(1, plan.count_tok - 1)
    last_rows, last_rows_ff = (plan.rows, plan.rows_ff) if plan.tok_here else (16, 16)
    low = jnp.bfloat16
    halves = lambda kind, size, rows, wide: pltpu.VMEM((kind, 2, size, rows, wide), low)
    got = pl.pallas_call(
        partial(gradient_kernel, plan),
        out_shape=out_shape,
        in_specs=[pl.BlockSpec(memory_space=pl.ANY)] * 14
        + [pl.BlockSpec(memory_space=pltpu.VMEM)],
        out_specs=[pl.BlockSpec(memory_space=pltpu.VMEM)] * 8,
        scratch_shapes=[pltpu.VMEM((2 * tokens, item.shape[1]), low) for item in lefts]
        + [pltpu.VMEM((2 * tokens, item.shape[1]), low) for item in rights]
        + [
            halves(9, plan.slots, plan.seg_rows, 512),
            halves(4, plan.slots, plan.seg_rows_ff, 128),
            halves(9, plan.slots - 1, plan.seg_rows, 512),
            halves(4, plan.slots - 1, plan.seg_rows_ff, 128),
            halves(9, far, last_rows, 512),
            halves(4, far, last_rows_ff, 128),
            pltpu.VMEM((plan.bits + far,) + small.shape, jnp.float32),
            pltpu.SemaphoreType.DMA((2, len(CHUNKS), 2, plan.stages)),
            pltpu.SemaphoreType.DMA((2, len(CHUNKS), 2, far)),
            pltpu.SemaphoreType.DMA((2, 7, EMBED_SIZE // max(128, plan.seg_rows) // 2 + 1)),
            pltpu.SemaphoreType.DMA((2, 7)),
            pltpu.SemaphoreType.DMA((2, plan.bits + far)),
        ],
        compiler_params=pltpu.CompilerParams(
            collective_id=0, has_side_effects=True, vmem_limit_bytes=VMEM_BYTES
        ),
        cost_estimate=pl.CostEstimate(
            flops=2 * tokens * 13 * EMBED_SIZE * EMBED_SIZE,
            bytes_accessed=30 << 20,
            transcendentals=0,
        ),
    )(*lefts, *rights, small)
    sums = dict(zip(NAMES, got[:7]))
    if not plan.tok_here:
        sums = {
            name: lax.psum_scatter(item, "tok", scatter_dimension=0, tiled=True)
            for name, item in sums.items()
        }
    return sums, got[7]


def shards(
    incoming_items,
    upstream_slope,
    timemix_prior_entry,
    featmix_prior_entry,
    opening_dividend,
    opening_divisor,
    opening_power,
    normalize_scales,
    normalize_shifts,
    shift_blends,
    logarithmic_fading_speed,
    present_reward,
    timemix_lookup_coeffs,
    timemix_payload_coeffs,
    timemix_accept_coeffs,
    timemix_emit_coeffs,
    featmix_lookup_coeffs,
    featmix_payload_coeffs,
    featmix_accept_coeffs,
):
    at_start = lax.axis_index("tok") == 0
    inputs32 = incoming_items.astype(jnp.float32)
    normed32, norm_pull = jax.vjp(layer_norm, inputs32, normalize_scales[0], normalize_shifts[0])
    normed = normed32.astype(jnp.bfloat16)
    arrived = passed_along(normed[:, -1, :], "tok", 1)
    lead_row = jnp.where(at_start, timemix_prior_entry, arrived)
    before = jnp.concatenate([lead_row[:, None, :], normed[:, :-1, :]], axis=1)
    normed_low = normed.astype(jnp.float32)
    before_low = before.astype(jnp.float32)
    key_mix = blend(normed_low, before_low, shift_blends[0]).astype(jnp.bfloat16)
    value_mix = blend(normed_low, before_low, shift_blends[1]).astype(jnp.bfloat16)
    recept_mix = blend(normed_low, before_low, shift_blends[2]).astype(jnp.bfloat16)
    lookup_mapped = dense(key_mix, timemix_lookup_coeffs).astype(jnp.bfloat16)
    payload_mapped = dense(value_mix, timemix_payload_coeffs).astype(jnp.bfloat16)
    recept = jax.nn.sigmoid(dense(recept_mix, timemix_accept_coeffs))
    key_chan, value_chan = (
        lax.all_to_all(lookup_mapped, "tok", split_axis=2, concat_axis=1, tiled=True),
        lax.all_to_all(payload_mapped, "tok", split_axis=2, concat_axis=1, tiled=True),
    )
    portion_breadth = key_chan.shape[2]
    lateral_displacement = lax.axis_index("tok") * portion_breadth
    fading_portion = lax.dynamic_slice_in_dim(
        logarithmic_fading_speed, lateral_displacement, portion_breadth
    )
    reward_portion = lax.dynamic_slice_in_dim(present_reward, lateral_displacement, portion_breadth)
    first_feature = (opening_dividend, opening_divisor, opening_power)
    wkv_chan, recurrence_backward, closing_memories = jax.vjp(
        partial(portion_iteration, first_feature=first_feature),
        key_chan.astype(jnp.float32),
        value_chan.astype(jnp.float32),
        fading_portion,
        reward_portion,
        has_aux=True,
    )
    blended_entries = lax.all_to_all(
        wkv_chan.astype(jnp.bfloat16), "tok", split_axis=1, concat_axis=2, tiled=True
    )
    mixed_low = blended_entries.astype(jnp.float32)
    weighted = (recept * mixed_low).astype(jnp.bfloat16)
    middle = inputs32 + dense(weighted, timemix_emit_coeffs)
    normed_two32, norm_pull_two = jax.vjp(
        layer_norm, middle, normalize_scales[1], normalize_shifts[1]
    )
    normed_two = normed_two32.astype(jnp.bfloat16)
    arrived_two = passed_along(normed_two[:, -1, :], "tok", 1)
    lead_two = jnp.where(at_start, featmix_prior_entry, arrived_two)
    before_two = jnp.concatenate([lead_two[:, None, :], normed_two[:, :-1, :]], axis=1)
    normed_two_low = normed_two.astype(jnp.float32)
    before_two_low = before_two.astype(jnp.float32)
    key_two = blend(normed_two_low, before_two_low, shift_blends[3]).astype(jnp.bfloat16)
    recept_two = blend(normed_two_low, before_two_low, shift_blends[4]).astype(jnp.bfloat16)
    hidden = dense(key_two, featmix_lookup_coeffs)
    squared = jnp.square(jax.nn.relu(hidden)).astype(jnp.bfloat16)
    handed_memory = dense(squared, featmix_payload_coeffs)
    gate_two = jax.nn.sigmoid(dense(recept_two, featmix_accept_coeffs))
    layer_out = (middle + gate_two * handed_memory).astype(jnp.bfloat16)
    upstream = upstream_slope.astype(jnp.float32)
    grad_carried = (upstream * gate_two).astype(jnp.bfloat16)
    grad_gate = (upstream * handed_memory * gate_two * (1.0 - gate_two)).astype(jnp.bfloat16)
    grad_hidden = (
        dense_back(grad_carried, featmix_payload_coeffs) * 2.0 * jax.nn.relu(hidden)
    ).astype(jnp.bfloat16)
    direct_two, across_two, mix_sums_two = unmix(
        (
            dense_back(grad_hidden, featmix_lookup_coeffs),
            dense_back(grad_gate, featmix_accept_coeffs),
        ),
        (shift_blends[3], shift_blends[4]),
        normed_two_low,
        before_two_low,
    )
    returned_two = passed_along(across_two[:, 0, :], "tok", -1)
    grad_normed_two = direct_two + jnp.concatenate(
        [across_two[:, 1:, :], returned_two[:, None, :]], axis=1
    ).astype(jnp.float32)
    grad_middle_norm, gain_two, bias_two = norm_pull_two(grad_normed_two)
    grad_middle = upstream + grad_middle_norm
    grad_branch = grad_middle.astype(jnp.bfloat16)
    grad_weighted = dense_back(grad_branch, timemix_emit_coeffs)
    grad_mixed = (grad_weighted * recept).astype(jnp.bfloat16)
    grad_recept = (grad_weighted * mixed_low * recept * (1.0 - recept)).astype(jnp.bfloat16)
    grad_mixed_chan = lax.all_to_all(grad_mixed, "tok", split_axis=2, concat_axis=1, tiled=True)
    lookup_feature_slope, payload_feature_slope, fading_portion_slope, reward_portion_slope = (
        recurrence_backward(grad_mixed_chan.astype(jnp.float32))
    )
    grad_key, grad_value = (
        lax.all_to_all(
            lookup_feature_slope.astype(jnp.bfloat16),
            "tok",
            split_axis=1,
            concat_axis=2,
            tiled=True,
        ),
        lax.all_to_all(
            payload_feature_slope.astype(jnp.bfloat16),
            "tok",
            split_axis=1,
            concat_axis=2,
            tiled=True,
        ),
    )
    direct_one, across_one, mix_sums_one = unmix(
        (
            dense_back(grad_key, timemix_lookup_coeffs),
            dense_back(grad_value, timemix_payload_coeffs),
            dense_back(grad_recept, timemix_accept_coeffs),
        ),
        (shift_blends[0], shift_blends[1], shift_blends[2]),
        normed_low,
        before_low,
    )
    returned_one = passed_along(across_one[:, 0, :], "tok", -1)
    grad_normed = direct_one + jnp.concatenate(
        [across_one[:, 1:, :], returned_one[:, None, :]], axis=1
    ).astype(jnp.float32)
    grad_inputs, gain_one, bias_one = norm_pull(grad_normed)
    token_grad = (grad_middle + grad_inputs).astype(jnp.bfloat16)
    gain_grads = jnp.stack([gain_one, gain_two])
    bias_grads = jnp.stack([bias_one, bias_two])
    mix_grads = jnp.stack(mix_sums_one + mix_sums_two)
    decay_full = lax.dynamic_update_slice_in_dim(
        jnp.zeros(logarithmic_fading_speed.shape, jnp.float32),
        fading_portion_slope,
        lateral_displacement,
        0,
    )
    entire_reward = lax.dynamic_update_slice_in_dim(
        jnp.zeros(present_reward.shape, jnp.float32), reward_portion_slope, lateral_displacement, 0
    )
    plan = Plan(lax.axis_size("seg"), lax.axis_size("tok"))
    flat = lambda item: item[0]
    small = jnp.concatenate(
        [gain_grads, bias_grads, mix_grads, decay_full[None], entire_reward[None]]
        + [jnp.zeros((5, EMBED_SIZE), jnp.float32)]
    )
    sums, small = gradient_sums(
        plan,
        [flat(x) for x in (squared, recept_two, key_two, weighted, recept_mix, value_mix, key_mix)],
        [
            flat(x)
            for x in (
                grad_carried,
                grad_gate,
                grad_hidden,
                grad_branch,
                grad_recept,
                grad_value,
                grad_key,
            )
        ],
        small,
    )
    share = EMBED_SIZE // (plan.count_seg * plan.count_tok)
    place = (lax.axis_index("seg") * plan.count_tok + lax.axis_index("tok")) * share
    small = lax.dynamic_slice_in_dim(small, place, share, 1)
    return (
        layer_out,
        token_grad,
        closing_memories[0],
        closing_memories[1],
        closing_memories[2],
        small[0:2],
        small[2:4],
        small[4:9],
        small[9],
        small[10],
        sums["akey"],
        sums["avalue"],
        sums["recept"],
        sums["out"],
        sums["fkey"],
        sums["value"],
        sums["frecept"],
    )


def solution(mesh):
    return jax.shard_map(
        shards,
        mesh=mesh,
        in_specs=(
            P("seg", "tok", None),
            P("seg", "tok", None),
            P("seg", None),
            P("seg", None),
            P("seg", "tok"),
            P("seg", "tok"),
            P("seg", "tok"),
            P(),
            P(),
            P(),
            P(),
            P(),
            P(),
            P(),
            P(),
            P(),
            P(),
            P(),
            P(),
        ),
        out_specs=(
            P("seg", "tok", None),
            P("seg", "tok", None),
            P("seg", "tok"),
            P("seg", "tok"),
            P("seg", "tok"),
            P(None, ("seg", "tok")),
            P(None, ("seg", "tok")),
            P(None, ("seg", "tok")),
            P(("seg", "tok")),
            P(("seg", "tok")),
            P(("seg", "tok"), None),
            P(("seg", "tok"), None),
            P(("seg", "tok"), None),
            P(("seg", "tok"), None),
            P(("seg", "tok"), None),
            P(("seg", "tok"), None),
            P(("seg", "tok"), None),
        ),
        check_vma=False,
    )
```

```python
from functools import partial
from typing import Any, NamedTuple

import jax
import jax.numpy as jnp
from jax import lax
from jax.experimental import pallas as pl
from jax.experimental.pallas import tpu as pltpu
from jax.sharding import PartitionSpec as P

EMBED_SIZE = 1024
FF = 4096
VMEM_BYTES = 62 << 20
MESH = pl.DeviceIdType.MESH


class Plan:
    def __init__(self, count_seg, count_tok):
        self.count_seg, self.count_tok = count_seg, count_tok
        self.bits = count_seg.bit_length() - 1
        self.seg_rows = EMBED_SIZE // count_seg
        self.seg_rows_ff = FF // count_seg
        self.low_bits = max(0, (128 // self.seg_rows).bit_length() - 1)
        self.pair = self.low_bits
        self.rest = [b for b in range(self.bits) if b != self.pair]
        self.orders = (self.rest, self.rest[::-1])
        self.stages = len(self.rest)
        self.slots = 1 << self.stages
        self.rows = self.seg_rows // count_tok
        self.rows_ff = self.seg_rows_ff // count_tok
        self.tok_here = self.rows % 16 == 0

    def recv_offset(self, stage):
        return self.slots - (self.slots >> stage)

    def slot(self, order, relative):
        total = 0
        for place, bit in enumerate(order):
            total = total + relative[bit] * (1 << (self.stages - 1 - place))
        return total


def bit_of(value, bit):
    return lax.rem(lax.div(value, 1 << bit), 2)


def flip(value, bit):
    return value + (1 - 2 * bit_of(value, bit)) * (1 << bit)


def seg_block(plan, seg, relative):
    total = bit_of(seg, plan.pair) * (1 << plan.pair)
    for bit, rel in relative.items():
        own = bit_of(seg, bit)
        total = total + (own + rel - 2 * own * rel) * (1 << bit)
    return total


def combos(bits):
    for index in range(1 << len(bits)):
        yield {bit: (index >> place) & 1 for place, bit in enumerate(bits)}


def greet(plan, seg, tok):
    barrier = pltpu.get_barrier_semaphore()
    for bit in range(plan.bits):
        pl.semaphore_signal(
            barrier, inc=1, device_id={"seg": flip(seg, bit)}, device_id_type=MESH
        )
    for step in range(1, plan.count_tok):
        pl.semaphore_signal(
            barrier,
            inc=1,
            device_id={"tok": lax.rem(tok + step, plan.count_tok)},
            device_id_type=MESH,
        )
    pl.semaphore_wait(barrier, plan.bits + plan.count_tok - 1)


class Copies:
    def __init__(self, local_sems, send_sems, recv_sems):
        self.local_sems, self.send_sems, self.recv_sems = local_sems, send_sems, recv_sems
        self.locals, self.remotes, self.open = 0, 0, []

    def local(self, source, target):
        copy = pltpu.make_async_copy(source, target, self.local_sems.at[self.locals])
        self.locals += 1
        copy.start()
        self.open.append(copy)
        return copy

    def remote(self, source, target, device):
        copy = pltpu.make_async_remote_copy(
            src_ref=source,
            dst_ref=target,
            send_sem=self.send_sems.at[self.remotes],
            recv_sem=self.recv_sems.at[self.remotes],
            device_id=device,
            device_id_type=MESH,
        )
        self.remotes += 1
        copy.start()
        self.open.append(copy)
        return copy

    def wait(self, *copies):
        for copy in copies:
            copy.wait()
            self.open = [item for item in self.open if item is not copy]

    def drain(self):
        self.wait(*list(self.open))


def rows16(index):
    return pl.ds(pl.multiple_of(index * 16, 16), 16)


def rows8(index):
    return pl.ds(pl.multiple_of(index * 8, 8), 8)


LANES = EMBED_SIZE // 128


def put_rows(staged, place, value):
    for block in range(LANES):
        staged[block, place] = value[:, 128 * block : 128 * block + 128]


def get_rows(staged, place):
    return jnp.concatenate([staged[block, place] for block in range(LANES)], axis=1)


def low(value):
    return value.astype(jnp.bfloat16).astype(jnp.float32)


def layer_norm(values, gain_row, bias_row):
    centre = values - jnp.mean(values, axis=-1, keepdims=True)
    spread = jnp.mean(centre * centre, axis=-1, keepdims=True)
    return centre * lax.rsqrt(spread + 1e-05) * gain_row + bias_row


def sweep(count, body, unroll=2):
    def step(index, carry):
        body(index)
        return carry

    lax.fori_loop(0, count, step, 0, unroll=unroll)


def matmul(left, right):
    return jnp.dot(left, right, preferred_element_type=jnp.float32)


def matmul_back(left, right):
    return lax.dot_general(
        left, right, (((1,), (1,)), ((), ())), preferred_element_type=jnp.float32
    )


def merge(state, later, faded):
    numer, denom, top = state
    reduced = top - faded
    peak = jnp.maximum(reduced, later[2])
    old, new = jnp.exp(reduced - peak), jnp.exp(later[2] - peak)
    return (old * numer + new * later[0], old * denom + new * later[1], peak)


def advance(state, key, value, fading):
    numer, denom, top = state
    reduced = top - fading
    peak = jnp.maximum(reduced, key)
    old, new = jnp.exp(reduced - peak), jnp.exp(key - peak)
    return (old * numer + new * value, old * denom + new, peak)


def row_of(state, index):
    return tuple(item[index : index + 1] for item in state)


def stack_rows(states):
    return tuple(jnp.concatenate([state[part] for state in states]) for part in range(len(states[0])))


def first_before(lead_row, last_tile):
    return jnp.concatenate([lead_row, last_tile[0:7]])


class ForwardRefs(NamedTuple):
    x: Any
    up: Any
    prior_one: Any
    prior_two: Any
    open_num: Any
    open_den: Any
    open_top: Any
    scales: Any
    shifts: Any
    blends: Any
    speed: Any
    reward: Any
    wk: Any
    wv: Any
    wr: Any
    wo: Any
    wl: Any
    wp: Any
    wa: Any
    layer_out: Any
    final: Any
    cat_squared: Any
    cat_recept_two: Any
    cat_key_two: Any
    cat_weighted: Any
    cat_recept_mix: Any
    cat_value_mix: Any
    cat_key_mix: Any
    cat_carried: Any
    cat_gate: Any
    sq_out: Any
    out_kf: Any
    out_vf: Any
    out_recept: Any
    out_mixed: Any
    out_xp: Any
    out_middle: Any
    out_upf: Any
    out_nf: Any
    out_nf2: Any
    out_entry: Any
    xb: Any
    ub: Any
    xs: Any
    xp: Any
    nf: Any
    nf2: Any
    kf: Any
    vf: Any
    recept: Any
    mixed: Any
    middle: Any
    upf: Any
    gate: Any
    carried: Any
    key_mix: Any
    value_mix: Any
    recept_mix: Any
    weighted: Any
    key_two: Any
    recept_two: Any
    sq: Any
    gc: Any
    gg: Any
    vk: Any
    vv: Any
    vr: Any
    vo: Any
    vl: Any
    vp: Any
    va: Any
    row_out: Any
    row_in: Any
    row_two_out: Any
    row_two_in: Any
    state_out: Any
    state_in: Any
    entry: Any
    whole: Any
    local_sems: Any
    send_sems: Any
    recv_sems: Any


class ForwardOut(NamedTuple):
    layer_out: Any
    final: Any
    cat_squared: Any
    cat_recept_two: Any
    cat_key_two: Any
    cat_weighted: Any
    cat_recept_mix: Any
    cat_value_mix: Any
    cat_key_mix: Any
    cat_carried: Any
    cat_gate: Any
    sq_out: Any
    out_kf: Any
    out_vf: Any
    out_recept: Any
    out_mixed: Any
    out_xp: Any
    out_middle: Any
    out_upf: Any
    out_nf: Any
    out_nf2: Any
    out_entry: Any


def right_of(plan, tok):
    return {"tok": lax.rem(tok + 1, plan.count_tok)}


def left_of(plan, tok):
    return {"tok": lax.rem(tok + plan.count_tok - 1, plan.count_tok)}


def forward_kernel(plan, *refs):
    r = ForwardRefs(*refs)
    seg, tok = lax.axis_index("seg"), lax.axis_index("tok")
    tokens = r.xs.shape[1]
    steps = tokens // 8
    every = lambda i: pl.ds(i, 8, stride=steps)
    pairs = tokens // 16
    copies = Copies(r.local_sems, r.send_sems, r.recv_sems)
    load_x = copies.local(r.x, r.xb)
    load_k, load_v = copies.local(r.wk, r.vk), copies.local(r.wv, r.vv)
    load_r, load_o = copies.local(r.wr, r.vr), copies.local(r.wo, r.vo)
    load_a = copies.local(r.wa, r.va)
    load_up = copies.local(r.up, r.ub)
    load_l = [copies.local(r.wl.at[:, pl.ds(1024 * j, 1024)], r.vl.at[j]) for j in range(4)]
    load_p = [copies.local(r.wp.at[pl.ds(1024 * j, 1024)], r.vp.at[j]) for j in range(4)]
    greet(plan, seg, tok)
    partner = {"seg": flip(seg, plan.pair)}
    mine = bit_of(seg, plan.pair)

    def share(source, target, wide, at=0):
        count = source.shape[1] // (2 * wide)
        for pick in range(count):
            own = pl.ds(pl.multiple_of((2 * pick + mine) * wide, wide), wide)
            other = pl.ds(pl.multiple_of((2 * pick + 1 - mine) * wide, wide), wide)
            place = pl.ds((at + pick) * wide, wide)
            copies.local(source.at[:, own], target.at[pl.ds(0, tokens), place])
            copies.remote(source.at[:, other], target.at[pl.ds(tokens, tokens), place], partner)

    def both(source, target):
        copies.local(source, target.at[pl.ds(0, tokens)])
        copies.remote(source, target.at[pl.ds(tokens, tokens)], partner)

    wide = max(128, plan.seg_rows)

    copies.wait(load_x)

    def widen(i):
        put_rows(r.xs, rows16(i), r.xb[rows16(i)].astype(jnp.float32))

    sweep(pairs, widen)
    gain, bias = r.scales[0:1], r.shifts[0:1]

    def norm_one(i):
        tile = get_rows(r.xs, every(i))
        r.xp[rows8(i)] = tile
        r.nf[rows8(i + 1)] = low(layer_norm(tile, gain, bias))

    norm_one(steps - 1)
    r.row_out[...] = r.nf[pl.ds(8 * steps, 8)]
    row = copies.remote(r.row_out, r.row_in, right_of(plan, tok))
    sweep(steps - 1, norm_one, 3)
    copies.wait(row)
    lead = jnp.where(tok == 0, r.prior_one[...].astype(jnp.float32), r.row_in[7:8])
    r.nf[0:8] = first_before(lead, r.nf[pl.ds(8 * steps, 8)])

    def mix_one(i):
        before = r.nf[pl.ds(pl.multiple_of(i * 16, 16), 16)]
        normed = r.nf[pl.ds(pl.multiple_of(i * 16 + 8, 8), 16)]
        for place, target in enumerate((r.key_mix, r.value_mix, r.recept_mix)):
            weight = r.blends[place : place + 1]
            target[rows16(i)] = (normed * weight + before * (1.0 - weight)).astype(jnp.bfloat16)

    sweep(pairs, mix_one)
    share(r.key_mix, r.cat_key_mix, wide)
    share(r.value_mix, r.cat_value_mix, wide)
    share(r.recept_mix, r.cat_recept_mix, wide)
    copies.local(r.xp, r.out_xp)
    copies.local(r.nf, r.out_nf)
    copies.wait(load_k)
    r.kf[...] = low(matmul(r.key_mix[...], r.vk[...]))
    copies.wait(load_v)
    r.vf[...] = low(matmul(r.value_mix[...], r.vv[...]))
    copies.local(r.kf, r.out_kf)
    copies.local(r.vf, r.out_vf)

    fading_row = jnp.exp(r.speed[...])
    fading = jnp.broadcast_to(fading_row, (8, EMBED_SIZE))
    reward = jnp.broadcast_to(r.reward[...], (8, EMBED_SIZE))
    zero = jnp.zeros((8, EMBED_SIZE), jnp.float32)

    def alone(i, state):
        return advance(state, r.kf[rows8(i)], r.vf[rows8(i)], fading)

    stretches = lax.fori_loop(0, steps, alone, (zero, zero, zero - 1e30), unroll=2)
    stretch_fade = fading_row * steps
    total = row_of(stretches, 0)
    for j in range(1, 8):
        total = merge(total, row_of(stretches, j), stretch_fade)
    portion = EMBED_SIZE // plan.count_tok
    lanes = pl.ds(pl.multiple_of(tok * portion, portion), portion)
    r.state_out[...] = zero
    for part, opening in enumerate((r.open_num, r.open_den, r.open_top)):
        r.state_out[part : part + 1] = total[part]
        r.state_out[3 + part : 4 + part, lanes] = opening[...]
    sent = [
        copies.remote(
            r.state_out, r.state_in.at[tok], {"tok": lax.rem(tok + step, plan.count_tok)}
        )
        for step in range(1, plan.count_tok)
    ]
    r.state_in[tok] = r.state_out[...]
    copies.wait(load_r)
    r.recept[...] = jax.nn.sigmoid(matmul(r.recept_mix[...], r.vr[...]))
    copies.local(r.recept, r.out_recept)
    copies.wait(*sent)
    state = tuple(
        sum(r.state_in[z, 3 + part : 4 + part] for z in range(plan.count_tok)) for part in range(3)
    )
    entry = state
    for z in range(plan.count_tok):
        entry = tuple(jnp.where(tok == z, new, old) for new, old in zip(state, entry))
        later = tuple(r.state_in[z, part : part + 1] for part in range(3))
        state = merge(state, later, fading_row * tokens)
    r.whole[...] = zero
    for part in range(3):
        r.whole[part : part + 1] = state[part]
    r.final[...] = r.whole[:, lanes]
    entries = [entry]
    for j in range(7):
        entries.append(merge(entries[-1], row_of(stretches, j), stretch_fade))
    entries = stack_rows(entries)
    for part in range(3):
        r.entry[8 * part : 8 * part + 8] = entries[part]
    keep_entry = copies.local(r.entry, r.out_entry)

    def emit(state, i):
        key, value = r.kf[rows8(i)], r.vf[rows8(i)]
        present = reward + key
        peak = jnp.maximum(state[2], present)
        old, new = jnp.exp(state[2] - peak), jnp.exp(present - peak)
        result = (old * state[0] + new * value) / (old * state[1] + new)
        return advance(state, key, value, fading), low(result)

    def recur(i, state):
        state, one = emit(state, 2 * i)
        state, two = emit(state, 2 * i + 1)
        both_rows = jnp.concatenate([one, two])
        r.mixed[rows16(i)] = both_rows
        r.weighted[rows16(i)] = (r.recept[rows16(i)] * both_rows).astype(jnp.bfloat16)
        return state

    lax.fori_loop(0, pairs, recur, entries)
    share(r.weighted, r.cat_weighted, wide)
    copies.local(r.mixed, r.out_mixed)
    copies.wait(load_o)
    r.middle[...] = r.xp[...] + matmul(r.weighted[...], r.vo[...])
    copies.local(r.middle, r.out_middle)

    gain_two, bias_two = r.scales[1:2], r.shifts[1:2]

    def norm_two(i):
        r.nf2[rows8(i + 1)] = low(layer_norm(r.middle[rows8(i)], gain_two, bias_two))

    norm_two(steps - 1)
    r.row_two_out[...] = r.nf2[pl.ds(8 * steps, 8)]
    row = copies.remote(r.row_two_out, r.row_two_in, right_of(plan, tok))
    sweep(steps - 1, norm_two, 3)
    copies.wait(row)
    lead = jnp.where(tok == 0, r.prior_two[...].astype(jnp.float32), r.row_two_in[7:8])
    r.nf2[0:8] = first_before(lead, r.nf2[pl.ds(8 * steps, 8)])

    def mix_two(i):
        before = r.nf2[pl.ds(pl.multiple_of(i * 16, 16), 16)]
        normed = r.nf2[pl.ds(pl.multiple_of(i * 16 + 8, 8), 16)]
        for place, target in ((3, r.key_two), (4, r.recept_two)):
            weight = r.blends[place : place + 1]
            target[rows16(i)] = (normed * weight + before * (1.0 - weight)).astype(jnp.bfloat16)

    sweep(pairs, mix_two)
    share(r.key_two, r.cat_key_two, wide)
    share(r.recept_two, r.cat_recept_two, wide)
    copies.local(r.nf2, r.out_nf2)
    copies.wait(load_a)
    r.gate[...] = jax.nn.sigmoid(matmul(r.recept_two[...], r.va[...]))
    copies.wait(load_up)

    def widen_up(i):
        put_rows(r.xs, rows16(i), r.ub[rows16(i)].astype(jnp.float32))

    sweep(pairs, widen_up)

    def carried_slope(i):
        up = jnp.concatenate(
            [get_rows(r.xs, every(2 * i)), get_rows(r.xs, every(2 * i + 1))]
        )
        r.upf[rows16(i)] = up
        r.gc[rows16(i)] = (up * r.gate[rows16(i)]).astype(jnp.bfloat16)

    sweep(pairs, carried_slope)
    both(r.gc, r.cat_carried)
    copies.local(r.upf, r.out_upf)
    for j in range(4):
        copies.wait(load_l[j])
        hidden = jnp.maximum(matmul(r.key_two[...], r.vl[j]), 0.0)
        r.sq[j] = (hidden * hidden).astype(jnp.bfloat16)
        share(r.sq.at[j], r.cat_squared, 4 * wide, j)
    copies.local(r.sq, r.sq_out)
    for j in range(4):
        copies.wait(load_p[j])
        part = matmul(r.sq[j], r.vp[j])
        r.carried[...] = part if j == 0 else r.carried[...] + part

    def close(i):
        gate, carried = r.gate[rows16(i)], r.carried[rows16(i)]
        gated = gate * carried
        result = r.middle[rows16(i)] + gated
        r.gg[rows16(i)] = (r.upf[rows16(i)] * gated * (1.0 - gate)).astype(jnp.bfloat16)
        put_rows(r.xs, every(2 * i), result[0:8])
        put_rows(r.xs, every(2 * i + 1), result[8:16])

    sweep(pairs, close)
    both(r.gg, r.cat_gate)

    def narrow(i):
        r.layer_out[rows16(i)] = get_rows(r.xs, rows16(i)).astype(jnp.bfloat16)

    sweep(pairs, narrow)
    copies.drain()


def forward(plan, arrays, tokens):
    f32, b16 = jnp.float32, jnp.bfloat16
    wide, half = (tokens, EMBED_SIZE), EMBED_SIZE // 2
    anywhere, vmem = pl.BlockSpec(memory_space=pl.ANY), pl.BlockSpec(memory_space=pltpu.VMEM)
    sds = jax.ShapeDtypeStruct
    out_shape = [sds(wide, b16), sds((8, EMBED_SIZE // plan.count_tok), f32)]
    out_shape += [sds((2 * tokens, FF // 2), b16)] + [sds((2 * tokens, half), b16)] * 6
    out_shape += [sds((2 * tokens, EMBED_SIZE), b16)] * 2 + [sds((4,) + wide, b16)]
    out_shape += [sds(wide, f32)] * 7
    out_shape += [sds((tokens + 8, EMBED_SIZE), f32)] * 2 + [sds((24, EMBED_SIZE), f32)]
    weight = pltpu.VMEM((EMBED_SIZE, EMBED_SIZE), b16)
    tile = pltpu.VMEM((8, EMBED_SIZE), f32)
    scratch = [pltpu.VMEM(wide, b16)] * 2
    scratch += [pltpu.VMEM((LANES, tokens, 128), f32), pltpu.VMEM(wide, f32)]
    scratch += [pltpu.VMEM((tokens + 8, EMBED_SIZE), f32)] * 2 + [pltpu.VMEM(wide, f32)] * 8
    scratch += [pltpu.VMEM(wide, b16)] * 6 + [pltpu.VMEM((4,) + wide, b16)]
    scratch += [pltpu.VMEM(wide, b16)] * 2 + [weight] * 4
    scratch += [pltpu.VMEM((4, EMBED_SIZE, EMBED_SIZE), b16)] * 2 + [weight]
    scratch += [tile] * 5 + [pltpu.VMEM((plan.count_tok, 8, EMBED_SIZE), f32)]
    scratch += [pltpu.VMEM((24, EMBED_SIZE), f32), tile]
    scratch += [pltpu.SemaphoreType.DMA((80,))] * 3
    got = pl.pallas_call(
        partial(forward_kernel, plan),
        out_shape=out_shape,
        in_specs=[anywhere] * 2 + [vmem] * 10 + [anywhere] * 7,
        out_specs=[vmem] * 2 + [anywhere] * (len(out_shape) - 2),
        scratch_shapes=scratch,
        compiler_params=pltpu.CompilerParams(
            collective_id=0, has_side_effects=True, vmem_limit_bytes=VMEM_BYTES
        ),
    )(*arrays)
    return ForwardOut(*got)


class Chunk:
    def __init__(self, number, ref, lane, wide, unit, share, out, column):
        self.number, self.ref, self.lane, self.wide = number, ref, lane, wide
        self.unit, self.share, self.out, self.column = unit, share, out, column


class Wire:
    RATE = 92e3
    LAG = 1.5
    BACKLOG = 5.0

    def __init__(self, plan, seg, tok, sems, far_sems):
        self.plan, self.seg, self.tok = plan, seg, tok
        self.send_sem, self.recv_sem = sems.at[0], sems.at[1]
        self.far_send, self.far_recv = far_sems.at[0], far_sems.at[1]
        self.clock, self.free = 0.0, {}
        self.waiting, self.flying = [], []

    def load(self, axis, amount):
        self.free[axis] = max(self.clock, self.free.get(axis, 0.0)) + amount / self.RATE
        return self.free[axis] + self.LAG

    def fly(self, arrival, action):
        self.flying.append((arrival, len(self.flying), action))

    def offer(self, chunk):
        self.waiting.append(chunk)
        self.serve()

    def tick(self, cost):
        self.clock += cost
        self.serve()

    def room(self):
        first = {order[0] for order in self.plan.orders}
        return min(self.free.get(axis, 0.0) for axis in first) - self.clock < self.BACKLOG

    def serve(self, rest=False):
        while self.flying or self.waiting:
            if self.waiting and self.room():
                self.start(self.waiting.pop(0))
                continue
            if not self.flying:
                break
            soonest = min(self.flying, key=lambda item: item[0])
            if soonest[0] > self.clock and not rest:
                break
            self.clock = max(self.clock, soonest[0])
            self.flying.remove(soonest)
            soonest[2]()

    def lanes(self, chunk, half):
        return pl.ds(chunk.lane + half * chunk.wide, chunk.wide)

    def recv_row(self, chunk, stage):
        return (self.plan.slots + self.plan.recv_offset(stage)) * chunk.unit

    def copy(self, chunk, half, stage):
        rows = (self.plan.slots >> (stage + 1)) * chunk.unit
        lanes = self.lanes(chunk, half)
        return pltpu.make_async_remote_copy(
            src_ref=chunk.ref.at[pl.ds(rows, rows), lanes],
            dst_ref=chunk.ref.at[pl.ds(self.recv_row(chunk, stage), rows), lanes],
            send_sem=self.send_sem.at[chunk.number, half, stage],
            recv_sem=self.recv_sem.at[chunk.number, half, stage],
            device_id={"seg": flip(self.seg, self.plan.orders[half][stage])},
            device_id_type=MESH,
        )

    def far_row(self, chunk, step):
        return (2 * self.plan.slots - 1) * chunk.unit + (step - 1) * chunk.share

    def far_copy(self, chunk, half, step):
        target = lax.rem(self.tok + step, self.plan.count_tok)
        lanes = self.lanes(chunk, half)
        start = pl.multiple_of(target * chunk.share, chunk.share)
        return pltpu.make_async_remote_copy(
            src_ref=chunk.ref.at[pl.ds(start, chunk.share), lanes],
            dst_ref=chunk.ref.at[pl.ds(self.far_row(chunk, step), chunk.share), lanes],
            send_sem=self.far_send.at[chunk.number, half, step - 1],
            recv_sem=self.far_recv.at[chunk.number, half, step - 1],
            device_id={"tok": target},
            device_id_type=MESH,
        )

    def start(self, chunk, stage=0):
        plan, arrivals = self.plan, [self.clock]
        for half in range(2):
            if stage < plan.stages:
                self.copy(chunk, half, stage).start()
                amount = (plan.slots >> (stage + 1)) * chunk.unit * chunk.wide * 4
                arrivals.append(self.load(plan.orders[half][stage], amount))
            elif plan.tok_here:
                for step in range(1, plan.count_tok):
                    self.far_copy(chunk, half, step).start()
                amount = chunk.share * chunk.wide * plan.count_tok * plan.count_tok
                arrivals.append(self.load(-1, amount))
        if stage < plan.stages:
            self.fly(max(arrivals), lambda: self.arrive(chunk, stage))
        else:
            self.fly(max(arrivals), lambda: self.finish(chunk))

    def arrive(self, chunk, stage):
        rows = (self.plan.slots >> (stage + 1)) * chunk.unit
        block = min(rows, 32768 // chunk.wide)
        for half in range(2):
            self.copy(chunk, half, stage).wait()
            lanes, base = self.lanes(chunk, half), self.recv_row(chunk, stage)

            def add(index):
                near = pl.ds(pl.multiple_of(index * block, block), block)
                came = pl.ds(pl.multiple_of(base + index * block, 16), block)
                total = chunk.ref[near, lanes].astype(jnp.float32)
                total = total + chunk.ref[came, lanes].astype(jnp.float32)
                chunk.ref[near, lanes] = total.astype(jnp.bfloat16)

            sweep(rows // block, add, 1)
        self.clock += 0.35 if stage == 0 else 0.2
        self.start(chunk, stage + 1)

    def finish(self, chunk):
        plan = self.plan
        for half in range(2):
            lanes = self.lanes(chunk, half)
            place = pl.ds(chunk.column + half * chunk.wide, chunk.wide)
            if not plan.tok_here:
                chunk.out[:, place] = chunk.ref[pl.ds(0, chunk.unit), lanes].astype(jnp.float32)
                continue
            mine = pl.ds(pl.multiple_of(self.tok * chunk.share, chunk.share), chunk.share)
            total = chunk.ref[mine, lanes].astype(jnp.float32)
            for step in range(1, plan.count_tok):
                self.far_copy(chunk, half, step).wait()
                came = pl.ds(self.far_row(chunk, step), chunk.share)
                total = total + chunk.ref[came, lanes].astype(jnp.float32)
            chunk.out[:, place] = total
        self.clock += 0.2


def outer_chunk(plan, seg, chunk, left, left_lane, right, right_lane):
    nsub = 1 << plan.low_bits
    high = [b for b in plan.rest if b >= plan.low_bits]
    columns = pl.ds(right_lane, 2 * chunk.wide)
    tall = chunk.unit == plan.seg_rows_ff
    for relative in combos(high):
        group = lax.div(lax.div(seg_block(plan, seg, relative), nsub), 2)
        span = chunk.unit if tall else chunk.unit * nsub
        for piece in range(nsub if tall else 1):
            index = group * nsub + piece if tall else group
            taken = left[:, pl.ds(pl.multiple_of(left_lane + index * span, 128), span)]
            result = lax.dot_general(
                taken,
                right[:, columns],
                (((0,), (0,)), ((), ())),
                preferred_element_type=jnp.float32,
            ).astype(jnp.bfloat16)
            for part in (piece,) if tall else range(nsub):
                full = dict(relative)
                for bit in range(plan.low_bits):
                    mine, want = bit_of(seg, bit), (part >> bit) & 1
                    full[bit] = mine + want - 2 * mine * want
                rows = result if tall else result[part * chunk.unit : (part + 1) * chunk.unit]
                for half in range(2):
                    slot = plan.slot(plan.orders[half], full)
                    start = slot * chunk.unit
                    if not isinstance(start, int):
                        start = pl.multiple_of(start, chunk.unit)
                    lanes = pl.ds(chunk.lane + half * chunk.wide, chunk.wide)
                    chunk.ref[pl.ds(start, chunk.unit), lanes] = rows[
                        :, half * chunk.wide : (half + 1) * chunk.wide
                    ]


def fold(value):
    return value[0:8] + value[8:16]


def total_rows(value):
    return jnp.sum(value, axis=0, keepdims=True)


def norm_back(values, slope, gain_row):
    centre = values - jnp.mean(values, axis=-1, keepdims=True)
    rate = lax.rsqrt(jnp.mean(centre * centre, axis=-1, keepdims=True) + 1e-05)
    scaled = centre * rate
    inner = slope * gain_row
    mean_inner = jnp.mean(inner, axis=-1, keepdims=True)
    mean_along = jnp.mean(inner * scaled, axis=-1, keepdims=True)
    return rate * (inner - mean_inner - scaled * mean_along), slope * scaled


class BackwardIn(NamedTuple):
    cat_squared: Any
    cat_recept_two: Any
    cat_key_two: Any
    cat_weighted: Any
    cat_recept_mix: Any
    cat_value_mix: Any
    cat_key_mix: Any
    cat_carried: Any
    cat_gate: Any
    sq_out: Any
    out_kf: Any
    out_vf: Any
    out_recept: Any
    out_mixed: Any
    out_xp: Any
    out_middle: Any
    out_upf: Any
    out_nf: Any
    out_nf2: Any
    entry: Any
    scales: Any
    blends: Any
    speed: Any
    reward: Any
    wk: Any
    wv: Any
    wr: Any
    wo: Any
    wl: Any
    wp: Any
    wa: Any


class BackwardOut(NamedTuple):
    token_grad: Any
    small: Any
    fvalue: Any
    frecept: Any
    fkey: Any
    aout: Any
    arecept: Any
    avalue: Any
    akey: Any


class BackwardRefs(NamedTuple):
    cat_squared: Any
    cat_recept_two: Any
    cat_key_two: Any
    cat_weighted: Any
    cat_recept_mix: Any
    cat_value_mix: Any
    cat_key_mix: Any
    cat_carried: Any
    cat_gate: Any
    sq_out: Any
    out_kf: Any
    out_vf: Any
    out_recept: Any
    out_mixed: Any
    out_xp: Any
    out_middle: Any
    out_upf: Any
    out_nf: Any
    out_nf2: Any
    entry: Any
    scales: Any
    blends: Any
    speed: Any
    reward: Any
    wk: Any
    wv: Any
    wr: Any
    wo: Any
    wl: Any
    wp: Any
    wa: Any
    token_grad: Any
    small: Any
    fvalue: Any
    frecept: Any
    fkey: Any
    aout: Any
    arecept: Any
    avalue: Any
    akey: Any
    vl: Any
    vp: Any
    va: Any
    early: Any
    tall: Any
    csq: Any
    cfr: Any
    cfk: Any
    gc: Any
    gg: Any
    gh: Any
    sqn: Any
    f0: Any
    f1: Any
    f2: Any
    f3: Any
    f4: Any
    f5: Any
    f6: Any
    row_out: Any
    row_in: Any
    row_one_out: Any
    row_one_in: Any
    state_out: Any
    state_in: Any
    small_in: Any
    sems: Any
    far_sems: Any
    local_sems: Any
    send_sems: Any
    recv_sems: Any
    ready: Any


def backward_kernel(plan, *refs):
    r = BackwardRefs(*refs)
    seg, tok = lax.axis_index("seg"), lax.axis_index("tok")
    tokens = r.sqn.shape[1]
    steps, pairs = tokens // 8, tokens // 16
    every = lambda i: pl.ds(i, 8, stride=steps)
    own_rows, pair_rows = pl.ds(0, tokens), pl.ds(tokens, tokens)
    partner = {"seg": flip(seg, plan.pair)}
    last_tok = plan.count_tok - 1
    copies = Copies(r.local_sems, r.send_sems, r.recv_sems)
    load = copies.local
    half = EMBED_SIZE // 2
    at_csq = load(r.cat_squared, r.csq)
    at_gc = load(r.cat_carried, r.gc)
    at_vp, at_sq = [None] * 4, [None] * 4
    for j in range(4):
        at_vp[j] = load(r.wp.at[pl.ds(1024 * j, 1024)], r.vp.at[j])
        if j < 2:
            at_sq[j] = load(r.sq_out.at[j], r.sqn.at[j])
    at_gg, at_cfr = load(r.cat_gate, r.gg), load(r.cat_recept_two, r.cfr)
    at_cfk = load(r.cat_key_two, r.cfk)
    at_vl = [load(r.wl.at[:, pl.ds(1024 * j, 1024)], r.vl.at[j]) for j in range(4)]
    at_va = load(r.wa, r.va)
    at_nf2 = load(r.out_nf2, r.f0)
    at_mid = load(r.out_middle, r.f1.at[own_rows])
    at_up = load(r.out_upf, r.f2.at[own_rows])
    at_rec = load(r.out_recept, r.f5.at[own_rows])
    greet(plan, seg, tok)
    wire = Wire(plan, seg, tok, r.sems, r.far_sems)

    share = plan.rows if plan.tok_here else 0
    share_ff = plan.rows_ff if plan.tok_here else 0
    tall = [
        Chunk(j, r.tall, 256 * j, 128, plan.seg_rows_ff, share_ff, r.fvalue, 256 * j)
        for j in range(4)
    ]
    flat = lambda number, ref, out, column: Chunk(
        number, ref, 0, half, plan.seg_rows, share, out, column
    )
    frecept = flat(4, r.early.at[0], r.frecept, 0)
    fkey = [flat(5 + j, r.early.at[1 + j], r.fkey, 1024 * j) for j in range(4)]
    late = [
        flat(9 + j, r.vl.at[j], out, 0)
        for j, out in enumerate((r.aout, r.arecept, r.avalue, r.akey))
    ]

    copies.wait(at_csq, at_gc)
    wire.clock = 4.0
    for j in range(4):
        outer_chunk(plan, seg, tall[j], r.csq, 0, r.gc, 256 * j)
        wire.clock += 1.1
        wire.offer(tall[j])
    cats = [
        load(cat, r.csq.at[:, pl.ds(half * j, half)])
        for j, cat in enumerate((r.cat_weighted, r.cat_recept_mix, r.cat_value_mix, r.cat_key_mix))
    ]
    sent = []
    for j in range(4):
        copies.wait(at_vp[j], at_sq[j])
        slope = matmul_back(r.gc[own_rows], r.vp[j])
        rate = 2.0 * jnp.sqrt(r.sqn[j % 2].astype(jnp.float32))
        r.gh[j, own_rows] = (slope * rate).astype(jnp.bfloat16)
        sent.append(copies.remote(r.gh.at[j, own_rows], r.gh.at[j, pair_rows], partner))
        if j < 2:
            at_sq[j + 2] = load(r.sq_out.at[j + 2], r.sqn.at[j])
        wire.tick(1.4)
    at_wo = load(r.wo, r.vp.at[3])
    at_wk, at_wv, at_wr = load(r.wk, r.vp.at[0]), load(r.wv, r.vp.at[1]), load(r.wr, r.vp.at[2])
    copies.wait(at_gg, at_cfr, at_cfk)
    outer_chunk(plan, seg, frecept, r.cfr, 0, r.gg, 0)
    wire.clock += 1.1
    wire.offer(frecept)
    for j in range(4):
        copies.wait(sent[j])
        outer_chunk(plan, seg, fkey[j], r.cfk, 0, r.gh.at[j], 0)
        wire.clock += 1.1
        wire.offer(fkey[j])
    for j in range(4):
        copies.wait(at_vl[j])
        part = matmul_back(r.gh[j, own_rows], r.vl[j])
        r.f3[own_rows] = part if j == 0 else r.f3[own_rows] + part
        wire.tick(1.1)
    copies.wait(at_va)
    r.f4[own_rows] = matmul_back(r.gg[own_rows], r.va[...])
    wire.tick(1.0)

    neighbours = [{"seg": flip(seg, bit)} for bit in range(plan.bits)]
    neighbours += [
        {"tok": lax.rem(tok + step, plan.count_tok)} for step in range(1, plan.count_tok)
    ]
    for device in neighbours:
        pl.semaphore_signal(r.ready, inc=1, device_id=device, device_id_type=MESH)

    def unmix(grads, weights, kept, row_out, row_in):
        def across(place):
            slopes = [grad[place] for grad in grads]
            total = slopes[0] * (1.0 - weights[0])
            for item, weight in zip(slopes[1:], weights[1:]):
                total = total + item * (1.0 - weight)
            return slopes, low(total)

        first = across(pl.ds(0, 8))[1]
        row_out[...] = first
        row = copies.remote(row_out, row_in, left_of(plan, tok))

        def step(i, sums):
            place = rows16(i)
            slopes, shifted = across(place)
            difference = kept[pl.ds(pl.multiple_of(16 * i + 8, 8), 16)] - kept[place]
            direct = slopes[0] * weights[0]
            for item, weight in zip(slopes[1:], weights[1:]):
                direct = direct + item * weight
            grads[0][place] = direct
            grads[-1][place] = shifted
            return tuple(fold(item * difference) + old for item, old in zip(slopes, sums))

        zero = jnp.zeros((8, EMBED_SIZE), jnp.float32)
        sums = lax.fori_loop(0, pairs, step, (zero,) * len(grads))
        copies.wait(row)
        end = jnp.where(tok == last_tok, 0.0, row_in[0:1])
        grads[-1][pl.ds(tokens, 8)] = jnp.concatenate([first[1:8], end])
        return [total_rows(item) for item in sums]

    def norm_pull(direct, shifted, values, gain_row, emit):
        def step(i, sums):
            place = rows16(i)
            slope = direct[place] + shifted[pl.ds(pl.multiple_of(16 * i + 8, 8), 16)]
            back, along = norm_back(values[place], slope, gain_row)
            emit(i, back)
            return fold(along) + sums[0], fold(slope) + sums[1]

        zero = jnp.zeros((8, EMBED_SIZE), jnp.float32)
        sums = lax.fori_loop(0, pairs, step, (zero, zero))
        return [total_rows(item) for item in sums]

    blend = lambda j: r.blends[j : j + 1]
    copies.wait(at_nf2)
    sums_two = unmix((r.f3, r.f4), (blend(3), blend(4)), r.f0, r.row_out, r.row_in)
    at_mixed = load(r.out_mixed, r.f0.at[own_rows])
    wire.tick(4.0)
    copies.wait(at_mid, at_up)

    def middle_slope(i, back):
        total = r.f2[rows16(i)] + back
        r.f2[rows16(i)] = total
        r.gh[0, rows16(i)] = total.astype(jnp.bfloat16)

    gain_two, bias_two = norm_pull(r.f3, r.f4, r.f1, r.scales[1:2], middle_slope)
    at_k = load(r.out_kf, r.f1.at[own_rows])
    at_v = load(r.out_vf, r.f4.at[own_rows])
    pl.semaphore_wait(r.ready, len(neighbours))
    to_pair = lambda j: copies.remote(r.gh.at[j, own_rows], r.gh.at[j, pair_rows], partner)
    pair_out = to_pair(0)
    wire.tick(4.0)
    copies.wait(at_wo)
    r.f3[own_rows] = matmul_back(r.gh[0, own_rows], r.vp[3])
    wire.tick(1.0)
    copies.wait(at_rec, at_mixed)

    def wkv_slope(i):
        place = rows16(i)
        slope, recept = r.f3[place], r.f5[place]
        gated = slope * recept
        r.f3[place] = low(gated)
        r.gh[1, place] = (gated * r.f0[place] * (1.0 - recept)).astype(jnp.bfloat16)

    sweep(pairs, wkv_slope)
    pair_recept = to_pair(1)
    wire.tick(1.5)
    copies.wait(pair_out, cats[0])
    outer_chunk(plan, seg, late[0], r.csq, 0, r.gh.at[0], 0)
    wire.clock += 1.1
    wire.offer(late[0])

    copies.wait(at_k, at_v)
    fading_row = jnp.exp(r.speed[...])
    fading = jnp.broadcast_to(fading_row, (8, EMBED_SIZE))
    reward = jnp.broadcast_to(r.reward[...], (8, EMBED_SIZE))
    zero = jnp.zeros((8, EMBED_SIZE), jnp.float32)
    key_ref, value_ref, slope_ref, top_ref, numer_ref, denom_ref = r.f1, r.f4, r.f3, r.f0, r.f5, r.f6

    def terms(state, key, value, slope):
        numer, denom, top = state
        present = reward + key
        peak = jnp.maximum(top, present)
        old, new = jnp.exp(top - peak), jnp.exp(present - peak)
        inverse = 1.0 / (old * denom + new)
        result = (old * numer + new * value) * inverse
        reduced = top - fading
        next_top = jnp.maximum(reduced, key)
        keep, put = jnp.exp(reduced - next_top), jnp.exp(key - next_top)
        scaled = slope * inverse
        return old * scaled, new * scaled, result, keep, put, next_top

    def onward(i, carry):
        numer, denom, top, alpha, beta, product = carry
        place = rows8(i)
        key, value = key_ref[place], value_ref[place]
        top_ref[place] = top
        numer_ref[place] = numer
        put_rows(denom_ref, place, denom)
        into, _, result, keep, put, next_top = terms((numer, denom, top), key, value, slope_ref[place])
        alpha = alpha + product * into
        beta = beta - product * into * result
        product = product * keep
        return keep * numer + put * value, keep * denom + put, next_top, alpha, beta, product

    entry = tuple(r.entry[8 * part : 8 * part + 8] for part in range(3))
    swept = lax.fori_loop(0, steps, onward, entry + (zero, zero, zero + 1.0))
    stretches = swept[3:]

    def pull_back(later, stretch):
        return (stretch[0] + stretch[2] * later[0], stretch[1] + stretch[2] * later[1])

    nothing = (jnp.zeros((1, EMBED_SIZE), jnp.float32),) * 2
    total, product = nothing, jnp.ones((1, EMBED_SIZE), jnp.float32)
    for j in range(7, -1, -1):
        total = pull_back(total, row_of(stretches, j))
        product = product * stretches[2][j : j + 1]
    r.state_out[...] = zero
    for part, item in enumerate(total + (product,)):
        r.state_out[part : part + 1] = item
    sent = [
        copies.remote(
            r.state_out, r.state_in.at[tok], {"tok": lax.rem(tok + step, plan.count_tok)}
        )
        for step in range(1, plan.count_tok)
    ]
    r.state_in[tok] = r.state_out[...]
    wire.tick(5.0)
    copies.wait(pair_recept, cats[1])
    outer_chunk(plan, seg, late[1], r.csq, half, r.gh.at[1], 0)
    wire.clock += 1.1
    wire.offer(late[1])
    copies.wait(*sent)
    later, entering = nothing, nothing
    for z in range(last_tok, -1, -1):
        entering = tuple(jnp.where(tok == z, new, old) for new, old in zip(later, entering))
        later = pull_back(later, tuple(r.state_in[z, part : part + 1] for part in range(3)))
    entries = [entering]
    for j in range(7, 0, -1):
        entries.insert(0, pull_back(entries[0], row_of(stretches, j)))
    entries = stack_rows(entries)

    def back(i, carry):
        alpha, beta, fade_sum, reward_sum = carry
        place = rows8(i)
        key, value, slope = key_ref[place], value_ref[place], slope_ref[place]
        numer, denom, top = numer_ref[place], get_rows(denom_ref, place), top_ref[place]
        into, now, result, keep, put, _ = terms((numer, denom, top), key, value, slope)
        reward_term = now * (value - result)
        key_slope = reward_term + put * (alpha * value + beta)
        value_slope = now + put * alpha
        fade_sum = fade_sum - keep * (alpha * numer + beta * denom)
        alpha, beta = keep * alpha + into, keep * beta - into * result
        return (alpha, beta, fade_sum, reward_sum + reward_term), key_slope, value_slope

    def backward_pair(index, carry):
        i = pairs - 1 - index
        carry, key_two, value_two = back(2 * i + 1, carry)
        carry, key_one, value_one = back(2 * i, carry)
        r.gh[2, rows16(i)] = jnp.concatenate([value_one, value_two]).astype(jnp.bfloat16)
        r.gh[3, rows16(i)] = jnp.concatenate([key_one, key_two]).astype(jnp.bfloat16)
        return carry

    _, _, fade_sum, reward_sum = lax.fori_loop(0, pairs, backward_pair, entries + (zero, zero))
    decay = total_rows(fade_sum) * fading_row
    bonus = total_rows(reward_sum)
    pair_value, pair_key = to_pair(2), to_pair(3)
    wire.tick(6.0)
    at_nf = load(r.out_nf, r.f4)
    at_xp = load(r.out_xp, r.f5.at[own_rows])
    copies.wait(at_wk)
    r.f0[own_rows] = matmul_back(r.gh[3, own_rows], r.vp[0])
    wire.tick(1.0)
    copies.wait(pair_value, cats[2])
    outer_chunk(plan, seg, late[2], r.csq, 2 * half, r.gh.at[2], 0)
    wire.clock += 1.1
    wire.offer(late[2])
    copies.wait(pair_key, cats[3])
    outer_chunk(plan, seg, late[3], r.csq, 3 * half, r.gh.at[3], 0)
    wire.clock += 1.1
    wire.offer(late[3])

    copies.wait(at_wv, at_wr)
    r.f1[own_rows] = matmul_back(r.gh[2, own_rows], r.vp[1])
    wire.tick(1.0)
    r.f3[own_rows] = matmul_back(r.gh[1, own_rows], r.vp[2])
    wire.tick(1.0)
    copies.wait(at_nf)
    sums_one = unmix(
        (r.f0, r.f1, r.f3),
        (blend(0), blend(1), blend(2)),
        r.f4,
        r.row_one_out,
        r.row_one_in,
    )
    wire.tick(4.5)
    copies.wait(at_xp)

    def input_slope(i, back):
        total = r.f2[rows16(i)] + back
        put_rows(r.f6, every(2 * i), total[0:8])
        put_rows(r.f6, every(2 * i + 1), total[8:16])

    gain_one, bias_one = norm_pull(r.f0, r.f3, r.f5, r.scales[0:1], input_slope)
    wire.tick(4.5)

    small_rows = [gain_one, gain_two, bias_one, bias_two] + sums_one + sums_two + [decay, bonus]
    r.small[...] = jnp.concatenate(
        small_rows + [jnp.zeros((16 - len(small_rows), EMBED_SIZE), jnp.float32)]
    )

    def small_stage(bit):
        copy = copies.remote(r.small, r.small_in.at[bit], {"seg": flip(seg, bit)})

        def next_stage():
            copies.wait(copy)
            r.small[...] += r.small_in[bit]
            if bit + 1 < plan.bits:
                small_stage(bit + 1)
            else:
                small_far()

        wire.fly(wire.clock + 4.0, next_stage)

    def small_far():
        base = plan.bits - 1
        sent = [
            copies.remote(
                r.small,
                r.small_in.at[base + step],
                {"tok": lax.rem(tok + step, plan.count_tok)},
            )
            for step in range(1, plan.count_tok)
        ]

        def end():
            copies.wait(*sent)
            total = r.small[...]
            for step in range(1, plan.count_tok):
                total = total + r.small_in[base + step]
            r.small[...] = total

        wire.fly(wire.clock + 6.0, end)

    small_stage(0)

    def narrow(i):
        r.token_grad[rows16(i)] = get_rows(r.f6, rows16(i)).astype(jnp.bfloat16)

    sweep(pairs, narrow)
    wire.serve(rest=True)
    copies.drain()


def backward(plan, arrays, tokens):
    f32, b16 = jnp.float32, jnp.bfloat16
    half = EMBED_SIZE // 2
    anywhere, vmem = pl.BlockSpec(memory_space=pl.ANY), pl.BlockSpec(memory_space=pltpu.VMEM)
    sds = jax.ShapeDtypeStruct
    far = plan.count_tok - 1
    rows = plan.rows if plan.tok_here else plan.seg_rows
    rows_ff = plan.rows_ff if plan.tok_here else plan.seg_rows_ff
    extra = far if plan.tok_here else 0
    out_shape = [sds((tokens, EMBED_SIZE), b16), sds((16, EMBED_SIZE), f32)]
    out_shape += [sds((rows_ff, EMBED_SIZE), f32), sds((rows, EMBED_SIZE), f32)]
    out_shape += [sds((rows, FF), f32)] + [sds((rows, EMBED_SIZE), f32)] * 4
    square = (4, EMBED_SIZE, EMBED_SIZE)
    held = (2 * plan.slots - 1) * plan.seg_rows + extra * plan.rows
    held_ff = (2 * plan.slots - 1) * plan.seg_rows_ff + extra * plan.rows_ff
    tile = pltpu.VMEM((8, EMBED_SIZE), f32)
    scratch = [pltpu.VMEM(square, b16)] * 2 + [pltpu.VMEM(square[1:], b16)]
    scratch += [pltpu.VMEM((5, held, EMBED_SIZE), b16), pltpu.VMEM((held_ff, EMBED_SIZE), b16)]
    scratch += [pltpu.VMEM((2 * tokens, FF // 2), b16)] + [pltpu.VMEM((2 * tokens, half), b16)] * 2
    scratch += [pltpu.VMEM((2 * tokens, EMBED_SIZE), b16)] * 2
    scratch += [pltpu.VMEM((4, 2 * tokens, EMBED_SIZE), b16), pltpu.VMEM((2, tokens, EMBED_SIZE), b16)]
    scratch += [pltpu.VMEM((tokens + 8, EMBED_SIZE), f32)] * 6
    scratch += [pltpu.VMEM((LANES, tokens, 128), f32)]
    scratch += [tile] * 5 + [pltpu.VMEM((plan.count_tok, 8, EMBED_SIZE), f32)]
    scratch += [pltpu.VMEM((plan.bits + far, 16, EMBED_SIZE), f32)]
    scratch += [pltpu.SemaphoreType.DMA((2, 13, 2, plan.stages)), pltpu.SemaphoreType.DMA((2, 13, 2, far))]
    scratch += [pltpu.SemaphoreType.DMA((80,))] * 3 + [pltpu.SemaphoreType.REGULAR]
    kinds = BackwardIn(*[anywhere] * len(arrays))
    kinds = kinds._replace(entry=vmem, scales=vmem, blends=vmem, speed=vmem, reward=vmem)
    got = pl.pallas_call(
        partial(backward_kernel, plan),
        out_shape=out_shape,
        in_specs=list(kinds),
        out_specs=[vmem] * len(out_shape),
        scratch_shapes=scratch,
        compiler_params=pltpu.CompilerParams(
            collective_id=1, has_side_effects=True, vmem_limit_bytes=VMEM_BYTES
        ),
    )(*arrays)
    return BackwardOut(*got)


def place_kernel(share, count, *refs):
    sources, finals, small = refs[:count], refs[count], refs[count + 1]
    targets, rest = refs[count + 2 : 2 * count + 2], refs[2 * count + 2 : -count - 1]
    held, sems = refs[-count - 1 : -1], refs[-1]
    into = [pltpu.make_async_copy(sources[i], held[i], sems.at[0, i]) for i in range(count)]
    away = [pltpu.make_async_copy(held[i], targets[i], sems.at[1, i]) for i in range(count)]
    for copy in into:
        copy.start()
    for part in range(3):
        rest[part][...] = finals[part : part + 1]
    device = lax.axis_index("seg") * lax.axis_size("tok") + lax.axis_index("tok")
    shift = lax.rem(EMBED_SIZE - device * share, EMBED_SIZE)
    turned = pltpu.roll(small[...], shift, 1)[:, :share]
    first = 0
    for target in rest[3:]:
        rows = target.shape[0]
        target[...] = turned[first : first + rows]
        first += rows
    for index in range(count):
        into[index].wait()
        away[index].start()
    for copy in away:
        copy.wait()


def place_results(plan, arrays, finals, small):
    share = EMBED_SIZE // (plan.count_seg * plan.count_tok)
    sds = jax.ShapeDtypeStruct
    anywhere, vmem = pl.BlockSpec(memory_space=pl.ANY), pl.BlockSpec(memory_space=pltpu.VMEM)
    count = len(arrays)
    small_shapes = [(1, finals.shape[1])] * 3 + [(2, share), (2, share), (5, share), (1, share), (1, share)]
    return pl.pallas_call(
        partial(place_kernel, share, count),
        out_shape=[sds(item.shape, item.dtype) for item in arrays]
        + [sds(shape, jnp.float32) for shape in small_shapes],
        in_specs=[anywhere] * count + [vmem] * 2,
        out_specs=[anywhere] * count + [vmem] * len(small_shapes),
        scratch_shapes=[pltpu.VMEM(item.shape, item.dtype) for item in arrays]
        + [pltpu.SemaphoreType.DMA((2, count))],
    )(*arrays, finals, small)


def shards(
    incoming_items,
    upstream_slope,
    timemix_prior_entry,
    featmix_prior_entry,
    opening_dividend,
    opening_divisor,
    opening_power,
    normalize_scales,
    normalize_shifts,
    shift_blends,
    logarithmic_fading_speed,
    present_reward,
    *weights,
):
    plan = Plan(lax.axis_size("seg"), lax.axis_size("tok"))
    tokens = incoming_items.shape[1]
    speed, reward = logarithmic_fading_speed[None], present_reward[None]
    ahead = forward(
        plan,
        (
            incoming_items[0],
            upstream_slope[0],
            timemix_prior_entry,
            featmix_prior_entry,
            opening_dividend,
            opening_divisor,
            opening_power,
            normalize_scales,
            normalize_shifts,
            shift_blends,
            speed,
            reward,
            *weights,
        ),
        tokens,
    )
    back = backward(
        plan,
        BackwardIn(*ahead[2:], normalize_scales, shift_blends, speed, reward, *weights),
        tokens,
    )
    sums = back[2:]
    if not plan.tok_here:
        sums = [lax.psum_scatter(item, "tok", scatter_dimension=0, tiled=True) for item in sums]
    placed = place_results(
        plan, [ahead.layer_out, back.token_grad, *sums], ahead.final, back.small
    )
    layer_out, token_grad, fvalue, frecept, fkey, aout, arecept, avalue, akey = placed[:9]
    numer, denom, top, gains, biases, mixes, decay, bonus = placed[9:]
    return (
        layer_out[None],
        token_grad[None],
        numer,
        denom,
        top,
        gains,
        biases,
        mixes,
        decay[0],
        bonus[0],
        akey,
        avalue,
        arecept,
        aout,
        fkey,
        fvalue,
        frecept,
    )


def solution(mesh):
    tokens, channels, whole = P("seg", "tok", None), P("seg", "tok"), P()
    spread, rows = P(None, ("seg", "tok")), P(("seg", "tok"), None)
    return jax.shard_map(
        shards,
        mesh=mesh,
        in_specs=(tokens,) * 2 + (P("seg", None),) * 2 + (channels,) * 3 + (whole,) * 12,
        out_specs=(tokens,) * 2
        + (channels,) * 3
        + (spread,) * 3
        + (P(("seg", "tok")),) * 2
        + (rows,) * 7,
        check_vma=False,
    )
```

```python
from functools import partial
from typing import Any, NamedTuple

import jax
import jax.numpy as jnp
from jax import lax
from jax.experimental import pallas as pl
from jax.experimental.pallas import tpu as pltpu
from jax.sharding import PartitionSpec as P

EMBED_SIZE = 1024
FF = 4096
VMEM_BYTES = 63 << 20
MESH = pl.DeviceIdType.MESH


class Plan:
    def __init__(self, count_seg, count_tok):
        self.count_seg, self.count_tok = count_seg, count_tok
        self.bits = count_seg.bit_length() - 1
        self.tok_bits = count_tok.bit_length() - 1
        self.seg_rows = EMBED_SIZE // count_seg
        self.seg_rows_ff = FF // count_seg
        self.low_bits = max(0, (128 // self.seg_rows).bit_length() - 1)
        self.pair = self.low_bits
        self.rest = [b for b in range(self.bits) if b != self.pair]
        self.orders = (self.rest, self.rest[::-1])
        self.stages = len(self.rest)
        self.slots = 1 << self.stages
        self.rows = self.seg_rows // count_tok
        self.rows_ff = self.seg_rows_ff // count_tok
        self.tok_here = self.rows % 16 == 0 and count_tok == 1 << self.tok_bits

    def recv_offset(self, stage):
        return self.slots - (self.slots >> stage)

    def slot(self, order, relative):
        total = 0
        for place, bit in enumerate(order):
            total = total + relative[bit] * (1 << (self.stages - 1 - place))
        return total


def bit_of(value, bit):
    return lax.rem(lax.div(value, 1 << bit), 2)


def flip(value, bit):
    return value + (1 - 2 * bit_of(value, bit)) * (1 << bit)


def seg_block(plan, seg, relative):
    total = bit_of(seg, plan.pair) * (1 << plan.pair)
    for bit, rel in relative.items():
        own = bit_of(seg, bit)
        total = total + (own + rel - 2 * own * rel) * (1 << bit)
    return total


def combos(bits):
    for index in range(1 << len(bits)):
        yield {bit: (index >> place) & 1 for place, bit in enumerate(bits)}


def greet(plan, seg, tok):
    barrier = pltpu.get_barrier_semaphore()
    for bit in range(plan.bits):
        pl.semaphore_signal(
            barrier, inc=1, device_id={"seg": flip(seg, bit)}, device_id_type=MESH
        )
    for step in range(1, plan.count_tok):
        pl.semaphore_signal(
            barrier,
            inc=1,
            device_id={"tok": lax.rem(tok + step, plan.count_tok)},
            device_id_type=MESH,
        )
    pl.semaphore_wait(barrier, plan.bits + plan.count_tok - 1)


class Copies:
    def __init__(self, local_sems, send_sems, recv_sems):
        self.local_sems, self.send_sems, self.recv_sems = local_sems, send_sems, recv_sems
        self.locals, self.remotes, self.open = 0, 0, []

    def local(self, source, target):
        copy = pltpu.make_async_copy(source, target, self.local_sems.at[self.locals])
        self.locals += 1
        copy.start()
        self.open.append(copy)
        return copy

    def remote(self, source, target, device):
        copy = pltpu.make_async_remote_copy(
            src_ref=source,
            dst_ref=target,
            send_sem=self.send_sems.at[self.remotes],
            recv_sem=self.recv_sems.at[self.remotes],
            device_id=device,
            device_id_type=MESH,
        )
        self.remotes += 1
        copy.start()
        self.open.append(copy)
        return copy

    def wait(self, *copies):
        for copy in copies:
            copy.wait()
            self.open = [item for item in self.open if item is not copy]

    def drain(self):
        self.wait(*list(self.open))


def rows16(index):
    return pl.ds(pl.multiple_of(index * 16, 16), 16)


def rows8(index):
    return pl.ds(pl.multiple_of(index * 8, 8), 8)


LANES = EMBED_SIZE // 128


def put_rows(staged, place, value):
    for block in range(LANES):
        staged[block, place] = value[:, 128 * block : 128 * block + 128]


def get_rows(staged, place):
    return jnp.concatenate([staged[block, place] for block in range(LANES)], axis=1)


def low(value):
    return value.astype(jnp.bfloat16).astype(jnp.float32)


def layer_norm(values, gain_row, bias_row):
    centre = values - jnp.mean(values, axis=-1, keepdims=True)
    spread = jnp.mean(centre * centre, axis=-1, keepdims=True)
    return centre * lax.rsqrt(spread + 1e-05) * gain_row + bias_row


def sweep(count, body, unroll=2):
    def step(index, carry):
        body(index)
        return carry

    lax.fori_loop(0, count, step, 0, unroll=unroll)


def matmul(left, right):
    return jnp.dot(left, right, preferred_element_type=jnp.float32)


def matmul_back(left, right):
    return lax.dot_general(
        left, right, (((1,), (1,)), ((), ())), preferred_element_type=jnp.float32
    )


def merge(state, later, faded):
    numer, denom, top = state
    reduced = top - faded
    peak = jnp.maximum(reduced, later[2])
    old, new = jnp.exp(reduced - peak), jnp.exp(later[2] - peak)
    return (old * numer + new * later[0], old * denom + new * later[1], peak)


def advance(state, key, value, fading):
    numer, denom, top = state
    reduced = top - fading
    peak = jnp.maximum(reduced, key)
    old, new = jnp.exp(reduced - peak), jnp.exp(key - peak)
    return (old * numer + new * value, old * denom + new, peak)


def row_of(state, index):
    return tuple(item[index : index + 1] for item in state)


def stack_rows(states):
    return tuple(jnp.concatenate([state[part] for state in states]) for part in range(len(states[0])))


def first_before(lead_row, last_tile):
    return jnp.concatenate([lead_row, last_tile[0:7]])


def right_of(plan, tok):
    return {"tok": lax.rem(tok + 1, plan.count_tok)}


def left_of(plan, tok):
    return {"tok": lax.rem(tok + plan.count_tok - 1, plan.count_tok)}


class Chunk:
    def __init__(self, ref, lane, wide, unit, share, out, column, far_first=False):
        self.ref, self.lane, self.wide = ref, lane, wide
        self.unit, self.share, self.out, self.column = unit, share, out, column
        self.far_first = far_first


class Strand:
    def __init__(self, plan, chunk, half):
        self.chunk, self.lanes = chunk, pl.ds(chunk.lane + half * chunk.wide, chunk.wide)
        self.place = pl.ds(chunk.column + half * chunk.wide, chunk.wide)
        self.route = list(plan.orders[half])
        far = [-1 - bit for bit in range(plan.tok_bits)] if plan.tok_here else []
        self.route = far + self.route if chunk.far_first else self.route + far
        self.slots, self.settled, self.free = plan.slots, 0, plan.slots * chunk.unit


class Wire:
    RATE = 86e3
    LAG = 2.5
    BACKLOG = 6.0

    def __init__(self, plan, seg, tok, send_sems, recv_sems):
        self.plan, self.seg, self.tok = plan, seg, tok
        self.send_sems, self.recv_sems, self.count = send_sems, recv_sems, 0
        self.clock, self.free = 0.0, {}
        self.waiting, self.flying = [], []

    def load(self, axis, amount):
        ends = []
        for link in range(axis, 0) if axis < 0 else (axis,):
            passing = amount << max(0, -1 - link)
            self.free[link] = max(self.clock, self.free.get(link, 0.0)) + passing / self.RATE
            ends.append(self.free[link])
        return max(ends) + self.LAG

    def fly(self, arrival, action):
        self.flying.append((arrival, action))

    def due(self, far):
        start = max([self.clock] + [self.free.get(link, 0.0) for link in (-2, -1) if far])
        return start + 2.3

    def meet(self, *times):
        self.clock = max(self.clock, *times)

    def offer(self, chunk):
        self.waiting += [Strand(self.plan, chunk, half) for half in range(2)]
        self.serve()

    def tick(self, cost):
        self.clock += cost
        self.serve()

    def room(self):
        for strand in self.waiting:
            if self.free.get(strand.route[0], 0.0) - self.clock < self.BACKLOG:
                return strand
        return None

    def serve(self, rest=False):
        while self.flying or self.waiting:
            strand = self.room()
            if strand is not None:
                self.waiting.remove(strand)
                self.start(strand)
                continue
            if not self.flying:
                break
            soonest = min(self.flying, key=lambda item: item[0])
            if soonest[0] > self.clock and not rest:
                break
            self.clock = max(self.clock, soonest[0])
            self.flying.remove(soonest)
            soonest[1]()

    def copy(self, strand, source, target, rows, device):
        index, self.count = self.count, self.count + 1
        made = pltpu.make_async_remote_copy(
            src_ref=strand.chunk.ref.at[pl.ds(source, rows), strand.lanes],
            dst_ref=strand.chunk.ref.at[pl.ds(target, rows), strand.lanes],
            send_sem=self.send_sems.at[index],
            recv_sem=self.recv_sems.at[index],
            device_id=device,
            device_id_type=MESH,
        )
        made.start()
        return made

    def start(self, strand):
        plan, chunk, base = self.plan, strand.chunk, strand.free
        axis, copies, pieces = strand.route.pop(0), [], []
        unit, share = chunk.unit, chunk.share
        kept = self.tok
        if axis < 0:
            bit = -1 - axis
            device = {"tok": flip(self.tok, bit)}
            sent, strand.settled = flip(self.tok, bit), bit + 1
        else:
            device, sent = {"seg": flip(self.seg, axis)}, self.tok
            strand.slots //= 2
        first = strand.slots if axis >= 0 else 0
        if strand.settled:
            step = 1 << strand.settled
            parts = plan.count_tok // step
            for slot in range(strand.slots):
                for part in range(parts):
                    there = lax.rem(sent, step) + step * part
                    source = pl.multiple_of((first + slot) * unit + there * share, share)
                    here = lax.rem(kept, step) + step * part
                    near = pl.multiple_of(slot * unit + here * share, share)
                    to = base + (slot * parts + part) * share
                    copies.append(self.copy(strand, source, to, share, device))
                    pieces.append((near, share, to))
            rows = strand.slots * parts * share
        else:
            rows = strand.slots * unit
            copies.append(self.copy(strand, rows, base, rows, device))
            pieces.append((0, rows, base))
        strand.free += rows
        arrival = self.load(axis, 4 * chunk.wide * rows)
        self.fly(arrival, lambda: self.arrive(strand, copies, pieces))

    def arrive(self, strand, copies, pieces):
        chunk = strand.chunk
        for copy in copies:
            copy.wait()
        for near, rows, came in pieces:
            block = min(rows, 32768 // chunk.wide)

            def add(index):
                offset = index * block
                place = pl.ds(pl.multiple_of(near + offset, 16), block)
                there = pl.ds(pl.multiple_of(came + offset, 16), block)
                total = chunk.ref[place, strand.lanes].astype(jnp.float32)
                total = total + chunk.ref[there, strand.lanes].astype(jnp.float32)
                if strand.route:
                    chunk.ref[place, strand.lanes] = total.astype(jnp.bfloat16)
                else:
                    chunk.out[pl.ds(pl.multiple_of(offset, 8), block), strand.place] = total

            sweep(rows // block, add, 1)
            self.clock += 1.2e-6 * rows * chunk.wide + 0.05
        if strand.route:
            self.start(strand)


def outer_chunk(plan, seg, chunk, left, left_lane, right, right_lane):
    nsub = 1 << plan.low_bits
    high = [b for b in plan.rest if b >= plan.low_bits]
    columns = pl.ds(right_lane, 2 * chunk.wide)
    tall = chunk.unit == plan.seg_rows_ff
    for relative in combos(high):
        group = lax.div(lax.div(seg_block(plan, seg, relative), nsub), 2)
        span = chunk.unit if tall else chunk.unit * nsub
        for piece in range(nsub if tall else 1):
            index = group * nsub + piece if tall else group
            taken = left[:, pl.ds(pl.multiple_of(left_lane + index * span, 128), span)]
            result = lax.dot_general(
                taken,
                right[:, columns],
                (((0,), (0,)), ((), ())),
                preferred_element_type=jnp.float32,
            ).astype(jnp.bfloat16)
            for part in (piece,) if tall else range(nsub):
                full = dict(relative)
                for bit in range(plan.low_bits):
                    mine, want = bit_of(seg, bit), (part >> bit) & 1
                    full[bit] = mine + want - 2 * mine * want
                rows = result if tall else result[part * chunk.unit : (part + 1) * chunk.unit]
                for half in range(2):
                    slot = plan.slot(plan.orders[half], full)
                    start = slot * chunk.unit
                    if not isinstance(start, int):
                        start = pl.multiple_of(start, chunk.unit)
                    lanes = pl.ds(chunk.lane + half * chunk.wide, chunk.wide)
                    chunk.ref[pl.ds(start, chunk.unit), lanes] = rows[
                        :, half * chunk.wide : (half + 1) * chunk.wide
                    ]


def fold(value):
    return value[0:8] + value[8:16]


def total_rows(value):
    return jnp.sum(value, axis=0, keepdims=True)


def norm_back(values, slope, gain_row):
    centre = values - jnp.mean(values, axis=-1, keepdims=True)
    rate = lax.rsqrt(jnp.mean(centre * centre, axis=-1, keepdims=True) + 1e-05)
    scaled = centre * rate
    inner = slope * gain_row
    mean_inner = jnp.mean(inner, axis=-1, keepdims=True)
    mean_along = jnp.mean(inner * scaled, axis=-1, keepdims=True)
    return rate * (inner - mean_inner - scaled * mean_along), slope * scaled


class LayerIn(NamedTuple):
    x: Any
    up: Any
    prior_one: Any
    prior_two: Any
    open_num: Any
    open_den: Any
    open_top: Any
    scales: Any
    shifts: Any
    blends: Any
    speed: Any
    reward: Any
    wk: Any
    wv: Any
    wr: Any
    wo: Any
    wl: Any
    wp: Any
    wa: Any


class LayerOut(NamedTuple):
    layer_out: Any
    token_grad: Any
    fvalue: Any
    frecept: Any
    fkey: Any
    aout: Any
    arecept: Any
    avalue: Any
    akey: Any
    final: Any
    small: Any
    cat_weighted: Any
    cat_recept_mix: Any
    cat_value_mix: Any
    cat_key_mix: Any
    out_kf: Any
    out_vf: Any
    out_recept: Any
    out_xp: Any
    out_nf: Any


class LayerHeld(NamedTuple):
    vl: Any
    vp: Any
    va: Any
    early: Any
    tall: Any
    csq: Any
    cfr: Any
    cfk: Any
    gc: Any
    gg: Any
    gh: Any
    sq: Any
    f0: Any
    f1: Any
    f2: Any
    f3: Any
    f4: Any
    f5: Any
    staged: Any
    row_out: Any
    row_in: Any
    state_out: Any
    state_in: Any
    back_out: Any
    back_in: Any
    entry: Any
    small_in: Any
    wire_send: Any
    wire_recv: Any
    local_sems: Any
    send_sems: Any
    recv_sems: Any
    ready: Any


def layer_kernel(plan, *refs):
    count_in, count_out = len(LayerIn._fields), len(LayerOut._fields)
    a = LayerIn(*refs[:count_in])
    o = LayerOut(*refs[count_in : count_in + count_out])
    h = LayerHeld(*refs[count_in + count_out :])
    seg, tok = lax.axis_index("seg"), lax.axis_index("tok")
    tokens = h.sq.shape[1]
    steps, pairs = tokens // 8, tokens // 16
    every = lambda i: pl.ds(i, 8, stride=steps)
    shifted16 = lambda i: pl.ds(pl.multiple_of(16 * i + 8, 8), 16)
    own_rows, pair_rows = pl.ds(0, tokens), pl.ds(tokens, tokens)
    partner = {"seg": flip(seg, plan.pair)}
    mine = bit_of(seg, plan.pair)
    last_tok = plan.count_tok - 1
    half = EMBED_SIZE // 2
    copies = Copies(h.local_sems, h.send_sems, h.recv_sems)
    load = copies.local
    tile_zero = jnp.zeros((8, EMBED_SIZE), jnp.float32)
    blend = lambda j: a.blends[j : j + 1]
    others = lambda: [
        {"tok": lax.rem(tok + step, plan.count_tok)} for step in range(1, plan.count_tok)
    ]

    xb, ub = h.gh.at[2, own_rows], h.gh.at[3, own_rows]
    at_x = load(a.x, xb)
    at_wk, at_wv = load(a.wk, h.vp.at[0]), load(a.wv, h.vp.at[1])
    at_wr, at_wo = load(a.wr, h.vp.at[2]), load(a.wo, h.vp.at[3])
    at_up = load(a.up, ub)
    at_va = load(a.wa, h.va)
    at_vl = [load(a.wl.at[:, pl.ds(1024 * j, 1024)], h.vl.at[j]) for j in range(4)]
    greet(plan, seg, tok)
    wire = Wire(plan, seg, tok, h.wire_send, h.wire_recv)

    def share(source, target, wide, at=0):
        count = source.shape[1] // (2 * wide)
        made = []
        for pick in range(count):
            own = pl.ds(pl.multiple_of((2 * pick + mine) * wide, wide), wide)
            other = pl.ds(pl.multiple_of((2 * pick + 1 - mine) * wide, wide), wide)
            place = pl.ds((at + pick) * wide, wide)
            made.append(load(source.at[:, own], target.at[own_rows, place]))
            made.append(copies.remote(source.at[:, other], target.at[pair_rows, place], partner))
        return made

    def to_pair(ref):
        return copies.remote(ref.at[own_rows], ref.at[pair_rows], partner), wire.due(False)

    def meet(*pairs):
        for copy, due in pairs:
            wire.meet(due)
            copies.wait(copy)

    wide = max(128, plan.seg_rows)

    nf, xp = h.f0, h.f1
    copies.wait(at_x)

    def widen(i):
        put_rows(h.staged, rows16(i), xb[rows16(i)].astype(jnp.float32))

    sweep(pairs, widen, 4)
    gain, bias = a.scales[0:1], a.shifts[0:1]

    def norm_one(i):
        tile = get_rows(h.staged, every(i))
        xp[rows8(i)] = tile
        nf[rows8(i + 1)] = low(layer_norm(tile, gain, bias))

    norm_one(steps - 1)
    h.row_out[0] = nf[pl.ds(8 * steps, 8)]
    row = copies.remote(h.row_out.at[0], h.row_in.at[0], right_of(plan, tok))
    sweep(steps, norm_one, 8)

    def mix_one(places):
        def step(i):
            before, normed = nf[rows16(i)], nf[shifted16(i)]
            for place in places:
                weight = blend(place)
                mixed = normed * weight + before * (1.0 - weight)
                h.sq[place, rows16(i)] = mixed.astype(jnp.bfloat16)

        return step

    sweep(pairs - 1, lambda i: mix_one((0, 1))(i + 1), 2)
    copies.wait(row)
    lead = jnp.where(tok == 0, a.prior_one[...].astype(jnp.float32), h.row_in[0, 7:8])
    nf[0:8] = first_before(lead, nf[pl.ds(8 * steps, 8)])
    mix_one((0, 1))(0)
    mixes = share(h.sq.at[0], o.cat_key_mix, wide) + share(h.sq.at[1], o.cat_value_mix, wide)
    at_nf, at_xp = load(nf, o.out_nf), load(xp.at[own_rows], o.out_xp)
    kf, vf, recept = h.f2, h.f3, h.f4
    copies.wait(at_wk)
    kf[own_rows] = low(matmul(h.sq[0], h.vp[0]))
    copies.wait(at_wv)
    vf[own_rows] = low(matmul(h.sq[1], h.vp[1]))
    at_kf, at_vf = load(kf.at[own_rows], o.out_kf), load(vf.at[own_rows], o.out_vf)

    fading_row = jnp.exp(a.speed[...])
    fading = jnp.broadcast_to(fading_row, (8, EMBED_SIZE))
    reward = jnp.broadcast_to(a.reward[...], (8, EMBED_SIZE))

    def alone(i, state):
        return advance(state, kf[rows8(i)], vf[rows8(i)], fading)

    stretches = lax.fori_loop(0, steps, alone, (tile_zero, tile_zero, tile_zero - 1e30), unroll=2)
    stretch_fade = fading_row * steps
    total = row_of(stretches, 0)
    for j in range(1, 8):
        total = merge(total, row_of(stretches, j), stretch_fade)
    portion = EMBED_SIZE // plan.count_tok
    lanes = pl.ds(pl.multiple_of(tok * portion, portion), portion)
    h.state_out[...] = tile_zero
    for part, opening in enumerate((a.open_num, a.open_den, a.open_top)):
        h.state_out[part : part + 1] = total[part]
        h.state_out[3 + part : 4 + part, lanes] = opening[...]
    sent = [copies.remote(h.state_out, h.state_in.at[tok], device) for device in others()]
    h.state_in[tok] = h.state_out[...]
    sweep(pairs, mix_one((2,)), 2)
    mixes += share(h.sq.at[2], o.cat_recept_mix, wide)
    copies.wait(at_wr)
    recept[own_rows] = jax.nn.sigmoid(matmul(h.sq[2], h.vp[2]))
    at_recept = load(recept.at[own_rows], o.out_recept)
    upf = h.f0
    copies.wait(at_up, at_nf)

    def widen_up(i):
        put_rows(h.staged, rows16(i), ub[rows16(i)].astype(jnp.float32))

    sweep(pairs, widen_up, 4)

    def permute_up(i):
        upf[rows8(i)] = get_rows(h.staged, every(i))

    sweep(steps, permute_up, 4)
    copies.wait(*sent)
    state = tuple(
        sum(h.state_in[z, 3 + part : 4 + part] for z in range(plan.count_tok)) for part in range(3)
    )
    entry = state
    for z in range(plan.count_tok):
        entry = tuple(jnp.where(tok == z, new, old) for new, old in zip(state, entry))
        later = tuple(h.state_in[z, part : part + 1] for part in range(3))
        state = merge(state, later, fading_row * tokens)
    for part in range(3):
        h.state_out[part : part + 1] = state[part]
    o.final[...] = h.state_out[:, lanes]
    entries = [entry]
    for j in range(7):
        entries.append(merge(entries[-1], row_of(stretches, j), stretch_fade))
    entries = stack_rows(entries)
    for part in range(3):
        h.entry[8 * part : 8 * part + 8] = entries[part]
    copies.wait(at_kf)
    mixed = h.f2

    def emit(state, i):
        key, value = kf[rows8(i)], vf[rows8(i)]
        present = reward + key
        peak = jnp.maximum(state[2], present)
        old, new = jnp.exp(state[2] - peak), jnp.exp(present - peak)
        result = (old * state[0] + new * value) / (old * state[1] + new)
        return advance(state, key, value, fading), low(result)

    def recur(i, state):
        state, one = emit(state, 2 * i)
        state, two = emit(state, 2 * i + 1)
        both_rows = jnp.concatenate([one, two])
        mixed[rows16(i)] = both_rows
        h.sq[3, rows16(i)] = (recept[rows16(i)] * both_rows).astype(jnp.bfloat16)
        return state

    lax.fori_loop(0, pairs, recur, entries, unroll=2)
    mixes += share(h.sq.at[3], o.cat_weighted, wide)
    copies.wait(at_wo, at_xp)
    middle = h.f1
    middle[own_rows] = xp[own_rows] + matmul(h.sq[3], h.vp[3])
    at_vp = [load(a.wp.at[pl.ds(1024 * j, 1024)], h.vp.at[j]) for j in range(4)]

    gain_two, bias_two = a.scales[1:2], a.shifts[1:2]
    nf2 = h.f5

    def norm_two(i):
        nf2[rows8(i + 1)] = low(layer_norm(middle[rows8(i)], gain_two, bias_two))

    norm_two(steps - 1)
    h.row_out[1] = nf2[pl.ds(8 * steps, 8)]
    row = copies.remote(h.row_out.at[1], h.row_in.at[1], right_of(plan, tok))
    sweep(steps, norm_two, 8)
    key_two, recept_two = h.gh.at[0, own_rows], h.gh.at[1, own_rows]

    def mix_two(i):
        before, normed = nf2[rows16(i)], nf2[shifted16(i)]
        for place, target in ((3, key_two), (4, recept_two)):
            weight = blend(place)
            target[rows16(i)] = (normed * weight + before * (1.0 - weight)).astype(jnp.bfloat16)

    sweep(pairs - 1, lambda i: mix_two(i + 1), 2)
    copies.wait(row)
    lead = jnp.where(tok == 0, a.prior_two[...].astype(jnp.float32), h.row_in[1, 7:8])
    nf2[0:8] = first_before(lead, nf2[pl.ds(8 * steps, 8)])
    mix_two(0)
    twos = share(key_two, h.cfk, wide) + share(recept_two, h.cfr, wide)
    gate, carried = h.f3, h.f4
    copies.wait(at_va, at_vf)
    gate[own_rows] = jax.nn.sigmoid(matmul(recept_two[...], h.va[...]))

    def carried_slope(i):
        h.gc[rows16(i)] = (upf[rows16(i)] * gate[rows16(i)]).astype(jnp.bfloat16)

    sweep(pairs, carried_slope, 2)
    pair_gc = to_pair(h.gc)
    copies.wait(*mixes)
    squares = []
    for j in range(4):
        copies.wait(at_vl[j])
        for side in range(2):
            columns = pl.ds(half * side, half)
            hidden = jnp.maximum(matmul(key_two[...], h.vl[j, :, columns]), 0.0)
            h.sq[j, :, columns] = (hidden * hidden).astype(jnp.bfloat16)
        squares += share(h.sq.at[j], h.csq, 4 * wide, j)

    share_rows = plan.rows if plan.tok_here else 0
    share_ff = plan.rows_ff if plan.tok_here else 0
    tall = [
        Chunk(h.tall, 256 * j, 128, plan.seg_rows_ff, share_ff, o.fvalue, 256 * j, j == 0)
        for j in range(4)
    ]
    flat = lambda ref, out, column, far_first: Chunk(
        ref, 0, half, plan.seg_rows, share_rows, out, column, far_first
    )
    frecept = flat(h.early.at[0], o.frecept, 0, False)
    fkey = [flat(h.early.at[1 + j], o.fkey, 1024 * j, False) for j in range(4)]
    late = [
        flat(h.vl.at[j], out, 0, j == 3)
        for j, out in enumerate((o.aout, o.arecept, o.avalue, o.akey))
    ]

    def offer(chunk, left, left_lane, right, right_lane, now=True):
        outer_chunk(plan, seg, chunk, left, left_lane, right, right_lane)
        wire.clock += 0.95
        if now:
            wire.offer(chunk)

    copies.wait(at_recept, at_vp[0])
    carried[own_rows] = matmul(h.sq[0], h.vp[0])
    copies.wait(pair_gc[0], *squares)
    wire.clock = 0.0
    for j in range(4):
        offer(tall[j], h.csq, 0, h.gc, 256 * j)
    cats = [
        load(cat, h.csq.at[:, pl.ds(half * j, half)])
        for j, cat in enumerate(
            (o.cat_weighted, o.cat_recept_mix, o.cat_value_mix, o.cat_key_mix)
        )
    ]
    for j in range(1, 4):
        copies.wait(at_vp[j])
        carried[own_rows] += matmul(h.sq[j], h.vp[j])
        wire.tick(1.0)

    def close(i):
        gates, sums = gate[rows16(i)], carried[rows16(i)]
        gated = gates * sums
        result = middle[rows16(i)] + gated
        h.gg[rows16(i)] = (upf[rows16(i)] * gated * (1.0 - gates)).astype(jnp.bfloat16)
        put_rows(h.staged, every(2 * i), result[0:8])
        put_rows(h.staged, every(2 * i + 1), result[8:16])

    sweep(pairs, close, 2)
    pair_gg = to_pair(h.gg)
    narrowed = h.gh.at[3, own_rows]

    def narrow(i):
        narrowed[rows16(i)] = get_rows(h.staged, rows16(i)).astype(jnp.bfloat16)

    sweep(pairs, narrow, 4)
    at_out = load(narrowed, o.layer_out)
    wire.tick(1.5)

    copies.wait(*twos)
    sent = []
    for j in range(4):
        h.f3[own_rows] = matmul_back(h.gc[own_rows], h.vp[j])
        if j == 3:
            copies.wait(at_out)

        def hidden_slope(i):
            rate = 2.0 * jnp.sqrt(h.sq[j, rows16(i)].astype(jnp.float32))
            h.gh[j, rows16(i)] = (h.f3[rows16(i)] * rate).astype(jnp.bfloat16)

        sweep(pairs, hidden_slope, 2)
        sent.append(to_pair(h.gh.at[j]))
        wire.tick(1.3)
    at_wo = load(a.wo, h.vp.at[3])
    at_wk, at_wv = load(a.wk, h.vp.at[0]), load(a.wv, h.vp.at[1])
    at_wr = load(a.wr, h.vp.at[2])
    meet(pair_gg)
    offer(frecept, h.cfr, 0, h.gg, 0)
    for j in range(4):
        meet(sent[j])
        offer(fkey[j], h.cfk, 0, h.gh.at[j], 0)
    for j in range(4):
        part = matmul_back(h.gh[j, own_rows], h.vl[j])
        h.f3[own_rows] = part if j == 0 else h.f3[own_rows] + part
        wire.tick(1.1)
    h.f4[own_rows] = matmul_back(h.gg[own_rows], h.va[...])
    wire.tick(1.0)

    neighbours = [{"seg": flip(seg, bit)} for bit in range(plan.bits)] + others()
    for device in neighbours:
        pl.semaphore_signal(h.ready, inc=1, device_id=device, device_id_type=MESH)

    def unmix(grads, weights, kept, row_place):
        def across(place):
            slopes = [grad[place] for grad in grads]
            total = slopes[0] * (1.0 - weights[0])
            for item, weight in zip(slopes[1:], weights[1:]):
                total = total + item * (1.0 - weight)
            return slopes, low(total)

        first = across(pl.ds(0, 8))[1]
        h.row_out[row_place] = first
        row = copies.remote(h.row_out.at[row_place], h.row_in.at[row_place], left_of(plan, tok))
        due = wire.due(True)

        def step(i, sums):
            place = rows16(i)
            slopes, moved = across(place)
            difference = kept[shifted16(i)] - kept[place]
            direct = slopes[0] * weights[0]
            for item, weight in zip(slopes[1:], weights[1:]):
                direct = direct + item * weight
            grads[0][place] = direct
            grads[-1][place] = moved
            return tuple(fold(item * difference) + old for item, old in zip(slopes, sums))

        sums = lax.fori_loop(0, pairs, step, (tile_zero,) * len(grads), unroll=2)
        wire.tick(1.5)
        wire.meet(due)
        copies.wait(row)
        end = jnp.where(tok == last_tok, 0.0, h.row_in[row_place, 0:1])
        grads[-1][pl.ds(tokens, 8)] = jnp.concatenate([first[1:8], end])
        return [total_rows(item) for item in sums]

    def norm_pull(direct, moved, values, gain_row, emit):
        def step(i, sums):
            place = rows16(i)
            slope = direct[place] + moved[shifted16(i)]
            back, along = norm_back(values[place], slope, gain_row)
            emit(i, back)
            return fold(along) + sums[0], fold(slope) + sums[1]

        sums = lax.fori_loop(0, pairs, step, (tile_zero, tile_zero), unroll=4)
        return [total_rows(item) for item in sums]

    sums_two = unmix((h.f3, h.f4), (blend(3), blend(4)), nf2, 2)
    recept = h.f5
    at_recept = load(o.out_recept, recept.at[own_rows])
    wire.tick(0.3)
    total_slope = h.f0

    def middle_slope(i, back):
        total = upf[rows16(i)] + back
        total_slope[rows16(i)] = total
        h.gh[0, rows16(i)] = total.astype(jnp.bfloat16)

    gain_sum_two, bias_sum_two = norm_pull(h.f3, h.f4, middle, gain_two, middle_slope)
    key_ref, value_ref, slope_ref, top_ref, numer_ref = h.f1, h.f4, h.f3, h.f2, h.f5
    at_k = load(o.out_kf, key_ref.at[own_rows])
    at_v = load(o.out_vf, value_ref.at[own_rows])
    pl.semaphore_wait(h.ready, len(neighbours))
    pair_out = to_pair(h.gh.at[0])
    wire.tick(2.5)
    copies.wait(at_wo)
    slope_ref[own_rows] = matmul_back(h.gh[0, own_rows], h.vp[3])
    wire.tick(1.0)
    copies.wait(at_recept)

    def wkv_slope(i):
        place = rows16(i)
        slope, gates = slope_ref[place], recept[place]
        gated = slope * gates
        slope_ref[place] = low(gated)
        h.gh[1, place] = (gated * mixed[place] * (1.0 - gates)).astype(jnp.bfloat16)

    sweep(pairs, wkv_slope, 2)
    pair_recept = to_pair(h.gh.at[1])
    wire.tick(1.0)
    meet(pair_out)
    copies.wait(cats[0])
    offer(late[0], h.csq, 0, h.gh.at[0], 0)

    copies.wait(at_k, at_v)

    def terms(state, key, value, slope):
        numer, denom, top = state
        present = reward + key
        peak = jnp.maximum(top, present)
        old, new = jnp.exp(top - peak), jnp.exp(present - peak)
        inverse = 1.0 / (old * denom + new)
        result = (old * numer + new * value) * inverse
        reduced = top - fading
        next_top = jnp.maximum(reduced, key)
        keep, put = jnp.exp(reduced - next_top), jnp.exp(key - next_top)
        scaled = slope * inverse
        return old * scaled, new * scaled, result, keep, put, next_top

    def onward(i, carry):
        numer, denom, top, alpha, beta, product = carry
        place = rows8(i)
        key, value = key_ref[place], value_ref[place]
        top_ref[place] = top
        numer_ref[place] = numer
        put_rows(h.staged, place, denom)
        into, _, result, keep, put, next_top = terms(
            (numer, denom, top), key, value, slope_ref[place]
        )
        alpha = alpha + product * into
        beta = beta - product * into * result
        product = product * keep
        return keep * numer + put * value, keep * denom + put, next_top, alpha, beta, product

    entry = tuple(h.entry[8 * part : 8 * part + 8] for part in range(3))
    swept = lax.fori_loop(
        0, steps, onward, entry + (tile_zero, tile_zero, tile_zero + 1.0), unroll=2
    )
    stretches = swept[3:]

    def pull_back(later, stretch):
        return (stretch[0] + stretch[2] * later[0], stretch[1] + stretch[2] * later[1])

    nothing = (jnp.zeros((1, EMBED_SIZE), jnp.float32),) * 2
    total, product = nothing, jnp.ones((1, EMBED_SIZE), jnp.float32)
    for j in range(7, -1, -1):
        total = pull_back(total, row_of(stretches, j))
        product = product * stretches[2][j : j + 1]
    h.back_out[...] = tile_zero
    for part, item in enumerate(total + (product,)):
        h.back_out[part : part + 1] = item
    wire.tick(4.0)
    sent = [copies.remote(h.back_out, h.back_in.at[tok], device) for device in others()]
    due = wire.due(True)
    h.back_in[tok] = h.back_out[...]
    meet(pair_recept)
    copies.wait(cats[1])
    offer(late[1], h.csq, half, h.gh.at[1], 0)
    wire.meet(due)
    copies.wait(*sent)
    later, entering = nothing, nothing
    for z in range(last_tok, -1, -1):
        entering = tuple(jnp.where(tok == z, new, old) for new, old in zip(later, entering))
        later = pull_back(later, tuple(h.back_in[z, part : part + 1] for part in range(3)))
    entries = [entering]
    for j in range(7, 0, -1):
        entries.insert(0, pull_back(entries[0], row_of(stretches, j)))
    entries = stack_rows(entries)

    def back(i, carry):
        alpha, beta, fade_sum, reward_sum = carry
        place = rows8(i)
        key, value, slope = key_ref[place], value_ref[place], slope_ref[place]
        numer, denom, top = numer_ref[place], get_rows(h.staged, place), top_ref[place]
        into, now, result, keep, put, _ = terms((numer, denom, top), key, value, slope)
        reward_term = now * (value - result)
        key_slope = reward_term + put * (alpha * value + beta)
        value_slope = now + put * alpha
        fade_sum = fade_sum - keep * (alpha * numer + beta * denom)
        alpha, beta = keep * alpha + into, keep * beta - into * result
        return (alpha, beta, fade_sum, reward_sum + reward_term), key_slope, value_slope

    def backward_pair(index, carry):
        i = pairs - 1 - index
        carry, key_two, value_two = back(2 * i + 1, carry)
        carry, key_one, value_one = back(2 * i, carry)
        h.gh[2, rows16(i)] = jnp.concatenate([value_one, value_two]).astype(jnp.bfloat16)
        h.gh[3, rows16(i)] = jnp.concatenate([key_one, key_two]).astype(jnp.bfloat16)
        return carry

    _, _, fade_sum, reward_sum = lax.fori_loop(
        0, pairs, backward_pair, entries + (tile_zero, tile_zero)
    )
    decay = total_rows(fade_sum) * fading_row
    bonus = total_rows(reward_sum)
    pair_value, pair_key = to_pair(h.gh.at[2]), to_pair(h.gh.at[3])
    nf, xp = h.f4, h.f5
    at_nf = load(o.out_nf, nf)
    at_xp = load(o.out_xp, xp.at[own_rows])
    wire.tick(5.5)
    copies.wait(at_wk)
    h.f2[own_rows] = matmul_back(h.gh[3, own_rows], h.vp[0])
    wire.tick(1.0)
    meet(pair_value)
    copies.wait(cats[2])
    offer(late[2], h.csq, 2 * half, h.gh.at[2], 0)
    meet(pair_key)
    copies.wait(cats[3])
    offer(late[3], h.csq, 3 * half, h.gh.at[3], 0, False)

    copies.wait(at_wv, at_wr)
    h.f1[own_rows] = matmul_back(h.gh[2, own_rows], h.vp[1])
    wire.tick(1.0)
    h.f3[own_rows] = matmul_back(h.gh[1, own_rows], h.vp[2])
    wire.tick(1.0)
    copies.wait(at_nf)
    sums_one = unmix((h.f2, h.f1, h.f3), (blend(0), blend(1), blend(2)), nf, 3)
    wire.offer(late[3])
    wire.tick(0.5)
    copies.wait(at_xp)

    def input_slope(i, back):
        total = total_slope[rows16(i)] + back
        put_rows(h.staged, every(2 * i), total[0:8])
        put_rows(h.staged, every(2 * i + 1), total[8:16])

    gain_sum_one, bias_sum_one = norm_pull(h.f2, h.f3, xp, a.scales[0:1], input_slope)
    wire.tick(2.5)

    small_rows = [gain_sum_one, gain_sum_two, bias_sum_one, bias_sum_two]
    small_rows += sums_one + sums_two + [decay, bonus]
    o.small[...] = jnp.concatenate(
        small_rows + [jnp.zeros((16 - len(small_rows), EMBED_SIZE), jnp.float32)]
    )

    def small_stage(bit):
        copy = copies.remote(o.small, h.small_in.at[bit], {"seg": flip(seg, bit)})

        def next_stage():
            copies.wait(copy)
            o.small[...] += h.small_in[bit]
            if bit + 1 < plan.bits:
                small_stage(bit + 1)
            else:
                small_far()

        wire.fly(wire.clock + 4.0, next_stage)

    def small_far():
        base = plan.bits - 1
        sent = [
            copies.remote(o.small, h.small_in.at[base + 1 + step], device)
            for step, device in enumerate(others())
        ]

        def end():
            copies.wait(*sent)
            total = o.small[...]
            for step in range(1, plan.count_tok):
                total = total + h.small_in[base + step]
            o.small[...] = total

        wire.fly(wire.clock + 6.0, end)

    small_stage(0)

    def narrow_slope(i):
        h.sq[0, rows16(i)] = get_rows(h.staged, rows16(i)).astype(jnp.bfloat16)

    sweep(pairs, narrow_slope, 4)
    load(h.sq.at[0], o.token_grad)
    wire.serve(rest=True)
    copies.drain()


def layer(plan, arrays, tokens):
    f32, b16 = jnp.float32, jnp.bfloat16
    half = EMBED_SIZE // 2
    anywhere, vmem = pl.BlockSpec(memory_space=pl.ANY), pl.BlockSpec(memory_space=pltpu.VMEM)
    sds, held = jax.ShapeDtypeStruct, pltpu.VMEM
    far = plan.count_tok - 1
    rows = plan.rows if plan.tok_here else plan.seg_rows
    rows_ff = plan.rows_ff if plan.tok_here else plan.seg_rows_ff
    extra = far if plan.tok_here else 0
    wide = (tokens, EMBED_SIZE)
    share = sds((rows, EMBED_SIZE), f32)
    cat, kept = sds((2 * tokens, half), b16), sds(wide, f32)
    out_shape = LayerOut(
        layer_out=sds(wide, b16),
        token_grad=sds(wide, b16),
        fvalue=sds((rows_ff, EMBED_SIZE), f32),
        frecept=share,
        fkey=sds((rows, FF), f32),
        aout=share,
        arecept=share,
        avalue=share,
        akey=share,
        final=sds((8, EMBED_SIZE // plan.count_tok), f32),
        small=sds((16, EMBED_SIZE), f32),
        cat_weighted=cat,
        cat_recept_mix=cat,
        cat_value_mix=cat,
        cat_key_mix=cat,
        out_kf=kept,
        out_vf=kept,
        out_recept=kept,
        out_xp=kept,
        out_nf=sds((tokens + 8, EMBED_SIZE), f32),
    )
    out_specs = LayerOut(*[anywhere] * 2, *[vmem] * 9, *[anywhere] * 9)
    in_specs = LayerIn(*[anywhere] * 2, *[vmem] * 10, *[anywhere] * 7)
    square = (4, EMBED_SIZE, EMBED_SIZE)
    units = 2 * plan.slots - 1
    one = held((tokens + 8, EMBED_SIZE), f32)
    tiles = held((4, 8, EMBED_SIZE), f32)
    states = held((plan.count_tok, 8, EMBED_SIZE), f32)
    several = pltpu.SemaphoreType.DMA((120,))
    scratch = LayerHeld(
        vl=held(square, b16),
        vp=held(square, b16),
        va=held(square[1:], b16),
        early=held((5, units * plan.seg_rows + extra * plan.rows, EMBED_SIZE), b16),
        tall=held((units * plan.seg_rows_ff + extra * plan.rows_ff, EMBED_SIZE), b16),
        csq=held((2 * tokens, FF // 2), b16),
        cfr=held((2 * tokens, half), b16),
        cfk=held((2 * tokens, half), b16),
        gc=held((2 * tokens, EMBED_SIZE), b16),
        gg=held((2 * tokens, EMBED_SIZE), b16),
        gh=held((4, 2 * tokens, EMBED_SIZE), b16),
        sq=held((4,) + wide, b16),
        f0=one,
        f1=one,
        f2=one,
        f3=one,
        f4=one,
        f5=one,
        staged=held((LANES, tokens, 128), f32),
        row_out=tiles,
        row_in=tiles,
        state_out=held((8, EMBED_SIZE), f32),
        state_in=states,
        back_out=held((8, EMBED_SIZE), f32),
        back_in=states,
        entry=held((24, EMBED_SIZE), f32),
        small_in=held((plan.bits + far, 16, EMBED_SIZE), f32),
        wire_send=pltpu.SemaphoreType.DMA((256,)),
        wire_recv=pltpu.SemaphoreType.DMA((256,)),
        local_sems=several,
        send_sems=several,
        recv_sems=several,
        ready=pltpu.SemaphoreType.REGULAR,
    )
    got = pl.pallas_call(
        partial(layer_kernel, plan),
        out_shape=list(out_shape),
        in_specs=list(in_specs),
        out_specs=list(out_specs),
        scratch_shapes=list(scratch),
        compiler_params=pltpu.CompilerParams(
            collective_id=0, has_side_effects=True, vmem_limit_bytes=VMEM_BYTES
        ),
    )(*arrays)
    return LayerOut(*got)


def place_kernel(share, count, *refs):
    sources, finals, small = refs[:count], refs[count], refs[count + 1]
    targets, rest = refs[count + 2 : 2 * count + 2], refs[2 * count + 2 : -count - 1]
    held, sems = refs[-count - 1 : -1], refs[-1]
    into = [pltpu.make_async_copy(sources[i], held[i], sems.at[0, i]) for i in range(count)]
    away = [pltpu.make_async_copy(held[i], targets[i], sems.at[1, i]) for i in range(count)]
    for copy in into:
        copy.start()
    for part in range(3):
        rest[part][...] = finals[part : part + 1]
    device = lax.axis_index("seg") * lax.axis_size("tok") + lax.axis_index("tok")
    shift = lax.rem(EMBED_SIZE - device * share, EMBED_SIZE)
    turned = pltpu.roll(small[...], shift, 1)[:, :share]
    first = 0
    for target in rest[3:]:
        rows = target.shape[0]
        target[...] = turned[first : first + rows]
        first += rows
    for index in range(count):
        into[index].wait()
        away[index].start()
    for copy in away:
        copy.wait()


def place_results(plan, arrays, finals, small):
    share = EMBED_SIZE // (plan.count_seg * plan.count_tok)
    sds = jax.ShapeDtypeStruct
    anywhere, vmem = pl.BlockSpec(memory_space=pl.ANY), pl.BlockSpec(memory_space=pltpu.VMEM)
    count = len(arrays)
    small_shapes = [(1, finals.shape[1])] * 3 + [(2, share), (2, share), (5, share), (1, share), (1, share)]
    return pl.pallas_call(
        partial(place_kernel, share, count),
        out_shape=[sds(item.shape, item.dtype) for item in arrays]
        + [sds(shape, jnp.float32) for shape in small_shapes],
        in_specs=[anywhere] * count + [vmem] * 2,
        out_specs=[anywhere] * count + [vmem] * len(small_shapes),
        scratch_shapes=[pltpu.VMEM(item.shape, item.dtype) for item in arrays]
        + [pltpu.SemaphoreType.DMA((2, count))],
    )(*arrays, finals, small)


def shards(
    incoming_items,
    upstream_slope,
    timemix_prior_entry,
    featmix_prior_entry,
    opening_dividend,
    opening_divisor,
    opening_power,
    normalize_scales,
    normalize_shifts,
    shift_blends,
    logarithmic_fading_speed,
    present_reward,
    *weights,
):
    plan = Plan(lax.axis_size("seg"), lax.axis_size("tok"))
    got = layer(
        plan,
        LayerIn(
            incoming_items[0],
            upstream_slope[0],
            timemix_prior_entry,
            featmix_prior_entry,
            opening_dividend,
            opening_divisor,
            opening_power,
            normalize_scales,
            normalize_shifts,
            shift_blends,
            logarithmic_fading_speed[None],
            present_reward[None],
            *weights,
        ),
        incoming_items.shape[1],
    )
    sums = got[2:9]
    if not plan.tok_here:
        sums = [lax.psum_scatter(item, "tok", scatter_dimension=0, tiled=True) for item in sums]
    placed = place_results(
        plan, [got.layer_out, got.token_grad, *sums], got.final, got.small
    )
    layer_out, token_grad, fvalue, frecept, fkey, aout, arecept, avalue, akey = placed[:9]
    numer, denom, top, gains, biases, mixes, decay, bonus = placed[9:]
    return (
        layer_out[None],
        token_grad[None],
        numer,
        denom,
        top,
        gains,
        biases,
        mixes,
        decay[0],
        bonus[0],
        akey,
        avalue,
        arecept,
        aout,
        fkey,
        fvalue,
        frecept,
    )


def solution(mesh):
    tokens, channels, whole = P("seg", "tok", None), P("seg", "tok"), P()
    spread, rows = P(None, ("seg", "tok")), P(("seg", "tok"), None)
    return jax.shard_map(
        shards,
        mesh=mesh,
        in_specs=(tokens,) * 2 + (P("seg", None),) * 2 + (channels,) * 3 + (whole,) * 12,
        out_specs=(tokens,) * 2
        + (channels,) * 3
        + (spread,) * 3
        + (P(("seg", "tok")),) * 2
        + (rows,) * 7,
        check_vma=False,
    )
```

```python
import copy
from functools import partial
from typing import Any, NamedTuple

import jax
import jax.numpy as jnp
from jax import lax
from jax.experimental import pallas as pl
from jax.experimental.pallas import tpu as pltpu
from jax.sharding import PartitionSpec as P

EMBED_SIZE = 1024
FF = 4096
VMEM_BYTES = 63 << 20
MESH = pl.DeviceIdType.MESH
FAR_FIRST = {0: (0,), 3: (1,), 5: (0,), 7: (0,), 10: (1,)}


class Plan:
    def __init__(self, count_seg, count_tok):
        self.count_seg, self.count_tok = count_seg, count_tok
        self.bits = count_seg.bit_length() - 1
        self.tok_bits = count_tok.bit_length() - 1
        self.seg_rows = EMBED_SIZE // count_seg
        self.seg_rows_ff = FF // count_seg
        self.low_bits = max(0, (128 // self.seg_rows).bit_length() - 1)
        self.pair = self.low_bits
        self.rest = [b for b in range(self.bits) if b != self.pair]
        self.orders = (self.rest, self.rest[::-1])
        self.stages = len(self.rest)
        self.slots = 1 << self.stages
        self.rows = self.seg_rows // count_tok
        self.rows_ff = self.seg_rows_ff // count_tok
        self.tok_here = self.rows % 16 == 0 and count_tok == 1 << self.tok_bits

    def recv_offset(self, stage):
        return self.slots - (self.slots >> stage)

    def slot(self, order, relative):
        total = 0
        for place, bit in enumerate(order):
            total = total + relative[bit] * (1 << (self.stages - 1 - place))
        return total


def bit_of(value, bit):
    return lax.rem(lax.div(value, 1 << bit), 2)


def flip(value, bit):
    return value + (1 - 2 * bit_of(value, bit)) * (1 << bit)


def seg_block(plan, seg, relative):
    total = bit_of(seg, plan.pair) * (1 << plan.pair)
    for bit, rel in relative.items():
        own = bit_of(seg, bit)
        total = total + (own + rel - 2 * own * rel) * (1 << bit)
    return total


def combos(bits):
    for index in range(1 << len(bits)):
        yield {bit: (index >> place) & 1 for place, bit in enumerate(bits)}


def greet(plan, seg, tok):
    barrier = pltpu.get_barrier_semaphore()
    for bit in range(plan.bits):
        pl.semaphore_signal(
            barrier, inc=1, device_id={"seg": flip(seg, bit)}, device_id_type=MESH
        )
    for step in range(1, plan.count_tok):
        pl.semaphore_signal(
            barrier,
            inc=1,
            device_id={"tok": lax.rem(tok + step, plan.count_tok)},
            device_id_type=MESH,
        )

    def wait():
        pl.semaphore_wait(barrier, plan.bits + plan.count_tok - 1)

    return wait


class Copies:
    def __init__(self, local_sems, send_sems, recv_sems):
        self.local_sems, self.send_sems, self.recv_sems = local_sems, send_sems, recv_sems
        self.locals, self.remotes, self.open = 0, 0, []

    def local(self, source, target):
        copy = pltpu.make_async_copy(source, target, self.local_sems.at[self.locals])
        self.locals += 1
        copy.start()
        self.open.append(copy)
        return copy

    def remote(self, source, target, device):
        copy = pltpu.make_async_remote_copy(
            src_ref=source,
            dst_ref=target,
            send_sem=self.send_sems.at[self.remotes],
            recv_sem=self.recv_sems.at[self.remotes],
            device_id=device,
            device_id_type=MESH,
        )
        self.remotes += 1
        copy.start()
        self.open.append(copy)
        return copy

    def wait(self, *copies):
        for copy in copies:
            copy.wait()
            self.open = [item for item in self.open if item is not copy]

    def drain(self):
        self.wait(*list(self.open))


def rows16(index):
    return pl.ds(pl.multiple_of(index * 16, 16), 16)


def rows8(index):
    return pl.ds(pl.multiple_of(index * 8, 8), 8)


LANES = EMBED_SIZE // 128


def put_rows(staged, place, value):
    for block in range(LANES):
        staged[block, place] = value[:, 128 * block : 128 * block + 128]


def get_rows(staged, place):
    return jnp.concatenate([staged[block, place] for block in range(LANES)], axis=1)


def low(value):
    return value.astype(jnp.bfloat16).astype(jnp.float32)


def layer_norm(values, gain_row, bias_row):
    centre = values - jnp.mean(values, axis=-1, keepdims=True)
    spread = jnp.mean(centre * centre, axis=-1, keepdims=True)
    return centre * lax.rsqrt(spread + 1e-05) * gain_row + bias_row


def sweep(count, body, unroll=2):
    def step(index, carry):
        body(index)
        return carry

    lax.fori_loop(0, count, step, 0, unroll=unroll)


def matmul(left, right):
    return jnp.dot(left, right, preferred_element_type=jnp.float32)


def matmul_back(left, right):
    return lax.dot_general(
        left, right, (((1,), (1,)), ((), ())), preferred_element_type=jnp.float32
    )


def merge(state, later, faded):
    numer, denom, top = state
    reduced = top - faded
    peak = jnp.maximum(reduced, later[2])
    old, new = jnp.exp(reduced - peak), jnp.exp(later[2] - peak)
    return (old * numer + new * later[0], old * denom + new * later[1], peak)


def advance(state, key, value, fading):
    numer, denom, top = state
    reduced = top - fading
    peak = jnp.maximum(reduced, key)
    old, new = jnp.exp(reduced - peak), jnp.exp(key - peak)
    return (old * numer + new * value, old * denom + new, peak)


def row_of(state, index):
    return tuple(item[index : index + 1] for item in state)


def stack_rows(states):
    return tuple(jnp.concatenate([state[part] for state in states]) for part in range(len(states[0])))


def first_before(lead_row, last_tile):
    return jnp.concatenate([lead_row, last_tile[0:7]])


def right_of(plan, tok):
    return {"tok": lax.rem(tok + 1, plan.count_tok)}


def left_of(plan, tok):
    return {"tok": lax.rem(tok + plan.count_tok - 1, plan.count_tok)}


class Chunk:
    def __init__(self, ref, lane, wide, unit, share, out, column, far_first=()):
        self.ref, self.lane, self.wide = ref, lane, wide
        self.unit, self.share, self.out, self.column = unit, share, out, column
        self.far_first = far_first


class Strand:
    def __init__(self, plan, chunk, half):
        self.chunk, self.half = chunk, half
        self.lanes = pl.ds(chunk.lane + half * chunk.wide, chunk.wide)
        self.place = pl.ds(chunk.column + half * chunk.wide, chunk.wide)
        self.far = [-1 - bit for bit in range(plan.tok_bits)] if plan.tok_here else []
        self.route = list(plan.orders[half])
        self.first, self.slots, self.settled = 0, plan.slots, 0
        self.free, self.after = plan.slots * chunk.unit, None
        self.made, self.due = [], 0.0

    def parts(self, plan):
        if not (self.half in self.chunk.far_first and self.far):
            self.route += self.far
            return [self], None
        made, room = [], (plan.count_tok - 1) * self.chunk.share
        for slot in range(plan.slots):
            part = copy.copy(self)
            part.route, part.first, part.slots = list(self.far), slot, 1
            part.free = self.free + slot * room
            made.append(part)
        self.settled, self.free = plan.tok_bits, self.free + plan.slots * room
        return made, self


class Wire:
    RATE = 86e3
    LAG = 2.5
    BACKLOG = 8.0
    FAR_BACKLOG = 2.0

    def __init__(self, plan, seg, tok, send_sems, recv_sems):
        self.plan, self.seg, self.tok = plan, seg, tok
        self.send_sems, self.recv_sems, self.count = send_sems, recv_sems, 0
        self.clock, self.free = 0.0, {}
        self.waiting, self.flying = [], []

    def load(self, axis, amount):
        ends = []
        for link in range(axis, 0) if axis < 0 else (axis,):
            passing = amount << max(0, -1 - link)
            self.free[link] = max(self.clock, self.free.get(link, 0.0)) + passing / self.RATE
            ends.append(self.free[link])
        return max(ends) + self.LAG

    def fly(self, arrival, action):
        self.flying.append((arrival, action))

    def due(self, far):
        start = max([self.clock] + [self.free.get(link, 0.0) for link in (-2, -1) if far])
        return start + 2.3

    def meet(self, *times):
        self.clock = max(self.clock, *times)

    def open(self, chunk):
        opened = []
        for half in range(2):
            parts, whole = Strand(self.plan, chunk, half).parts(self.plan)
            left = [len(parts)]

            def after(left=left, whole=whole):
                left[0] -= 1
                if not left[0]:
                    self.start(whole)

            for part in parts:
                part.after = after if whole else None
            opened += parts
        return opened

    def offer(self, chunk):
        self.waiting += self.open(chunk)
        self.serve()

    def slot_made(self, opened, relative):
        for strand in opened:
            slot = self.plan.slot(self.plan.orders[strand.half], relative)
            size, unit = strand.slots // 2, strand.chunk.unit
            if strand.after:
                if strand.first == slot:
                    self.start(strand)
            elif slot >= size:
                axis = strand.route[0]
                device = {"seg": flip(self.seg, axis)}
                to = strand.free + (slot - size) * unit
                strand.made.append(self.copy(strand, slot * unit, to, unit, device))
                strand.due = self.load(axis, 4 * strand.chunk.wide * unit)

    def slots_made(self, opened):
        for strand in opened:
            if strand.after:
                continue
            strand.route.pop(0)
            rows = strand.slots // 2 * strand.chunk.unit
            pieces = [(0, rows, strand.free)]
            strand.slots //= 2
            strand.free += rows
            self.fly(strand.due, partial(self.arrive, strand, strand.made, pieces))

    def tick(self, cost):
        self.clock += cost
        self.serve()

    def room(self):
        for strand in self.waiting:
            axis = strand.route[0]
            limit = self.BACKLOG if axis >= 0 else self.FAR_BACKLOG
            if self.free.get(axis, 0.0) - self.clock < limit:
                return strand
        return None

    def serve(self, rest=False):
        while self.flying or self.waiting:
            strand = self.room()
            if strand is not None:
                self.waiting.remove(strand)
                self.start(strand)
                continue
            if not self.flying:
                break
            soonest = min(self.flying, key=lambda item: item[0])
            if soonest[0] > self.clock and not rest:
                break
            self.clock = max(self.clock, soonest[0])
            self.flying.remove(soonest)
            soonest[1]()

    def copy(self, strand, source, target, rows, device):
        index, self.count = self.count, self.count + 1
        made = pltpu.make_async_remote_copy(
            src_ref=strand.chunk.ref.at[pl.ds(source, rows), strand.lanes],
            dst_ref=strand.chunk.ref.at[pl.ds(target, rows), strand.lanes],
            send_sem=self.send_sems.at[index],
            recv_sem=self.recv_sems.at[index],
            device_id=device,
            device_id_type=MESH,
        )
        made.start()
        return made

    def start(self, strand):
        plan, chunk, base = self.plan, strand.chunk, strand.free
        axis, copies, pieces = strand.route.pop(0), [], []
        unit, share = chunk.unit, chunk.share
        kept = self.tok
        if axis < 0:
            bit = -1 - axis
            device = {"tok": flip(self.tok, bit)}
            sent, strand.settled = flip(self.tok, bit), bit + 1
        else:
            device, sent = {"seg": flip(self.seg, axis)}, self.tok
            strand.slots //= 2
        first = strand.slots if axis >= 0 else strand.first
        if strand.settled:
            step = 1 << strand.settled
            parts = plan.count_tok // step
            for slot in range(strand.slots):
                for part in range(parts):
                    there = lax.rem(sent, step) + step * part
                    source = pl.multiple_of((first + slot) * unit + there * share, share)
                    here = lax.rem(kept, step) + step * part
                    near = pl.multiple_of((strand.first + slot) * unit + here * share, share)
                    to = base + (slot * parts + part) * share
                    copies.append(self.copy(strand, source, to, share, device))
                    pieces.append((near, share, to))
            rows = strand.slots * parts * share
        else:
            rows = strand.slots * unit
            copies.append(self.copy(strand, rows, base, rows, device))
            pieces.append((0, rows, base))
        strand.free += rows
        arrival = self.load(axis, 4 * chunk.wide * rows)
        self.fly(arrival, lambda: self.arrive(strand, copies, pieces))

    def arrive(self, strand, copies, pieces):
        chunk = strand.chunk
        for copy in copies:
            copy.wait()
        for near, rows, came in pieces:
            block = min(rows, 32768 // chunk.wide)

            def add(index):
                offset = index * block
                place = pl.ds(pl.multiple_of(near + offset, 16), block)
                there = pl.ds(pl.multiple_of(came + offset, 16), block)
                total = chunk.ref[place, strand.lanes].astype(jnp.float32)
                total = total + chunk.ref[there, strand.lanes].astype(jnp.float32)
                if strand.route or strand.after:
                    chunk.ref[place, strand.lanes] = total.astype(jnp.bfloat16)
                else:
                    chunk.out[pl.ds(pl.multiple_of(offset, 8), block), strand.place] = total

            sweep(rows // block, add, 1)
            self.clock += 1.2e-6 * rows * chunk.wide + 0.05
        if strand.route:
            self.start(strand)
        elif strand.after:
            strand.after()


def outer_chunk(plan, seg, chunk, left, left_lane, right, right_lane, only=None):
    nsub = 1 << plan.low_bits
    high = [b for b in plan.rest if b >= plan.low_bits]
    columns = pl.ds(right_lane, 2 * chunk.wide)
    tall = chunk.unit == plan.seg_rows_ff
    for relative in only or combos(high):
        group = lax.div(lax.div(seg_block(plan, seg, relative), nsub), 2)
        span = chunk.unit if tall else chunk.unit * nsub
        for piece in range(nsub if tall else 1):
            index = group * nsub + piece if tall else group
            taken = left[:, pl.ds(pl.multiple_of(left_lane + index * span, 128), span)]
            result = lax.dot_general(
                taken,
                right[:, columns],
                (((0,), (0,)), ((), ())),
                preferred_element_type=jnp.float32,
            ).astype(jnp.bfloat16)
            for part in (piece,) if tall else range(nsub):
                full = dict(relative)
                for bit in range(plan.low_bits):
                    mine, want = bit_of(seg, bit), (part >> bit) & 1
                    full[bit] = mine + want - 2 * mine * want
                rows = result if tall else result[part * chunk.unit : (part + 1) * chunk.unit]
                for half in range(2):
                    slot = plan.slot(plan.orders[half], full)
                    start = slot * chunk.unit
                    if not isinstance(start, int):
                        start = pl.multiple_of(start, chunk.unit)
                    lanes = pl.ds(chunk.lane + half * chunk.wide, chunk.wide)
                    chunk.ref[pl.ds(start, chunk.unit), lanes] = rows[
                        :, half * chunk.wide : (half + 1) * chunk.wide
                    ]


def fold(value):
    return value[0:8] + value[8:16]


def total_rows(value):
    return jnp.sum(value, axis=0, keepdims=True)


def norm_back(values, slope, gain_row):
    centre = values - jnp.mean(values, axis=-1, keepdims=True)
    rate = lax.rsqrt(jnp.mean(centre * centre, axis=-1, keepdims=True) + 1e-05)
    scaled = centre * rate
    inner = slope * gain_row
    mean_inner = jnp.mean(inner, axis=-1, keepdims=True)
    mean_along = jnp.mean(inner * scaled, axis=-1, keepdims=True)
    return rate * (inner - mean_inner - scaled * mean_along), slope * scaled


class LayerIn(NamedTuple):
    x: Any
    up: Any
    prior_one: Any
    prior_two: Any
    open_num: Any
    open_den: Any
    open_top: Any
    scales: Any
    shifts: Any
    blends: Any
    speed: Any
    reward: Any
    wk: Any
    wv: Any
    wr: Any
    wo: Any
    wl: Any
    wp: Any
    wa: Any


class LayerOut(NamedTuple):
    layer_out: Any
    token_grad: Any
    fvalue: Any
    frecept: Any
    fkey: Any
    aout: Any
    arecept: Any
    avalue: Any
    akey: Any
    final: Any
    small: Any
    cat_weighted: Any
    cat_recept_mix: Any
    cat_value_mix: Any
    cat_key_mix: Any
    out_kf: Any
    out_vf: Any
    out_recept: Any
    out_xp: Any
    out_nf: Any


class LayerHeld(NamedTuple):
    vl: Any
    vp: Any
    va: Any
    early: Any
    tall: Any
    csq: Any
    cfr: Any
    cfk: Any
    gc: Any
    gg: Any
    gh: Any
    sq: Any
    f0: Any
    f1: Any
    f2: Any
    f3: Any
    f4: Any
    f5: Any
    staged: Any
    row_out: Any
    row_in: Any
    state_out: Any
    state_in: Any
    back_out: Any
    back_in: Any
    entry: Any
    small_in: Any
    wire_send: Any
    wire_recv: Any
    local_sems: Any
    send_sems: Any
    recv_sems: Any
    ready: Any


def layer_kernel(plan, *refs):
    count_in, count_out = len(LayerIn._fields), len(LayerOut._fields)
    a = LayerIn(*refs[:count_in])
    o = LayerOut(*refs[count_in : count_in + count_out])
    h = LayerHeld(*refs[count_in + count_out :])
    seg, tok = lax.axis_index("seg"), lax.axis_index("tok")
    tokens = h.sq.shape[1]
    steps, pairs = tokens // 8, tokens // 16
    every = lambda i: pl.ds(i, 8, stride=steps)
    shifted16 = lambda i: pl.ds(pl.multiple_of(16 * i + 8, 8), 16)
    own_rows, pair_rows = pl.ds(0, tokens), pl.ds(tokens, tokens)
    partner = {"seg": flip(seg, plan.pair)}
    mine = bit_of(seg, plan.pair)
    last_tok = plan.count_tok - 1
    half = EMBED_SIZE // 2
    copies = Copies(h.local_sems, h.send_sems, h.recv_sems)
    load = copies.local
    tile_zero = jnp.zeros((8, EMBED_SIZE), jnp.float32)
    blend = lambda j: a.blends[j : j + 1]
    others = lambda: [
        {"tok": lax.rem(tok + step, plan.count_tok)} for step in range(1, plan.count_tok)
    ]

    xb, ub = h.gh.at[2, own_rows], h.gh.at[3, own_rows]
    at_x = load(a.x, xb)
    at_wk, at_wv = load(a.wk, h.vp.at[0]), load(a.wv, h.vp.at[1])
    at_wr, at_wo = load(a.wr, h.vp.at[2]), load(a.wo, h.vp.at[3])
    at_up = load(a.up, ub)
    at_va = load(a.wa, h.va)
    at_vl = [load(a.wl.at[:, pl.ds(1024 * j, 1024)], h.vl.at[j]) for j in range(4)]
    all_here = greet(plan, seg, tok)
    wire = Wire(plan, seg, tok, h.wire_send, h.wire_recv)

    def share(source, target, wide, at=0):
        count = source.shape[1] // (2 * wide)
        made = []
        for pick in range(count):
            own = pl.ds(pl.multiple_of((2 * pick + mine) * wide, wide), wide)
            other = pl.ds(pl.multiple_of((2 * pick + 1 - mine) * wide, wide), wide)
            place = pl.ds(pl.multiple_of((at + pick) * wide, wide), wide)
            made.append(load(source.at[:, own], target.at[own_rows, place]))
            made.append(copies.remote(source.at[:, other], target.at[pair_rows, place], partner))
        return made

    def to_pair(ref):
        return copies.remote(ref.at[own_rows], ref.at[pair_rows], partner), wire.due(False)

    def meet(*pairs):
        for copy, due in pairs:
            wire.meet(due)
            copies.wait(copy)

    wide = max(128, plan.seg_rows)

    nf, xp = h.f0, h.f1
    copies.wait(at_x)

    def widen(i):
        put_rows(h.staged, rows16(i), xb[rows16(i)].astype(jnp.float32))

    sweep(pairs, widen, 4)
    gain, bias = a.scales[0:1], a.shifts[0:1]

    def norm_one(i):
        tile = get_rows(h.staged, every(i))
        xp[rows8(i)] = tile
        nf[rows8(i + 1)] = low(layer_norm(tile, gain, bias))

    norm_one(steps - 1)
    h.row_out[0] = nf[pl.ds(8 * steps, 8)]
    all_here()
    row = copies.remote(h.row_out.at[0], h.row_in.at[0], right_of(plan, tok))
    sweep(steps, norm_one, 8)

    def mix_one(places):
        def step(i):
            before, normed = nf[rows16(i)], nf[shifted16(i)]
            for place in places:
                weight = blend(place)
                mixed = normed * weight + before * (1.0 - weight)
                h.sq[place, rows16(i)] = mixed.astype(jnp.bfloat16)

        return step

    sweep(pairs - 1, lambda i: mix_one((0, 1))(i + 1), 2)
    copies.wait(row)
    lead = jnp.where(tok == 0, a.prior_one[...].astype(jnp.float32), h.row_in[0, 7:8])
    nf[0:8] = first_before(lead, nf[pl.ds(8 * steps, 8)])
    mix_one((0, 1))(0)
    mixes = share(h.sq.at[0], o.cat_key_mix, wide) + share(h.sq.at[1], o.cat_value_mix, wide)
    at_nf, at_xp = load(nf, o.out_nf), load(xp.at[own_rows], o.out_xp)
    kf, vf, recept = h.f2, h.f3, h.f4
    copies.wait(at_wk)
    kf[own_rows] = low(matmul(h.sq[0], h.vp[0]))
    copies.wait(at_wv)
    vf[own_rows] = low(matmul(h.sq[1], h.vp[1]))
    at_kf, at_vf = load(kf.at[own_rows], o.out_kf), load(vf.at[own_rows], o.out_vf)

    fading_row = jnp.exp(a.speed[...])
    fading = jnp.broadcast_to(fading_row, (8, EMBED_SIZE))
    reward = jnp.broadcast_to(a.reward[...], (8, EMBED_SIZE))

    def alone(i, state):
        return advance(state, kf[rows8(i)], vf[rows8(i)], fading)

    stretches = lax.fori_loop(0, steps, alone, (tile_zero, tile_zero, tile_zero - 1e30), unroll=2)
    stretch_fade = fading_row * steps
    total = row_of(stretches, 0)
    for j in range(1, 8):
        total = merge(total, row_of(stretches, j), stretch_fade)
    portion = EMBED_SIZE // plan.count_tok
    lanes = pl.ds(pl.multiple_of(tok * portion, portion), portion)
    h.state_out[...] = tile_zero
    for part, opening in enumerate((a.open_num, a.open_den, a.open_top)):
        h.state_out[part : part + 1] = total[part]
        h.state_out[3 + part : 4 + part, lanes] = opening[...]
    sent = [copies.remote(h.state_out, h.state_in.at[tok], device) for device in others()]
    h.state_in[tok] = h.state_out[...]
    sweep(pairs, mix_one((2,)), 2)
    mixes += share(h.sq.at[2], o.cat_recept_mix, wide)
    copies.wait(at_wr)
    recept[own_rows] = jax.nn.sigmoid(matmul(h.sq[2], h.vp[2]))
    at_recept = load(recept.at[own_rows], o.out_recept)
    upf = h.f0
    copies.wait(at_up, at_nf)

    def widen_up(i):
        put_rows(h.staged, rows16(i), ub[rows16(i)].astype(jnp.float32))

    sweep(pairs, widen_up, 4)

    copies.wait(*sent)
    state = tuple(
        sum(h.state_in[z, 3 + part : 4 + part] for z in range(plan.count_tok)) for part in range(3)
    )
    entry = state
    for z in range(plan.count_tok):
        entry = tuple(jnp.where(tok == z, new, old) for new, old in zip(state, entry))
        later = tuple(h.state_in[z, part : part + 1] for part in range(3))
        state = merge(state, later, fading_row * tokens)
    for part in range(3):
        h.state_out[part : part + 1] = state[part]
    o.final[...] = h.state_out[:, lanes]
    entries = [entry]
    for j in range(7):
        entries.append(merge(entries[-1], row_of(stretches, j), stretch_fade))
    entries = stack_rows(entries)
    for part in range(3):
        h.entry[8 * part : 8 * part + 8] = entries[part]
    copies.wait(at_kf)
    mixed = h.f2

    def emit(state, i):
        key, value = kf[rows8(i)], vf[rows8(i)]
        present = reward + key
        peak = jnp.maximum(state[2], present)
        old, new = jnp.exp(state[2] - peak), jnp.exp(present - peak)
        result = (old * state[0] + new * value) / (old * state[1] + new)
        return advance(state, key, value, fading), low(result)

    def recur(i, state):
        state, one = emit(state, 2 * i)
        state, two = emit(state, 2 * i + 1)
        both_rows = jnp.concatenate([one, two])
        mixed[rows16(i)] = both_rows
        h.sq[3, rows16(i)] = (recept[rows16(i)] * both_rows).astype(jnp.bfloat16)
        return state

    lax.fori_loop(0, pairs, recur, entries, unroll=2)
    mixes += share(h.sq.at[3], o.cat_weighted, wide)
    copies.wait(at_wo, at_xp)
    middle = h.f1
    middle[own_rows] = xp[own_rows] + matmul(h.sq[3], h.vp[3])
    at_vp = [load(a.wp.at[pl.ds(1024 * j, 1024)], h.vp.at[j]) for j in range(4)]

    gain_two, bias_two = a.scales[1:2], a.shifts[1:2]
    nf2 = h.f5

    def norm_two(i):
        nf2[rows8(i + 1)] = low(layer_norm(middle[rows8(i)], gain_two, bias_two))

    norm_two(steps - 1)
    h.row_out[1] = nf2[pl.ds(8 * steps, 8)]
    row = copies.remote(h.row_out.at[1], h.row_in.at[1], right_of(plan, tok))
    sweep(steps, norm_two, 8)
    key_two, recept_two = h.gh.at[0, own_rows], h.gh.at[1, own_rows]

    def mix_two(i):
        before, normed = nf2[rows16(i)], nf2[shifted16(i)]
        for place, target in ((3, key_two), (4, recept_two)):
            weight = blend(place)
            target[rows16(i)] = (normed * weight + before * (1.0 - weight)).astype(jnp.bfloat16)

    sweep(pairs - 1, lambda i: mix_two(i + 1), 2)
    copies.wait(row)
    lead = jnp.where(tok == 0, a.prior_two[...].astype(jnp.float32), h.row_in[1, 7:8])
    nf2[0:8] = first_before(lead, nf2[pl.ds(8 * steps, 8)])
    mix_two(0)
    twos = share(key_two, h.cfk, wide) + share(recept_two, h.cfr, wide)
    gate, carried = h.f3, h.f4
    copies.wait(at_va, at_vf)
    gate[own_rows] = jax.nn.sigmoid(matmul(recept_two[...], h.va[...]))

    def carried_slope(i):
        up = jnp.concatenate([get_rows(h.staged, every(2 * i)), get_rows(h.staged, every(2 * i + 1))])
        upf[rows16(i)] = up
        h.gc[rows16(i)] = (up * gate[rows16(i)]).astype(jnp.bfloat16)

    sweep(pairs, carried_slope, 2)
    pair_gc = to_pair(h.gc)
    copies.wait(*mixes)
    share_rows = plan.rows if plan.tok_here else 0
    share_ff = plan.rows_ff if plan.tok_here else 0
    tall = [
        Chunk(h.tall, 256 * j, 128, plan.seg_rows_ff, share_ff, o.fvalue, 256 * j, FAR_FIRST.get(j, ()))
        for j in range(4)
    ]
    flat = lambda ref, out, column, far_first: Chunk(
        ref, 0, half, plan.seg_rows, share_rows, out, column, far_first
    )
    frecept = flat(h.early.at[0], o.frecept, 0, FAR_FIRST.get(4, ()))
    fkey = [flat(h.early.at[1 + j], o.fkey, 1024 * j, FAR_FIRST.get(5 + j, ())) for j in range(4)]
    late = [
        flat(h.vl.at[j], out, 0, FAR_FIRST.get(9 + j, ()))
        for j, out in enumerate((o.aout, o.arecept, o.avalue, o.akey))
    ]

    def offer(chunk, left, left_lane, right, right_lane):
        outer_chunk(plan, seg, chunk, left, left_lane, right, right_lane)
        wire.clock += 0.95
        wire.offer(chunk)

    nsub = 1 << plan.low_bits
    high = [bit for bit in plan.rest if bit >= plan.low_bits]
    blocks = sorted(combos(high), key=lambda relative: -sum(relative.values()))
    opened = [wire.open(chunk) for chunk in tall]
    copies.wait(*at_vl)

    def hidden_block(relative):
        block = lax.div(lax.div(seg_block(plan, seg, relative), nsub), 2)
        for side in range(2):
            columns = pl.ds(half * side, half)
            hidden = jnp.maximum(matmul(key_two[...], h.vl[block, :, columns]), 0.0)
            h.sq[block, :, columns] = (hidden * hidden).astype(jnp.bfloat16)
        return share(h.sq.at[block], h.csq, 4 * wide, block)

    def payload_slot(relative, squares):
        copies.wait(*squares)
        for j in (1, 2, 3, 0):
            outer_chunk(plan, seg, tall[j], h.csq, 0, h.gc, 256 * j, [relative])
            wire.clock += 0.24
            if not plan.low_bits:
                wire.slot_made(opened[j], relative)

    squares = [hidden_block(blocks[0])]
    for place in range(1, len(blocks)):
        squares.append(hidden_block(blocks[place]))
        if place == 1:
            copies.wait(pair_gc[0])
            wire.clock = 0.0
        else:
            wire.clock += 1.1
        payload_slot(blocks[place - 1], squares[place - 1])
    copies.wait(at_recept, at_vp[0])
    carried[own_rows] = matmul(h.sq[0], h.vp[0])
    wire.clock += 1.0
    payload_slot(blocks[-1], squares[-1])
    for chunk, strands in zip(tall, opened):
        if plan.low_bits:
            wire.waiting += strands
        else:
            wire.slots_made(strands)
    wire.serve()
    cats = [
        load(cat, h.csq.at[:, pl.ds(half * j, half)])
        for j, cat in enumerate(
            (o.cat_weighted, o.cat_recept_mix, o.cat_value_mix, o.cat_key_mix)
        )
    ]
    for j in range(1, 4):
        copies.wait(at_vp[j])
        carried[own_rows] += matmul(h.sq[j], h.vp[j])
        wire.tick(1.0)

    def close(i):
        gates, sums = gate[rows16(i)], carried[rows16(i)]
        gated = gates * sums
        result = middle[rows16(i)] + gated
        h.gg[rows16(i)] = (upf[rows16(i)] * gated * (1.0 - gates)).astype(jnp.bfloat16)
        put_rows(h.staged, every(2 * i), result[0:8])
        put_rows(h.staged, every(2 * i + 1), result[8:16])

    sweep(pairs, close, 2)
    pair_gg = to_pair(h.gg)
    narrowed = h.gh.at[3, own_rows]

    def narrow(i):
        narrowed[rows16(i)] = get_rows(h.staged, rows16(i)).astype(jnp.bfloat16)

    sweep(pairs, narrow, 4)
    at_out = load(narrowed, o.layer_out)
    wire.tick(1.5)

    def unmix(grads, weights, kept, row_place):
        def across(place):
            slopes = [grad[place] for grad in grads]
            total = slopes[0] * (1.0 - weights[0])
            for item, weight in zip(slopes[1:], weights[1:]):
                total = total + item * (1.0 - weight)
            return slopes, low(total)

        first = across(pl.ds(0, 8))[1]
        h.row_out[row_place] = first
        row = copies.remote(h.row_out.at[row_place], h.row_in.at[row_place], left_of(plan, tok))
        due = wire.due(True)

        def step(i, sums):
            place = rows16(i)
            slopes, moved = across(place)
            difference = kept[shifted16(i)] - kept[place]
            direct = slopes[0] * weights[0]
            for item, weight in zip(slopes[1:], weights[1:]):
                direct = direct + item * weight
            grads[0][place] = direct
            grads[-1][place] = moved
            return tuple(fold(item * difference) + old for item, old in zip(slopes, sums))

        def finish():
            sums = lax.fori_loop(0, pairs, step, (tile_zero,) * len(grads), unroll=2)
            wire.tick(1.5)
            wire.meet(due)
            copies.wait(row)
            end = jnp.where(tok == last_tok, 0.0, h.row_in[row_place, 0:1])
            grads[-1][pl.ds(tokens, 8)] = jnp.concatenate([first[1:8], end])
            return [total_rows(item) for item in sums]

        return finish

    copies.wait(*twos)
    sent = []
    for j in range(4):
        h.f3[own_rows] = matmul_back(h.gc[own_rows], h.vp[j])
        if j == 3:
            copies.wait(at_out)

        def hidden_slope(i):
            rate = 2.0 * jnp.sqrt(h.sq[j, rows16(i)].astype(jnp.float32))
            h.gh[j, rows16(i)] = (h.f3[rows16(i)] * rate).astype(jnp.bfloat16)

        sweep(pairs, hidden_slope, 2)
        sent.append(to_pair(h.gh.at[j]))
        wire.tick(1.3)
    at_wo = load(a.wo, h.vp.at[3])
    at_wk, at_wv = load(a.wk, h.vp.at[0]), load(a.wv, h.vp.at[1])
    at_wr = load(a.wr, h.vp.at[2])
    for j in range(4):
        part = matmul_back(h.gh[j, own_rows], h.vl[j])
        h.f3[own_rows] = part if j == 0 else h.f3[own_rows] + part
        wire.tick(1.1)
    h.f4[own_rows] = matmul_back(h.gg[own_rows], h.va[...])
    wire.tick(1.0)
    finish_two = unmix((h.f3, h.f4), (blend(3), blend(4)), nf2, 2)
    meet(pair_gg)
    offer(frecept, h.cfr, 0, h.gg, 0)
    for j in range(4):
        meet(sent[j])
        offer(fkey[j], h.cfk, 0, h.gh.at[j], 0)

    neighbours = [{"seg": flip(seg, bit)} for bit in range(plan.bits)] + others()
    for device in neighbours:
        pl.semaphore_signal(h.ready, inc=1, device_id=device, device_id_type=MESH)

    def norm_pull(direct, moved, values, gain_row, emit):
        def step(i, sums):
            place = rows16(i)
            slope = direct[place] + moved[shifted16(i)]
            back, along = norm_back(values[place], slope, gain_row)
            emit(i, back)
            return fold(along) + sums[0], fold(slope) + sums[1]

        sums = lax.fori_loop(0, pairs, step, (tile_zero, tile_zero), unroll=4)
        return [total_rows(item) for item in sums]

    sums_two = finish_two()
    recept = h.f5
    at_recept = load(o.out_recept, recept.at[own_rows])
    wire.tick(0.3)
    total_slope = h.f0

    def middle_slope(i, back):
        total = upf[rows16(i)] + back
        total_slope[rows16(i)] = total
        h.gh[0, rows16(i)] = total.astype(jnp.bfloat16)

    gain_sum_two, bias_sum_two = norm_pull(h.f3, h.f4, middle, gain_two, middle_slope)
    key_ref, value_ref, slope_ref, top_ref, numer_ref = h.f1, h.f4, h.f3, h.f2, h.f5
    at_k = load(o.out_kf, key_ref.at[own_rows])
    at_v = load(o.out_vf, value_ref.at[own_rows])
    pl.semaphore_wait(h.ready, len(neighbours))
    pair_out = to_pair(h.gh.at[0])
    wire.tick(2.5)
    copies.wait(at_wo)
    slope_ref[own_rows] = matmul_back(h.gh[0, own_rows], h.vp[3])
    wire.tick(1.0)
    copies.wait(at_recept)

    def wkv_slope(i):
        place = rows16(i)
        slope, gates = slope_ref[place], recept[place]
        gated = slope * gates
        slope_ref[place] = low(gated)
        h.gh[1, place] = (gated * mixed[place] * (1.0 - gates)).astype(jnp.bfloat16)

    sweep(pairs, wkv_slope, 2)
    pair_recept = to_pair(h.gh.at[1])
    wire.tick(1.0)

    copies.wait(at_k, at_v)

    def terms(state, key, value, slope):
        numer, denom, top = state
        present = reward + key
        peak = jnp.maximum(top, present)
        old, new = jnp.exp(top - peak), jnp.exp(present - peak)
        inverse = 1.0 / (old * denom + new)
        result = (old * numer + new * value) * inverse
        reduced = top - fading
        next_top = jnp.maximum(reduced, key)
        keep, put = jnp.exp(reduced - next_top), jnp.exp(key - next_top)
        scaled = slope * inverse
        return old * scaled, new * scaled, result, keep, put, next_top

    def onward(i, carry):
        numer, denom, top, alpha, beta, product = carry
        place = rows8(i)
        key, value = key_ref[place], value_ref[place]
        top_ref[place] = top
        numer_ref[place] = numer
        put_rows(h.staged, place, denom)
        into, _, result, keep, put, next_top = terms(
            (numer, denom, top), key, value, slope_ref[place]
        )
        alpha = alpha + product * into
        beta = beta - product * into * result
        product = product * keep
        return keep * numer + put * value, keep * denom + put, next_top, alpha, beta, product

    entry = tuple(h.entry[8 * part : 8 * part + 8] for part in range(3))
    swept = lax.fori_loop(
        0, steps, onward, entry + (tile_zero, tile_zero, tile_zero + 1.0), unroll=2
    )
    stretches = swept[3:]

    def pull_back(later, stretch):
        return (stretch[0] + stretch[2] * later[0], stretch[1] + stretch[2] * later[1])

    nothing = (jnp.zeros((1, EMBED_SIZE), jnp.float32),) * 2
    total, product = nothing, jnp.ones((1, EMBED_SIZE), jnp.float32)
    for j in range(7, -1, -1):
        total = pull_back(total, row_of(stretches, j))
        product = product * stretches[2][j : j + 1]
    h.back_out[...] = tile_zero
    for part, item in enumerate(total + (product,)):
        h.back_out[part : part + 1] = item
    wire.tick(4.0)
    sent = [copies.remote(h.back_out, h.back_in.at[tok], device) for device in others()]
    due = wire.due(True)
    h.back_in[tok] = h.back_out[...]
    meet(pair_out)
    copies.wait(cats[0])
    offer(late[0], h.csq, 0, h.gh.at[0], 0)
    meet(pair_recept)
    copies.wait(cats[1])
    offer(late[1], h.csq, half, h.gh.at[1], 0)
    wire.meet(due)
    copies.wait(*sent)
    later, entering = nothing, nothing
    for z in range(last_tok, -1, -1):
        entering = tuple(jnp.where(tok == z, new, old) for new, old in zip(later, entering))
        later = pull_back(later, tuple(h.back_in[z, part : part + 1] for part in range(3)))
    entries = [entering]
    for j in range(7, 0, -1):
        entries.insert(0, pull_back(entries[0], row_of(stretches, j)))
    entries = stack_rows(entries)

    def back(i, carry):
        alpha, beta, fade_sum, reward_sum = carry
        place = rows8(i)
        key, value, slope = key_ref[place], value_ref[place], slope_ref[place]
        numer, denom, top = numer_ref[place], get_rows(h.staged, place), top_ref[place]
        into, now, result, keep, put, _ = terms((numer, denom, top), key, value, slope)
        reward_term = now * (value - result)
        key_slope = reward_term + put * (alpha * value + beta)
        value_slope = now + put * alpha
        fade_sum = fade_sum - keep * (alpha * numer + beta * denom)
        alpha, beta = keep * alpha + into, keep * beta - into * result
        return (alpha, beta, fade_sum, reward_sum + reward_term), key_slope, value_slope

    def backward_pair(index, carry):
        i = pairs - 1 - index
        carry, key_two, value_two = back(2 * i + 1, carry)
        carry, key_one, value_one = back(2 * i, carry)
        h.gh[2, rows16(i)] = jnp.concatenate([value_one, value_two]).astype(jnp.bfloat16)
        h.gh[3, rows16(i)] = jnp.concatenate([key_one, key_two]).astype(jnp.bfloat16)
        return carry

    _, _, fade_sum, reward_sum = lax.fori_loop(
        0, pairs, backward_pair, entries + (tile_zero, tile_zero)
    )
    decay = total_rows(fade_sum) * fading_row
    bonus = total_rows(reward_sum)
    pair_value, pair_key = to_pair(h.gh.at[2]), to_pair(h.gh.at[3])
    nf, xp = h.f4, h.f5
    at_nf = load(o.out_nf, nf)
    at_xp = load(o.out_xp, xp.at[own_rows])
    wire.tick(5.5)
    copies.wait(at_wk)
    h.f2[own_rows] = matmul_back(h.gh[3, own_rows], h.vp[0])
    wire.tick(1.0)
    copies.wait(at_wv, at_wr)
    h.f1[own_rows] = matmul_back(h.gh[2, own_rows], h.vp[1])
    wire.tick(1.0)
    h.f3[own_rows] = matmul_back(h.gh[1, own_rows], h.vp[2])
    wire.tick(1.0)
    copies.wait(at_nf)
    finish_one = unmix((h.f2, h.f1, h.f3), (blend(0), blend(1), blend(2)), nf, 3)
    meet(pair_value)
    copies.wait(cats[2])
    offer(late[2], h.csq, 2 * half, h.gh.at[2], 0)
    meet(pair_key)
    copies.wait(cats[3])
    offer(late[3], h.csq, 3 * half, h.gh.at[3], 0)
    sums_one = finish_one()
    wire.tick(0.5)
    copies.wait(at_xp)

    def input_slope(i, back):
        total = total_slope[rows16(i)] + back
        put_rows(h.staged, every(2 * i), total[0:8])
        put_rows(h.staged, every(2 * i + 1), total[8:16])

    gain_sum_one, bias_sum_one = norm_pull(h.f2, h.f3, xp, a.scales[0:1], input_slope)
    wire.tick(2.5)

    small_rows = [gain_sum_one, gain_sum_two, bias_sum_one, bias_sum_two]
    small_rows += sums_one + sums_two + [decay, bonus]
    o.small[...] = jnp.concatenate(
        small_rows + [jnp.zeros((16 - len(small_rows), EMBED_SIZE), jnp.float32)]
    )

    def small_stage(bit):
        copy = copies.remote(o.small, h.small_in.at[bit], {"seg": flip(seg, bit)})

        def next_stage():
            copies.wait(copy)
            o.small[...] += h.small_in[bit]
            if bit + 1 < plan.bits:
                small_stage(bit + 1)
            else:
                small_far()

        wire.fly(wire.clock + 4.0, next_stage)

    def small_far():
        base = plan.bits - 1
        sent = [
            copies.remote(o.small, h.small_in.at[base + 1 + step], device)
            for step, device in enumerate(others())
        ]

        def end():
            copies.wait(*sent)
            total = o.small[...]
            for step in range(1, plan.count_tok):
                total = total + h.small_in[base + step]
            o.small[...] = total

        wire.fly(wire.clock + 6.0, end)

    small_stage(0)

    def narrow_slope(i):
        h.sq[0, rows16(i)] = get_rows(h.staged, rows16(i)).astype(jnp.bfloat16)

    sweep(pairs, narrow_slope, 4)
    load(h.sq.at[0], o.token_grad)
    wire.serve(rest=True)
    copies.drain()


def layer(plan, arrays, tokens):
    f32, b16 = jnp.float32, jnp.bfloat16
    half = EMBED_SIZE // 2
    anywhere, vmem = pl.BlockSpec(memory_space=pl.ANY), pl.BlockSpec(memory_space=pltpu.VMEM)
    sds, held = jax.ShapeDtypeStruct, pltpu.VMEM
    far = plan.count_tok - 1
    rows = plan.rows if plan.tok_here else plan.seg_rows
    rows_ff = plan.rows_ff if plan.tok_here else plan.seg_rows_ff
    extra = far if plan.tok_here else 0
    wide = (tokens, EMBED_SIZE)
    share = sds((rows, EMBED_SIZE), f32)
    cat, kept = sds((2 * tokens, half), b16), sds(wide, f32)
    out_shape = LayerOut(
        layer_out=sds(wide, b16),
        token_grad=sds(wide, b16),
        fvalue=sds((rows_ff, EMBED_SIZE), f32),
        frecept=share,
        fkey=sds((rows, FF), f32),
        aout=share,
        arecept=share,
        avalue=share,
        akey=share,
        final=sds((8, EMBED_SIZE // plan.count_tok), f32),
        small=sds((16, EMBED_SIZE), f32),
        cat_weighted=cat,
        cat_recept_mix=cat,
        cat_value_mix=cat,
        cat_key_mix=cat,
        out_kf=kept,
        out_vf=kept,
        out_recept=kept,
        out_xp=kept,
        out_nf=sds((tokens + 8, EMBED_SIZE), f32),
    )
    out_specs = LayerOut(*[anywhere] * 2, *[vmem] * 9, *[anywhere] * 9)
    in_specs = LayerIn(*[anywhere] * 2, *[vmem] * 10, *[anywhere] * 7)
    square = (4, EMBED_SIZE, EMBED_SIZE)
    units = 2 * plan.slots - 1
    one = held((tokens + 8, EMBED_SIZE), f32)
    tiles = held((4, 8, EMBED_SIZE), f32)
    states = held((plan.count_tok, 8, EMBED_SIZE), f32)
    several = pltpu.SemaphoreType.DMA((120,))
    scratch = LayerHeld(
        vl=held(square, b16),
        vp=held(square, b16),
        va=held(square[1:], b16),
        early=held((5, units * plan.seg_rows + extra * plan.rows, EMBED_SIZE), b16),
        tall=held((units * plan.seg_rows_ff + extra * plan.rows_ff, EMBED_SIZE), b16),
        csq=held((2 * tokens, FF // 2), b16),
        cfr=held((2 * tokens, half), b16),
        cfk=held((2 * tokens, half), b16),
        gc=held((2 * tokens, EMBED_SIZE), b16),
        gg=held((2 * tokens, EMBED_SIZE), b16),
        gh=held((4, 2 * tokens, EMBED_SIZE), b16),
        sq=held((4,) + wide, b16),
        f0=one,
        f1=one,
        f2=one,
        f3=one,
        f4=one,
        f5=one,
        staged=held((LANES, tokens, 128), f32),
        row_out=tiles,
        row_in=tiles,
        state_out=held((8, EMBED_SIZE), f32),
        state_in=states,
        back_out=held((8, EMBED_SIZE), f32),
        back_in=states,
        entry=held((24, EMBED_SIZE), f32),
        small_in=held((plan.bits + far, 16, EMBED_SIZE), f32),
        wire_send=pltpu.SemaphoreType.DMA((256,)),
        wire_recv=pltpu.SemaphoreType.DMA((256,)),
        local_sems=several,
        send_sems=several,
        recv_sems=several,
        ready=pltpu.SemaphoreType.REGULAR,
    )
    got = pl.pallas_call(
        partial(layer_kernel, plan),
        out_shape=list(out_shape),
        in_specs=list(in_specs),
        out_specs=list(out_specs),
        scratch_shapes=list(scratch),
        compiler_params=pltpu.CompilerParams(
            collective_id=0, has_side_effects=True, vmem_limit_bytes=VMEM_BYTES
        ),
    )(*arrays)
    return LayerOut(*got)


def place_kernel(share, count, *refs):
    sources, finals, small = refs[:count], refs[count], refs[count + 1]
    targets, rest = refs[count + 2 : 2 * count + 2], refs[2 * count + 2 : -count - 1]
    held, sems = refs[-count - 1 : -1], refs[-1]
    into = [pltpu.make_async_copy(sources[i], held[i], sems.at[0, i]) for i in range(count)]
    away = [pltpu.make_async_copy(held[i], targets[i], sems.at[1, i]) for i in range(count)]
    for copy in into:
        copy.start()
    for part in range(3):
        rest[part][...] = finals[part : part + 1]
    device = lax.axis_index("seg") * lax.axis_size("tok") + lax.axis_index("tok")
    shift = lax.rem(EMBED_SIZE - device * share, EMBED_SIZE)
    turned = pltpu.roll(small[...], shift, 1)[:, :share]
    first = 0
    for target in rest[3:]:
        rows = target.shape[0]
        target[...] = turned[first : first + rows]
        first += rows
    for index in range(count):
        into[index].wait()
        away[index].start()
    for copy in away:
        copy.wait()


def place_results(plan, arrays, finals, small):
    share = EMBED_SIZE // (plan.count_seg * plan.count_tok)
    sds = jax.ShapeDtypeStruct
    anywhere, vmem = pl.BlockSpec(memory_space=pl.ANY), pl.BlockSpec(memory_space=pltpu.VMEM)
    count = len(arrays)
    small_shapes = [(1, finals.shape[1])] * 3 + [(2, share), (2, share), (5, share), (1, share), (1, share)]
    return pl.pallas_call(
        partial(place_kernel, share, count),
        out_shape=[sds(item.shape, item.dtype) for item in arrays]
        + [sds(shape, jnp.float32) for shape in small_shapes],
        in_specs=[anywhere] * count + [vmem] * 2,
        out_specs=[anywhere] * count + [vmem] * len(small_shapes),
        scratch_shapes=[pltpu.VMEM(item.shape, item.dtype) for item in arrays]
        + [pltpu.SemaphoreType.DMA((2, count))],
    )(*arrays, finals, small)


def shards(
    incoming_items,
    upstream_slope,
    timemix_prior_entry,
    featmix_prior_entry,
    opening_dividend,
    opening_divisor,
    opening_power,
    normalize_scales,
    normalize_shifts,
    shift_blends,
    logarithmic_fading_speed,
    present_reward,
    *weights,
):
    plan = Plan(lax.axis_size("seg"), lax.axis_size("tok"))
    got = layer(
        plan,
        LayerIn(
            incoming_items[0],
            upstream_slope[0],
            timemix_prior_entry,
            featmix_prior_entry,
            opening_dividend,
            opening_divisor,
            opening_power,
            normalize_scales,
            normalize_shifts,
            shift_blends,
            logarithmic_fading_speed[None],
            present_reward[None],
            *weights,
        ),
        incoming_items.shape[1],
    )
    sums = got[2:9]
    if not plan.tok_here:
        sums = [lax.psum_scatter(item, "tok", scatter_dimension=0, tiled=True) for item in sums]
    placed = place_results(
        plan, [got.layer_out, got.token_grad, *sums], got.final, got.small
    )
    layer_out, token_grad, fvalue, frecept, fkey, aout, arecept, avalue, akey = placed[:9]
    numer, denom, top, gains, biases, mixes, decay, bonus = placed[9:]
    return (
        layer_out[None],
        token_grad[None],
        numer,
        denom,
        top,
        gains,
        biases,
        mixes,
        decay[0],
        bonus[0],
        akey,
        avalue,
        arecept,
        aout,
        fkey,
        fvalue,
        frecept,
    )


def solution(mesh):
    tokens, channels, whole = P("seg", "tok", None), P("seg", "tok"), P()
    spread, rows = P(None, ("seg", "tok")), P(("seg", "tok"), None)
    return jax.shard_map(
        shards,
        mesh=mesh,
        in_specs=(tokens,) * 2 + (P("seg", None),) * 2 + (channels,) * 3 + (whole,) * 12,
        out_specs=(tokens,) * 2
        + (channels,) * 3
        + (spread,) * 3
        + (P(("seg", "tok")),) * 2
        + (rows,) * 7,
        check_vma=False,
    )
```

```python
import copy
from functools import partial
from typing import Any, NamedTuple

import jax
import jax.numpy as jnp
from jax import lax
from jax.experimental import pallas as pl
from jax.experimental.pallas import tpu as pltpu
from jax.sharding import PartitionSpec as P

EMBED_SIZE = 1024
FF = 4096
VMEM_BYTES = 63 << 20
MESH = pl.DeviceIdType.MESH
FAR_FIRST = {0: (0,), 3: (1,), 5: (0,), 7: (0,), 10: (1,)}


class Plan:
    def __init__(self, count_seg, count_tok):
        self.count_seg, self.count_tok = count_seg, count_tok
        self.bits = count_seg.bit_length() - 1
        self.tok_bits = count_tok.bit_length() - 1
        self.seg_rows = EMBED_SIZE // count_seg
        self.seg_rows_ff = FF // count_seg
        self.low_bits = max(0, (128 // self.seg_rows).bit_length() - 1)
        self.pair = self.low_bits
        self.rest = [b for b in range(self.bits) if b != self.pair]
        self.orders = (self.rest, self.rest[::-1])
        self.stages = len(self.rest)
        self.slots = 1 << self.stages
        self.rows = self.seg_rows // count_tok
        self.rows_ff = self.seg_rows_ff // count_tok
        self.tok_here = self.rows % 16 == 0 and count_tok == 1 << self.tok_bits

    def recv_offset(self, stage):
        return self.slots - (self.slots >> stage)

    def slot(self, order, relative):
        total = 0
        for place, bit in enumerate(order):
            total = total + relative[bit] * (1 << (self.stages - 1 - place))
        return total


def bit_of(value, bit):
    return lax.rem(lax.div(value, 1 << bit), 2)


def flip(value, bit):
    return value + (1 - 2 * bit_of(value, bit)) * (1 << bit)


def seg_block(plan, seg, relative):
    total = bit_of(seg, plan.pair) * (1 << plan.pair)
    for bit, rel in relative.items():
        own = bit_of(seg, bit)
        total = total + (own + rel - 2 * own * rel) * (1 << bit)
    return total


def combos(bits):
    for index in range(1 << len(bits)):
        yield {bit: (index >> place) & 1 for place, bit in enumerate(bits)}


def greet(plan, seg, tok):
    barrier = pltpu.get_barrier_semaphore()
    for bit in range(plan.bits):
        pl.semaphore_signal(
            barrier, inc=1, device_id={"seg": flip(seg, bit)}, device_id_type=MESH
        )
    for step in range(1, plan.count_tok):
        pl.semaphore_signal(
            barrier,
            inc=1,
            device_id={"tok": lax.rem(tok + step, plan.count_tok)},
            device_id_type=MESH,
        )

    def wait():
        pl.semaphore_wait(barrier, plan.bits + plan.count_tok - 1)

    return wait


class Copies:
    def __init__(self, local_sems, send_sems, recv_sems):
        self.local_sems, self.send_sems, self.recv_sems = local_sems, send_sems, recv_sems
        self.locals, self.remotes, self.open = 0, 0, []

    def local(self, source, target):
        copy = pltpu.make_async_copy(source, target, self.local_sems.at[self.locals])
        self.locals += 1
        copy.start()
        self.open.append(copy)
        return copy

    def remote(self, source, target, device):
        copy = pltpu.make_async_remote_copy(
            src_ref=source,
            dst_ref=target,
            send_sem=self.send_sems.at[self.remotes],
            recv_sem=self.recv_sems.at[self.remotes],
            device_id=device,
            device_id_type=MESH,
        )
        self.remotes += 1
        copy.start()
        self.open.append(copy)
        return copy

    def wait(self, *copies):
        for copy in copies:
            copy.wait()
            self.open = [item for item in self.open if item is not copy]

    def drain(self):
        self.wait(*list(self.open))


def rows16(index):
    return pl.ds(pl.multiple_of(index * 16, 16), 16)


def rows8(index):
    return pl.ds(pl.multiple_of(index * 8, 8), 8)


LANES = EMBED_SIZE // 128


def put_rows(staged, place, value):
    for block in range(LANES):
        staged[block, place] = value[:, 128 * block : 128 * block + 128]


def get_rows(staged, place):
    return jnp.concatenate([staged[block, place] for block in range(LANES)], axis=1)


def low(value):
    return value.astype(jnp.bfloat16).astype(jnp.float32)


def layer_norm(values, gain_row, bias_row):
    centre = values - jnp.mean(values, axis=-1, keepdims=True)
    spread = jnp.mean(centre * centre, axis=-1, keepdims=True)
    return centre * lax.rsqrt(spread + 1e-05) * gain_row + bias_row


def sweep(count, body, unroll=2):
    def step(index, carry):
        body(index)
        return carry

    lax.fori_loop(0, count, step, 0, unroll=unroll)


def matmul(left, right):
    return jnp.dot(left, right, preferred_element_type=jnp.float32)


def matmul_back(left, right):
    return lax.dot_general(
        left, right, (((1,), (1,)), ((), ())), preferred_element_type=jnp.float32
    )


def merge(state, later, faded):
    numer, denom, top = state
    reduced = top - faded
    peak = jnp.maximum(reduced, later[2])
    old, new = jnp.exp(reduced - peak), jnp.exp(later[2] - peak)
    return (old * numer + new * later[0], old * denom + new * later[1], peak)


def advance(state, key, value, fading):
    numer, denom, top = state
    reduced = top - fading
    peak = jnp.maximum(reduced, key)
    old, new = jnp.exp(reduced - peak), jnp.exp(key - peak)
    return (old * numer + new * value, old * denom + new, peak)


def row_of(state, index):
    return tuple(item[index : index + 1] for item in state)


def stack_rows(states):
    return tuple(jnp.concatenate([state[part] for state in states]) for part in range(len(states[0])))


def first_before(lead_row, last_tile):
    return jnp.concatenate([lead_row, last_tile[0:7]])


def right_of(plan, tok):
    return {"tok": lax.rem(tok + 1, plan.count_tok)}


def left_of(plan, tok):
    return {"tok": lax.rem(tok + plan.count_tok - 1, plan.count_tok)}


class Chunk:
    def __init__(self, ref, lane, wide, unit, share, out, column, far_first=()):
        self.ref, self.lane, self.wide = ref, lane, wide
        self.unit, self.share, self.out, self.column = unit, share, out, column
        self.far_first, self.left, self.flush = far_first, 2, None


class Strand:
    def __init__(self, plan, chunk, half):
        self.chunk, self.half = chunk, half
        self.lanes = pl.ds(chunk.lane + half * chunk.wide, chunk.wide)
        self.place = pl.ds(chunk.column + half * chunk.wide, chunk.wide)
        self.far = [-1 - bit for bit in range(plan.tok_bits)] if plan.tok_here else []
        self.route = list(plan.orders[half])
        self.first, self.slots, self.settled = 0, plan.slots, 0
        self.free, self.after = plan.slots * chunk.unit, None
        self.made, self.due = [], 0.0

    def parts(self, plan):
        if not (self.half in self.chunk.far_first and self.far):
            self.route += self.far
            return [self], None
        made, room = [], (plan.count_tok - 1) * self.chunk.share
        for slot in range(plan.slots):
            part = copy.copy(self)
            part.route, part.first, part.slots = list(self.far), slot, 1
            part.free = self.free + slot * room
            made.append(part)
        self.settled, self.free = plan.tok_bits, self.free + plan.slots * room
        return made, self


class Wire:
    RATE = 86e3
    LAG = 2.5
    BACKLOG = 8.0
    FAR_BACKLOG = 2.0

    def __init__(self, plan, seg, tok, send_sems, recv_sems):
        self.plan, self.seg, self.tok = plan, seg, tok
        self.send_sems, self.recv_sems, self.count = send_sems, recv_sems, 0
        self.clock, self.free = 0.0, {}
        self.waiting, self.flying = [], []

    def load(self, axis, amount):
        ends = []
        for link in range(axis, 0) if axis < 0 else (axis,):
            passing = amount << max(0, -1 - link)
            self.free[link] = max(self.clock, self.free.get(link, 0.0)) + passing / self.RATE
            ends.append(self.free[link])
        return max(ends) + self.LAG

    def fly(self, arrival, action):
        self.flying.append((arrival, action))

    def due(self, far):
        start = max([self.clock] + [self.free.get(link, 0.0) for link in (-2, -1) if far])
        return start + 2.3

    def meet(self, *times):
        self.clock = max(self.clock, *times)

    def open(self, chunk):
        opened = []
        for half in range(2):
            parts, whole = Strand(self.plan, chunk, half).parts(self.plan)
            left = [len(parts)]

            def after(left=left, whole=whole):
                left[0] -= 1
                if not left[0]:
                    self.start(whole)

            for part in parts:
                part.after = after if whole else None
            opened += parts
        return opened

    def offer(self, chunk):
        self.waiting += self.open(chunk)
        self.serve()

    def slot_made(self, opened, relative):
        for strand in opened:
            slot = self.plan.slot(self.plan.orders[strand.half], relative)
            size, unit = strand.slots // 2, strand.chunk.unit
            if strand.after:
                if strand.first == slot:
                    self.start(strand)
            elif slot >= size:
                axis = strand.route[0]
                device = {"seg": flip(self.seg, axis)}
                to = strand.free + (slot - size) * unit
                strand.made.append(self.copy(strand, slot * unit, to, unit, device))
                strand.due = self.load(axis, 4 * strand.chunk.wide * unit)

    def slots_made(self, opened):
        for strand in opened:
            if strand.after:
                continue
            strand.route.pop(0)
            rows = strand.slots // 2 * strand.chunk.unit
            pieces = [(0, rows, strand.free)]
            strand.slots //= 2
            strand.free += rows
            self.fly(strand.due, partial(self.arrive, strand, strand.made, pieces))

    def tick(self, cost):
        self.clock += cost
        self.serve()

    def room(self):
        for strand in self.waiting:
            axis = strand.route[0]
            limit = self.BACKLOG if axis >= 0 else self.FAR_BACKLOG
            if self.free.get(axis, 0.0) - self.clock < limit:
                return strand
        return None

    def serve(self, rest=False):
        while self.flying or self.waiting:
            strand = self.room()
            if strand is not None:
                self.waiting.remove(strand)
                self.start(strand)
                continue
            if not self.flying:
                break
            soonest = min(self.flying, key=lambda item: item[0])
            if soonest[0] > self.clock and not rest:
                break
            self.clock = max(self.clock, soonest[0])
            self.flying.remove(soonest)
            soonest[1]()

    def copy(self, strand, source, target, rows, device):
        index, self.count = self.count, self.count + 1
        made = pltpu.make_async_remote_copy(
            src_ref=strand.chunk.ref.at[pl.ds(source, rows), strand.lanes],
            dst_ref=strand.chunk.ref.at[pl.ds(target, rows), strand.lanes],
            send_sem=self.send_sems.at[index],
            recv_sem=self.recv_sems.at[index],
            device_id=device,
            device_id_type=MESH,
        )
        made.start()
        return made

    def start(self, strand):
        plan, chunk, base = self.plan, strand.chunk, strand.free
        axis, copies, pieces = strand.route.pop(0), [], []
        unit, share = chunk.unit, chunk.share
        kept = self.tok
        if axis < 0:
            bit = -1 - axis
            device = {"tok": flip(self.tok, bit)}
            sent, strand.settled = flip(self.tok, bit), bit + 1
        else:
            device, sent = {"seg": flip(self.seg, axis)}, self.tok
            strand.slots //= 2
        first = strand.slots if axis >= 0 else strand.first
        if strand.settled:
            step = 1 << strand.settled
            parts = plan.count_tok // step
            for slot in range(strand.slots):
                for part in range(parts):
                    there = lax.rem(sent, step) + step * part
                    source = pl.multiple_of((first + slot) * unit + there * share, share)
                    here = lax.rem(kept, step) + step * part
                    near = pl.multiple_of((strand.first + slot) * unit + here * share, share)
                    to = base + (slot * parts + part) * share
                    copies.append(self.copy(strand, source, to, share, device))
                    pieces.append((near, share, to))
            rows = strand.slots * parts * share
        else:
            rows = strand.slots * unit
            copies.append(self.copy(strand, rows, base, rows, device))
            pieces.append((0, rows, base))
        strand.free += rows
        arrival = self.load(axis, 4 * chunk.wide * rows)
        self.fly(arrival, lambda: self.arrive(strand, copies, pieces))

    def arrive(self, strand, copies, pieces):
        chunk = strand.chunk
        for copy in copies:
            copy.wait()
        for near, rows, came in pieces:
            block = min(rows, 32768 // chunk.wide)

            def add(index):
                offset = index * block
                place = pl.ds(pl.multiple_of(near + offset, 16), block)
                there = pl.ds(pl.multiple_of(came + offset, 16), block)
                total = chunk.ref[place, strand.lanes].astype(jnp.float32)
                total = total + chunk.ref[there, strand.lanes].astype(jnp.float32)
                if strand.route or strand.after:
                    chunk.ref[place, strand.lanes] = total.astype(jnp.bfloat16)
                else:
                    chunk.out[pl.ds(pl.multiple_of(offset, 8), block), strand.place] = total

            sweep(rows // block, add, 1)
            self.clock += 1.2e-6 * rows * chunk.wide + 0.05
        if strand.route:
            self.start(strand)
        elif strand.after:
            strand.after()
        else:
            chunk.left -= 1
            if not chunk.left:
                chunk.flush()


def outer_chunk(plan, seg, chunk, left, left_lane, right, right_lane, only=None):
    nsub = 1 << plan.low_bits
    high = [b for b in plan.rest if b >= plan.low_bits]
    columns = pl.ds(right_lane, 2 * chunk.wide)
    tall = chunk.unit == plan.seg_rows_ff
    for relative in only or combos(high):
        group = lax.div(lax.div(seg_block(plan, seg, relative), nsub), 2)
        span = chunk.unit if tall else chunk.unit * nsub
        for piece in range(nsub if tall else 1):
            index = group * nsub + piece if tall else group
            taken = left[:, pl.ds(pl.multiple_of(left_lane + index * span, 128), span)]
            result = lax.dot_general(
                taken,
                right[:, columns],
                (((0,), (0,)), ((), ())),
                preferred_element_type=jnp.float32,
            ).astype(jnp.bfloat16)
            for part in (piece,) if tall else range(nsub):
                full = dict(relative)
                for bit in range(plan.low_bits):
                    mine, want = bit_of(seg, bit), (part >> bit) & 1
                    full[bit] = mine + want - 2 * mine * want
                rows = result if tall else result[part * chunk.unit : (part + 1) * chunk.unit]
                for half in range(2):
                    slot = plan.slot(plan.orders[half], full)
                    start = slot * chunk.unit
                    if not isinstance(start, int):
                        start = pl.multiple_of(start, chunk.unit)
                    lanes = pl.ds(chunk.lane + half * chunk.wide, chunk.wide)
                    chunk.ref[pl.ds(start, chunk.unit), lanes] = rows[
                        :, half * chunk.wide : (half + 1) * chunk.wide
                    ]


def fold(value):
    return value[0:8] + value[8:16]


def total_rows(value):
    return jnp.sum(value, axis=0, keepdims=True)


def norm_back(values, slope, gain_row):
    centre = values - jnp.mean(values, axis=-1, keepdims=True)
    rate = lax.rsqrt(jnp.mean(centre * centre, axis=-1, keepdims=True) + 1e-05)
    scaled = centre * rate
    inner = slope * gain_row
    mean_inner = jnp.mean(inner, axis=-1, keepdims=True)
    mean_along = jnp.mean(inner * scaled, axis=-1, keepdims=True)
    return rate * (inner - mean_inner - scaled * mean_along), slope * scaled


class LayerIn(NamedTuple):
    x: Any
    up: Any
    prior_one: Any
    prior_two: Any
    open_num: Any
    open_den: Any
    open_top: Any
    scales: Any
    shifts: Any
    blends: Any
    speed: Any
    reward: Any
    wk: Any
    wv: Any
    wr: Any
    wo: Any
    wl: Any
    wp: Any
    wa: Any


class LayerOut(NamedTuple):
    layer_out: Any
    token_grad: Any
    fvalue: Any
    frecept: Any
    fkey: Any
    aout: Any
    arecept: Any
    avalue: Any
    akey: Any
    final: Any
    small: Any
    cat_weighted: Any
    cat_recept_mix: Any
    cat_value_mix: Any
    cat_key_mix: Any
    out_kf: Any
    out_vf: Any
    out_recept: Any
    out_xp: Any
    out_nf: Any


class LayerHeld(NamedTuple):
    vl: Any
    vp: Any
    va: Any
    early: Any
    tall: Any
    csq: Any
    cfr: Any
    cfk: Any
    gc: Any
    gg: Any
    gh: Any
    sq: Any
    f0: Any
    f1: Any
    f2: Any
    f3: Any
    f4: Any
    f5: Any
    staged: Any
    held_fvalue: Any
    held_frecept: Any
    held_fkey: Any
    held_aout: Any
    held_arecept: Any
    held_avalue: Any
    held_akey: Any
    row_out: Any
    row_in: Any
    state_out: Any
    state_in: Any
    back_out: Any
    back_in: Any
    entry: Any
    small_in: Any
    wire_send: Any
    wire_recv: Any
    local_sems: Any
    send_sems: Any
    recv_sems: Any
    ready: Any


def layer_kernel(plan, *refs):
    count_in, count_out = len(LayerIn._fields), len(LayerOut._fields)
    a = LayerIn(*refs[:count_in])
    o = LayerOut(*refs[count_in : count_in + count_out])
    h = LayerHeld(*refs[count_in + count_out :])
    seg, tok = lax.axis_index("seg"), lax.axis_index("tok")
    tokens = h.sq.shape[1]
    steps, pairs = tokens // 8, tokens // 16
    every = lambda i: pl.ds(i, 8, stride=steps)
    shifted16 = lambda i: pl.ds(pl.multiple_of(16 * i + 8, 8), 16)
    own_rows, pair_rows = pl.ds(0, tokens), pl.ds(tokens, tokens)
    partner = {"seg": flip(seg, plan.pair)}
    mine = bit_of(seg, plan.pair)
    last_tok = plan.count_tok - 1
    half = EMBED_SIZE // 2
    copies = Copies(h.local_sems, h.send_sems, h.recv_sems)
    load = copies.local
    tile_zero = jnp.zeros((8, EMBED_SIZE), jnp.float32)
    blend = lambda j: a.blends[j : j + 1]
    others = lambda: [
        {"tok": lax.rem(tok + step, plan.count_tok)} for step in range(1, plan.count_tok)
    ]

    xb, ub = h.gh.at[2, own_rows], h.gh.at[3, own_rows]
    at_x = load(a.x, xb)
    at_wk, at_wv = load(a.wk, h.vp.at[0]), load(a.wv, h.vp.at[1])
    at_wr, at_wo = load(a.wr, h.vp.at[2]), load(a.wo, h.vp.at[3])
    at_up = load(a.up, ub)
    at_va = load(a.wa, h.va)
    at_vl = [load(a.wl.at[:, pl.ds(1024 * j, 1024)], h.vl.at[j]) for j in range(4)]
    all_here = greet(plan, seg, tok)
    wire = Wire(plan, seg, tok, h.wire_send, h.wire_recv)

    def share(source, target, wide, at=0):
        count = source.shape[1] // (2 * wide)
        made = []
        for pick in range(count):
            own = pl.ds(pl.multiple_of((2 * pick + mine) * wide, wide), wide)
            other = pl.ds(pl.multiple_of((2 * pick + 1 - mine) * wide, wide), wide)
            place = pl.ds(pl.multiple_of((at + pick) * wide, wide), wide)
            made.append(load(source.at[:, own], target.at[own_rows, place]))
            made.append(copies.remote(source.at[:, other], target.at[pair_rows, place], partner))
        return made

    def to_pair(ref):
        return copies.remote(ref.at[own_rows], ref.at[pair_rows], partner), wire.due(False)

    def meet(*pairs):
        for copy, due in pairs:
            wire.meet(due)
            copies.wait(copy)

    wide = max(128, plan.seg_rows)

    nf, xp = h.f0, h.f1
    copies.wait(at_x)

    def widen(i):
        put_rows(h.staged, rows16(i), xb[rows16(i)].astype(jnp.float32))

    sweep(pairs, widen, 4)
    gain, bias = a.scales[0:1], a.shifts[0:1]

    def norm_one(i):
        tile = get_rows(h.staged, every(i))
        xp[rows8(i)] = tile
        nf[rows8(i + 1)] = low(layer_norm(tile, gain, bias))

    norm_one(steps - 1)
    h.row_out[0] = nf[pl.ds(8 * steps, 8)]
    all_here()
    row = copies.remote(h.row_out.at[0], h.row_in.at[0], right_of(plan, tok))
    sweep(steps, norm_one, 8)

    def mix_one(places):
        def step(i):
            before, normed = nf[rows16(i)], nf[shifted16(i)]
            for place in places:
                weight = blend(place)
                mixed = normed * weight + before * (1.0 - weight)
                h.sq[place, rows16(i)] = mixed.astype(jnp.bfloat16)

        return step

    sweep(pairs - 1, lambda i: mix_one((0, 1))(i + 1), 2)
    copies.wait(row)
    lead = jnp.where(tok == 0, a.prior_one[...].astype(jnp.float32), h.row_in[0, 7:8])
    nf[0:8] = first_before(lead, nf[pl.ds(8 * steps, 8)])
    mix_one((0, 1))(0)
    mixes = share(h.sq.at[0], o.cat_key_mix, wide) + share(h.sq.at[1], o.cat_value_mix, wide)
    at_nf, at_xp = load(nf, o.out_nf), load(xp.at[own_rows], o.out_xp)
    kf, vf, recept = h.f2, h.f3, h.f4
    copies.wait(at_wk)
    kf[own_rows] = low(matmul(h.sq[0], h.vp[0]))
    copies.wait(at_wv)
    vf[own_rows] = low(matmul(h.sq[1], h.vp[1]))
    at_kf, at_vf = load(kf.at[own_rows], o.out_kf), load(vf.at[own_rows], o.out_vf)

    fading_row = jnp.exp(a.speed[...])
    fading = jnp.broadcast_to(fading_row, (8, EMBED_SIZE))
    reward = jnp.broadcast_to(a.reward[...], (8, EMBED_SIZE))

    def alone(i, state):
        return advance(state, kf[rows8(i)], vf[rows8(i)], fading)

    stretches = lax.fori_loop(0, steps, alone, (tile_zero, tile_zero, tile_zero - 1e30), unroll=2)
    stretch_fade = fading_row * steps
    total = row_of(stretches, 0)
    for j in range(1, 8):
        total = merge(total, row_of(stretches, j), stretch_fade)
    portion = EMBED_SIZE // plan.count_tok
    lanes = pl.ds(pl.multiple_of(tok * portion, portion), portion)
    h.state_out[...] = tile_zero
    for part, opening in enumerate((a.open_num, a.open_den, a.open_top)):
        h.state_out[part : part + 1] = total[part]
        h.state_out[3 + part : 4 + part, lanes] = opening[...]
    sent = [copies.remote(h.state_out, h.state_in.at[tok], device) for device in others()]
    h.state_in[tok] = h.state_out[...]
    sweep(pairs, mix_one((2,)), 2)
    mixes += share(h.sq.at[2], o.cat_recept_mix, wide)
    copies.wait(at_wr)
    recept[own_rows] = jax.nn.sigmoid(matmul(h.sq[2], h.vp[2]))
    at_recept = load(recept.at[own_rows], o.out_recept)
    upf = h.f0
    copies.wait(at_up, at_nf)

    def widen_up(i):
        put_rows(h.staged, rows16(i), ub[rows16(i)].astype(jnp.float32))

    sweep(pairs, widen_up, 4)

    copies.wait(*sent)
    state = tuple(
        sum(h.state_in[z, 3 + part : 4 + part] for z in range(plan.count_tok)) for part in range(3)
    )
    entry = state
    for z in range(plan.count_tok):
        entry = tuple(jnp.where(tok == z, new, old) for new, old in zip(state, entry))
        later = tuple(h.state_in[z, part : part + 1] for part in range(3))
        state = merge(state, later, fading_row * tokens)
    for part in range(3):
        h.state_out[part : part + 1] = state[part]
    o.final[...] = h.state_out[:, lanes]
    entries = [entry]
    for j in range(7):
        entries.append(merge(entries[-1], row_of(stretches, j), stretch_fade))
    entries = stack_rows(entries)
    for part in range(3):
        h.entry[8 * part : 8 * part + 8] = entries[part]
    copies.wait(at_kf)
    mixed = h.f2

    def emit(state, i):
        key, value = kf[rows8(i)], vf[rows8(i)]
        present = reward + key
        peak = jnp.maximum(state[2], present)
        old, new = jnp.exp(state[2] - peak), jnp.exp(present - peak)
        result = (old * state[0] + new * value) / (old * state[1] + new)
        return advance(state, key, value, fading), low(result)

    def recur(i, state):
        state, one = emit(state, 2 * i)
        state, two = emit(state, 2 * i + 1)
        both_rows = jnp.concatenate([one, two])
        mixed[rows16(i)] = both_rows
        h.sq[3, rows16(i)] = (recept[rows16(i)] * both_rows).astype(jnp.bfloat16)
        return state

    lax.fori_loop(0, pairs, recur, entries, unroll=2)
    mixes += share(h.sq.at[3], o.cat_weighted, wide)
    copies.wait(at_wo, at_xp)
    middle = h.f1
    middle[own_rows] = xp[own_rows] + matmul(h.sq[3], h.vp[3])
    at_vp = [load(a.wp.at[pl.ds(1024 * j, 1024)], h.vp.at[j]) for j in range(4)]

    gain_two, bias_two = a.scales[1:2], a.shifts[1:2]
    nf2 = h.f5

    def norm_two(i):
        nf2[rows8(i + 1)] = low(layer_norm(middle[rows8(i)], gain_two, bias_two))

    norm_two(steps - 1)
    h.row_out[1] = nf2[pl.ds(8 * steps, 8)]
    row = copies.remote(h.row_out.at[1], h.row_in.at[1], right_of(plan, tok))
    sweep(steps, norm_two, 8)
    key_two, recept_two = h.gh.at[0, own_rows], h.gh.at[1, own_rows]

    def mix_two(i):
        before, normed = nf2[rows16(i)], nf2[shifted16(i)]
        for place, target in ((3, key_two), (4, recept_two)):
            weight = blend(place)
            target[rows16(i)] = (normed * weight + before * (1.0 - weight)).astype(jnp.bfloat16)

    sweep(pairs - 1, lambda i: mix_two(i + 1), 2)
    copies.wait(row)
    lead = jnp.where(tok == 0, a.prior_two[...].astype(jnp.float32), h.row_in[1, 7:8])
    nf2[0:8] = first_before(lead, nf2[pl.ds(8 * steps, 8)])
    mix_two(0)
    twos = share(key_two, h.cfk, wide) + share(recept_two, h.cfr, wide)
    gate, carried = h.f3, h.f4
    copies.wait(at_va, at_vf)
    gate[own_rows] = jax.nn.sigmoid(matmul(recept_two[...], h.va[...]))

    def carried_slope(i):
        up = jnp.concatenate([get_rows(h.staged, every(2 * i)), get_rows(h.staged, every(2 * i + 1))])
        upf[rows16(i)] = up
        h.gc[rows16(i)] = (up * gate[rows16(i)]).astype(jnp.bfloat16)

    sweep(pairs, carried_slope, 2)
    pair_gc = to_pair(h.gc)
    copies.wait(*mixes)
    share_rows = plan.rows if plan.tok_here else 0
    share_ff = plan.rows_ff if plan.tok_here else 0
    tall = [
        Chunk(h.tall, 256 * j, 128, plan.seg_rows_ff, share_ff, h.held_fvalue, 256 * j, FAR_FIRST.get(j, ()))
        for j in range(4)
    ]
    flat = lambda ref, out, column, far_first: Chunk(
        ref, 0, half, plan.seg_rows, share_rows, out, column, far_first
    )
    frecept = flat(h.early.at[0], h.held_frecept, 0, FAR_FIRST.get(4, ()))
    fkey = [flat(h.early.at[1 + j], h.held_fkey, 1024 * j, FAR_FIRST.get(5 + j, ())) for j in range(4)]
    late = [
        flat(h.vl.at[j], out, 0, FAR_FIRST.get(9 + j, ()))
        for j, out in enumerate((h.held_aout, h.held_arecept, h.held_avalue, h.held_akey))
    ]

    def flush_to(chunk, target):
        place = pl.ds(chunk.column, 2 * chunk.wide)
        chunk.flush = lambda: load(chunk.out.at[:, place], target.at[:, place])

    targets = [o.fvalue] * 4 + [o.frecept] + [o.fkey] * 4 + [o.aout, o.arecept, o.avalue, o.akey]
    for chunk, target in zip(tall + [frecept] + fkey + late, targets):
        flush_to(chunk, target)

    def offer(chunk, left, left_lane, right, right_lane):
        outer_chunk(plan, seg, chunk, left, left_lane, right, right_lane)
        wire.clock += 0.95
        wire.offer(chunk)

    nsub = 1 << plan.low_bits
    high = [bit for bit in plan.rest if bit >= plan.low_bits]
    blocks = sorted(combos(high), key=lambda relative: -sum(relative.values()))
    opened = [wire.open(chunk) for chunk in tall]
    copies.wait(*at_vl)

    def hidden_block(relative):
        block = lax.div(lax.div(seg_block(plan, seg, relative), nsub), 2)
        for side in range(2):
            columns = pl.ds(half * side, half)
            hidden = jnp.maximum(matmul(key_two[...], h.vl[block, :, columns]), 0.0)
            h.sq[block, :, columns] = (hidden * hidden).astype(jnp.bfloat16)
        return share(h.sq.at[block], h.csq, 4 * wide, block)

    def payload_slot(relative, squares):
        copies.wait(*squares)
        for j in (1, 2, 3, 0):
            outer_chunk(plan, seg, tall[j], h.csq, 0, h.gc, 256 * j, [relative])
            wire.clock += 0.24
            if not plan.low_bits:
                wire.slot_made(opened[j], relative)

    squares = [hidden_block(blocks[0])]
    for place in range(1, len(blocks)):
        squares.append(hidden_block(blocks[place]))
        if place == 1:
            copies.wait(pair_gc[0])
            wire.clock = 0.0
        else:
            wire.clock += 1.1
        payload_slot(blocks[place - 1], squares[place - 1])
    copies.wait(at_recept, at_vp[0])
    carried[own_rows] = matmul(h.sq[0], h.vp[0])
    wire.clock += 1.0
    payload_slot(blocks[-1], squares[-1])
    for chunk, strands in zip(tall, opened):
        if plan.low_bits:
            wire.waiting += strands
        else:
            wire.slots_made(strands)
    wire.serve()
    cats = [
        load(cat, h.csq.at[:, pl.ds(half * j, half)])
        for j, cat in enumerate(
            (o.cat_weighted, o.cat_recept_mix, o.cat_value_mix, o.cat_key_mix)
        )
    ]
    for j in range(1, 4):
        copies.wait(at_vp[j])
        carried[own_rows] += matmul(h.sq[j], h.vp[j])
        wire.tick(1.0)

    def close(i):
        gates, sums = gate[rows16(i)], carried[rows16(i)]
        gated = gates * sums
        result = middle[rows16(i)] + gated
        h.gg[rows16(i)] = (upf[rows16(i)] * gated * (1.0 - gates)).astype(jnp.bfloat16)
        put_rows(h.staged, every(2 * i), result[0:8])
        put_rows(h.staged, every(2 * i + 1), result[8:16])

    sweep(pairs, close, 2)
    pair_gg = to_pair(h.gg)
    narrowed = h.gh.at[3, own_rows]

    def narrow(i):
        narrowed[rows16(i)] = get_rows(h.staged, rows16(i)).astype(jnp.bfloat16)

    sweep(pairs, narrow, 4)
    at_out = load(narrowed, o.layer_out)
    wire.tick(1.5)

    def unmix(grads, weights, kept, row_place):
        def across(place):
            slopes = [grad[place] for grad in grads]
            total = slopes[0] * (1.0 - weights[0])
            for item, weight in zip(slopes[1:], weights[1:]):
                total = total + item * (1.0 - weight)
            return slopes, low(total)

        first = across(pl.ds(0, 8))[1]
        h.row_out[row_place] = first
        row = copies.remote(h.row_out.at[row_place], h.row_in.at[row_place], left_of(plan, tok))
        due = wire.due(True)

        def step(i, sums):
            place = rows16(i)
            slopes, moved = across(place)
            difference = kept[shifted16(i)] - kept[place]
            direct = slopes[0] * weights[0]
            for item, weight in zip(slopes[1:], weights[1:]):
                direct = direct + item * weight
            grads[0][place] = direct
            grads[-1][place] = moved
            return tuple(fold(item * difference) + old for item, old in zip(slopes, sums))

        def finish():
            sums = lax.fori_loop(0, pairs, step, (tile_zero,) * len(grads), unroll=2)
            wire.tick(1.5)
            wire.meet(due)
            copies.wait(row)
            end = jnp.where(tok == last_tok, 0.0, h.row_in[row_place, 0:1])
            grads[-1][pl.ds(tokens, 8)] = jnp.concatenate([first[1:8], end])
            return [total_rows(item) for item in sums]

        return finish

    copies.wait(*twos)
    sent = []
    for j in range(4):
        h.f3[own_rows] = matmul_back(h.gc[own_rows], h.vp[j])
        if j == 3:
            copies.wait(at_out)

        def hidden_slope(i):
            rate = 2.0 * jnp.sqrt(h.sq[j, rows16(i)].astype(jnp.float32))
            h.gh[j, rows16(i)] = (h.f3[rows16(i)] * rate).astype(jnp.bfloat16)

        sweep(pairs, hidden_slope, 2)
        sent.append(to_pair(h.gh.at[j]))
        wire.tick(1.3)
    at_wo = load(a.wo, h.vp.at[3])
    at_wk, at_wv = load(a.wk, h.vp.at[0]), load(a.wv, h.vp.at[1])
    at_wr = load(a.wr, h.vp.at[2])
    for j in range(4):
        part = matmul_back(h.gh[j, own_rows], h.vl[j])
        h.f3[own_rows] = part if j == 0 else h.f3[own_rows] + part
        wire.tick(1.1)
    h.f4[own_rows] = matmul_back(h.gg[own_rows], h.va[...])
    wire.tick(1.0)
    finish_two = unmix((h.f3, h.f4), (blend(3), blend(4)), nf2, 2)
    meet(pair_gg)
    offer(frecept, h.cfr, 0, h.gg, 0)
    for j in range(4):
        meet(sent[j])
        offer(fkey[j], h.cfk, 0, h.gh.at[j], 0)

    neighbours = [{"seg": flip(seg, bit)} for bit in range(plan.bits)] + others()
    for device in neighbours:
        pl.semaphore_signal(h.ready, inc=1, device_id=device, device_id_type=MESH)

    def norm_pull(direct, moved, values, gain_row, emit):
        def step(i, sums):
            place = rows16(i)
            slope = direct[place] + moved[shifted16(i)]
            back, along = norm_back(values[place], slope, gain_row)
            emit(i, back)
            return fold(along) + sums[0], fold(slope) + sums[1]

        sums = lax.fori_loop(0, pairs, step, (tile_zero, tile_zero), unroll=4)
        return [total_rows(item) for item in sums]

    sums_two = finish_two()
    recept = h.f5
    at_recept = load(o.out_recept, recept.at[own_rows])
    wire.tick(0.3)
    total_slope = h.f0

    def middle_slope(i, back):
        total = upf[rows16(i)] + back
        total_slope[rows16(i)] = total
        h.gh[0, rows16(i)] = total.astype(jnp.bfloat16)

    gain_sum_two, bias_sum_two = norm_pull(h.f3, h.f4, middle, gain_two, middle_slope)
    key_ref, value_ref, slope_ref, top_ref, numer_ref = h.f1, h.f4, h.f3, h.f2, h.f5
    at_k = load(o.out_kf, key_ref.at[own_rows])
    at_v = load(o.out_vf, value_ref.at[own_rows])
    pl.semaphore_wait(h.ready, len(neighbours))
    pair_out = to_pair(h.gh.at[0])
    wire.tick(2.5)
    copies.wait(at_wo)
    slope_ref[own_rows] = matmul_back(h.gh[0, own_rows], h.vp[3])
    wire.tick(1.0)
    copies.wait(at_recept)

    def wkv_slope(i):
        place = rows16(i)
        slope, gates = slope_ref[place], recept[place]
        gated = slope * gates
        slope_ref[place] = low(gated)
        h.gh[1, place] = (gated * mixed[place] * (1.0 - gates)).astype(jnp.bfloat16)

    sweep(pairs, wkv_slope, 2)
    pair_recept = to_pair(h.gh.at[1])
    wire.tick(1.0)

    copies.wait(at_k, at_v)

    def terms(state, key, value, slope):
        numer, denom, top = state
        present = reward + key
        peak = jnp.maximum(top, present)
        old, new = jnp.exp(top - peak), jnp.exp(present - peak)
        inverse = 1.0 / (old * denom + new)
        result = (old * numer + new * value) * inverse
        reduced = top - fading
        next_top = jnp.maximum(reduced, key)
        keep, put = jnp.exp(reduced - next_top), jnp.exp(key - next_top)
        scaled = slope * inverse
        return old * scaled, new * scaled, result, keep, put, next_top

    def onward(i, carry):
        numer, denom, top, alpha, beta, product = carry
        place = rows8(i)
        key, value = key_ref[place], value_ref[place]
        top_ref[place] = top
        numer_ref[place] = numer
        put_rows(h.staged, place, denom)
        into, _, result, keep, put, next_top = terms(
            (numer, denom, top), key, value, slope_ref[place]
        )
        alpha = alpha + product * into
        beta = beta - product * into * result
        product = product * keep
        return keep * numer + put * value, keep * denom + put, next_top, alpha, beta, product

    entry = tuple(h.entry[8 * part : 8 * part + 8] for part in range(3))
    swept = lax.fori_loop(
        0, steps, onward, entry + (tile_zero, tile_zero, tile_zero + 1.0), unroll=2
    )
    stretches = swept[3:]

    def pull_back(later, stretch):
        return (stretch[0] + stretch[2] * later[0], stretch[1] + stretch[2] * later[1])

    nothing = (jnp.zeros((1, EMBED_SIZE), jnp.float32),) * 2
    total, product = nothing, jnp.ones((1, EMBED_SIZE), jnp.float32)
    for j in range(7, -1, -1):
        total = pull_back(total, row_of(stretches, j))
        product = product * stretches[2][j : j + 1]
    h.back_out[...] = tile_zero
    for part, item in enumerate(total + (product,)):
        h.back_out[part : part + 1] = item
    wire.tick(4.0)
    sent = [copies.remote(h.back_out, h.back_in.at[tok], device) for device in others()]
    due = wire.due(True)
    h.back_in[tok] = h.back_out[...]
    meet(pair_out)
    copies.wait(cats[0])
    offer(late[0], h.csq, 0, h.gh.at[0], 0)
    meet(pair_recept)
    copies.wait(cats[1])
    offer(late[1], h.csq, half, h.gh.at[1], 0)
    wire.meet(due)
    copies.wait(*sent)
    later, entering = nothing, nothing
    for z in range(last_tok, -1, -1):
        entering = tuple(jnp.where(tok == z, new, old) for new, old in zip(later, entering))
        later = pull_back(later, tuple(h.back_in[z, part : part + 1] for part in range(3)))
    entries = [entering]
    for j in range(7, 0, -1):
        entries.insert(0, pull_back(entries[0], row_of(stretches, j)))
    entries = stack_rows(entries)

    def back(i, carry):
        alpha, beta, fade_sum, reward_sum = carry
        place = rows8(i)
        key, value, slope = key_ref[place], value_ref[place], slope_ref[place]
        numer, denom, top = numer_ref[place], get_rows(h.staged, place), top_ref[place]
        into, now, result, keep, put, _ = terms((numer, denom, top), key, value, slope)
        reward_term = now * (value - result)
        key_slope = reward_term + put * (alpha * value + beta)
        value_slope = now + put * alpha
        fade_sum = fade_sum - keep * (alpha * numer + beta * denom)
        alpha, beta = keep * alpha + into, keep * beta - into * result
        return (alpha, beta, fade_sum, reward_sum + reward_term), key_slope, value_slope

    def backward_pair(index, carry):
        i = pairs - 1 - index
        carry, key_two, value_two = back(2 * i + 1, carry)
        carry, key_one, value_one = back(2 * i, carry)
        h.gh[2, rows16(i)] = jnp.concatenate([value_one, value_two]).astype(jnp.bfloat16)
        h.gh[3, rows16(i)] = jnp.concatenate([key_one, key_two]).astype(jnp.bfloat16)
        return carry

    _, _, fade_sum, reward_sum = lax.fori_loop(
        0, pairs, backward_pair, entries + (tile_zero, tile_zero)
    )
    decay = total_rows(fade_sum) * fading_row
    bonus = total_rows(reward_sum)
    pair_value, pair_key = to_pair(h.gh.at[2]), to_pair(h.gh.at[3])
    nf, xp = h.f4, h.f5
    at_nf = load(o.out_nf, nf)
    at_xp = load(o.out_xp, xp.at[own_rows])
    wire.tick(5.5)
    copies.wait(at_wk)
    h.f2[own_rows] = matmul_back(h.gh[3, own_rows], h.vp[0])
    wire.tick(1.0)
    copies.wait(at_wv, at_wr)
    h.f1[own_rows] = matmul_back(h.gh[2, own_rows], h.vp[1])
    wire.tick(1.0)
    h.f3[own_rows] = matmul_back(h.gh[1, own_rows], h.vp[2])
    wire.tick(1.0)
    copies.wait(at_nf)
    finish_one = unmix((h.f2, h.f1, h.f3), (blend(0), blend(1), blend(2)), nf, 3)
    meet(pair_value)
    copies.wait(cats[2])
    offer(late[2], h.csq, 2 * half, h.gh.at[2], 0)
    meet(pair_key)
    copies.wait(cats[3])
    offer(late[3], h.csq, 3 * half, h.gh.at[3], 0)
    sums_one = finish_one()
    wire.tick(0.5)
    copies.wait(at_xp)

    def input_slope(i, back):
        total = total_slope[rows16(i)] + back
        put_rows(h.staged, every(2 * i), total[0:8])
        put_rows(h.staged, every(2 * i + 1), total[8:16])

    gain_sum_one, bias_sum_one = norm_pull(h.f2, h.f3, xp, a.scales[0:1], input_slope)
    wire.tick(2.5)

    small_rows = [gain_sum_one, gain_sum_two, bias_sum_one, bias_sum_two]
    small_rows += sums_one + sums_two + [decay, bonus]
    o.small[...] = jnp.concatenate(
        small_rows + [jnp.zeros((16 - len(small_rows), EMBED_SIZE), jnp.float32)]
    )

    def small_stage(bit):
        copy = copies.remote(o.small, h.small_in.at[bit], {"seg": flip(seg, bit)})

        def next_stage():
            copies.wait(copy)
            o.small[...] += h.small_in[bit]
            if bit + 1 < plan.bits:
                small_stage(bit + 1)
            else:
                small_far()

        wire.fly(wire.clock + 4.0, next_stage)

    def small_far():
        base = plan.bits - 1
        sent = [
            copies.remote(o.small, h.small_in.at[base + 1 + step], device)
            for step, device in enumerate(others())
        ]

        def end():
            copies.wait(*sent)
            total = o.small[...]
            for step in range(1, plan.count_tok):
                total = total + h.small_in[base + step]
            o.small[...] = total

        wire.fly(wire.clock + 6.0, end)

    small_stage(0)

    def narrow_slope(i):
        h.sq[0, rows16(i)] = get_rows(h.staged, rows16(i)).astype(jnp.bfloat16)

    sweep(pairs, narrow_slope, 4)
    load(h.sq.at[0], o.token_grad)
    wire.serve(rest=True)
    copies.drain()


def layer(plan, arrays, tokens):
    f32, b16 = jnp.float32, jnp.bfloat16
    half = EMBED_SIZE // 2
    anywhere, vmem = pl.BlockSpec(memory_space=pl.ANY), pl.BlockSpec(memory_space=pltpu.VMEM)
    sds, held = jax.ShapeDtypeStruct, pltpu.VMEM
    far = plan.count_tok - 1
    rows = plan.rows if plan.tok_here else plan.seg_rows
    rows_ff = plan.rows_ff if plan.tok_here else plan.seg_rows_ff
    extra = far if plan.tok_here else 0
    wide = (tokens, EMBED_SIZE)
    share = sds((rows, EMBED_SIZE), f32)
    cat, kept = sds((2 * tokens, half), b16), sds(wide, f32)
    out_shape = LayerOut(
        layer_out=sds(wide, b16),
        token_grad=sds(wide, b16),
        fvalue=sds((rows_ff, EMBED_SIZE), f32),
        frecept=share,
        fkey=sds((rows, FF), f32),
        aout=share,
        arecept=share,
        avalue=share,
        akey=share,
        final=sds((8, EMBED_SIZE // plan.count_tok), f32),
        small=sds((16, EMBED_SIZE), f32),
        cat_weighted=cat,
        cat_recept_mix=cat,
        cat_value_mix=cat,
        cat_key_mix=cat,
        out_kf=kept,
        out_vf=kept,
        out_recept=kept,
        out_xp=kept,
        out_nf=sds((tokens + 8, EMBED_SIZE), f32),
    )
    out_specs = LayerOut(*[anywhere] * 9, *[vmem] * 2, *[anywhere] * 9)
    in_specs = LayerIn(*[anywhere] * 2, *[vmem] * 10, *[anywhere] * 7)
    square = (4, EMBED_SIZE, EMBED_SIZE)
    units = 2 * plan.slots - 1
    one = held((tokens + 8, EMBED_SIZE), f32)
    tiles = held((4, 8, EMBED_SIZE), f32)
    states = held((plan.count_tok, 8, EMBED_SIZE), f32)
    several = pltpu.SemaphoreType.DMA((120,))
    scratch = LayerHeld(
        vl=held(square, b16),
        vp=held(square, b16),
        va=held(square[1:], b16),
        early=held((5, units * plan.seg_rows + extra * plan.rows, EMBED_SIZE), b16),
        tall=held((units * plan.seg_rows_ff + extra * plan.rows_ff, EMBED_SIZE), b16),
        csq=held((2 * tokens, FF // 2), b16),
        cfr=held((2 * tokens, half), b16),
        cfk=held((2 * tokens, half), b16),
        gc=held((2 * tokens, EMBED_SIZE), b16),
        gg=held((2 * tokens, EMBED_SIZE), b16),
        gh=held((4, 2 * tokens, EMBED_SIZE), b16),
        sq=held((4,) + wide, b16),
        f0=one,
        f1=one,
        f2=one,
        f3=one,
        f4=one,
        f5=one,
        staged=held((LANES, tokens, 128), f32),
        held_fvalue=held(out_shape.fvalue.shape, f32),
        held_frecept=held(out_shape.frecept.shape, f32),
        held_fkey=held(out_shape.fkey.shape, f32),
        held_aout=held(out_shape.aout.shape, f32),
        held_arecept=held(out_shape.arecept.shape, f32),
        held_avalue=held(out_shape.avalue.shape, f32),
        held_akey=held(out_shape.akey.shape, f32),
        row_out=tiles,
        row_in=tiles,
        state_out=held((8, EMBED_SIZE), f32),
        state_in=states,
        back_out=held((8, EMBED_SIZE), f32),
        back_in=states,
        entry=held((24, EMBED_SIZE), f32),
        small_in=held((plan.bits + far, 16, EMBED_SIZE), f32),
        wire_send=pltpu.SemaphoreType.DMA((256,)),
        wire_recv=pltpu.SemaphoreType.DMA((256,)),
        local_sems=several,
        send_sems=several,
        recv_sems=several,
        ready=pltpu.SemaphoreType.REGULAR,
    )
    got = pl.pallas_call(
        partial(layer_kernel, plan),
        out_shape=list(out_shape),
        in_specs=list(in_specs),
        out_specs=list(out_specs),
        scratch_shapes=list(scratch),
        compiler_params=pltpu.CompilerParams(
            collective_id=0, has_side_effects=True, vmem_limit_bytes=VMEM_BYTES
        ),
    )(*arrays)
    return LayerOut(*got)


def place_kernel(share, count, *refs):
    sources, finals, small = refs[:count], refs[count], refs[count + 1]
    targets, rest = refs[count + 2 : 2 * count + 2], refs[2 * count + 2 : -count - 1]
    held, sems = refs[-count - 1 : -1], refs[-1]
    into = [pltpu.make_async_copy(sources[i], held[i], sems.at[0, i]) for i in range(count)]
    away = [pltpu.make_async_copy(held[i], targets[i], sems.at[1, i]) for i in range(count)]
    for copy in into:
        copy.start()
    for part in range(3):
        rest[part][...] = finals[part : part + 1]
    device = lax.axis_index("seg") * lax.axis_size("tok") + lax.axis_index("tok")
    shift = lax.rem(EMBED_SIZE - device * share, EMBED_SIZE)
    turned = pltpu.roll(small[...], shift, 1)[:, :share]
    first = 0
    for target in rest[3:]:
        rows = target.shape[0]
        target[...] = turned[first : first + rows]
        first += rows
    for index in range(count):
        into[index].wait()
        away[index].start()
    for copy in away:
        copy.wait()


def place_results(plan, arrays, finals, small):
    share = EMBED_SIZE // (plan.count_seg * plan.count_tok)
    sds = jax.ShapeDtypeStruct
    anywhere, vmem = pl.BlockSpec(memory_space=pl.ANY), pl.BlockSpec(memory_space=pltpu.VMEM)
    count = len(arrays)
    small_shapes = [(1, finals.shape[1])] * 3 + [(2, share), (2, share), (5, share), (1, share), (1, share)]
    return pl.pallas_call(
        partial(place_kernel, share, count),
        out_shape=[sds(item.shape, item.dtype) for item in arrays]
        + [sds(shape, jnp.float32) for shape in small_shapes],
        in_specs=[anywhere] * count + [vmem] * 2,
        out_specs=[anywhere] * count + [vmem] * len(small_shapes),
        scratch_shapes=[pltpu.VMEM(item.shape, item.dtype) for item in arrays]
        + [pltpu.SemaphoreType.DMA((2, count))],
    )(*arrays, finals, small)


def shards(
    incoming_items,
    upstream_slope,
    timemix_prior_entry,
    featmix_prior_entry,
    opening_dividend,
    opening_divisor,
    opening_power,
    normalize_scales,
    normalize_shifts,
    shift_blends,
    logarithmic_fading_speed,
    present_reward,
    *weights,
):
    plan = Plan(lax.axis_size("seg"), lax.axis_size("tok"))
    got = layer(
        plan,
        LayerIn(
            incoming_items[0],
            upstream_slope[0],
            timemix_prior_entry,
            featmix_prior_entry,
            opening_dividend,
            opening_divisor,
            opening_power,
            normalize_scales,
            normalize_shifts,
            shift_blends,
            logarithmic_fading_speed[None],
            present_reward[None],
            *weights,
        ),
        incoming_items.shape[1],
    )
    sums = got[2:9]
    if not plan.tok_here:
        sums = [lax.psum_scatter(item, "tok", scatter_dimension=0, tiled=True) for item in sums]
    placed = place_results(
        plan, [got.layer_out, got.token_grad, *sums], got.final, got.small
    )
    layer_out, token_grad, fvalue, frecept, fkey, aout, arecept, avalue, akey = placed[:9]
    numer, denom, top, gains, biases, mixes, decay, bonus = placed[9:]
    return (
        layer_out[None],
        token_grad[None],
        numer,
        denom,
        top,
        gains,
        biases,
        mixes,
        decay[0],
        bonus[0],
        akey,
        avalue,
        arecept,
        aout,
        fkey,
        fvalue,
        frecept,
    )


def solution(mesh):
    tokens, channels, whole = P("seg", "tok", None), P("seg", "tok"), P()
    spread, rows = P(None, ("seg", "tok")), P(("seg", "tok"), None)
    return jax.shard_map(
        shards,
        mesh=mesh,
        in_specs=(tokens,) * 2 + (P("seg", None),) * 2 + (channels,) * 3 + (whole,) * 12,
        out_specs=(tokens,) * 2
        + (channels,) * 3
        + (spread,) * 3
        + (P(("seg", "tok")),) * 2
        + (rows,) * 7,
        check_vma=False,
    )
```
